32 devices in a mesh: copy: 4 (over x, core), space: 8 (over z, y).
Axes of the slice: x: 2, y: 2, z: 4, core: 2. Of those that a mesh axis runs over, the one named last changes fastest.
Arguments:
- noisy_tokens: bfloat16 [4, 256, 256, 384], P('copy', 'space'), may hold values from -6 to 6
- grad_out: bfloat16 [4, 256, 256, 384], P('copy', 'space'), may hold values from -6 to 6
- filter_weight: bfloat16 [2, 256, 256, 384], P(None, None, 'space'), may hold values from -4 to 4
- weight_in: bfloat16 [384, 1536], replicated, may hold values from -0.3125 to 0.3125
- weight_out: bfloat16 [1536, 384], replicated, may hold values from -0.15625 to 0.15625
- gain_one: float32 [384], replicated, may hold values from 0.1 to 1.9
- gain_two: float32 [384], replicated, may hold values from 0.1 to 1.9
Outputs:
- block_out: bfloat16 [4, 256, 256, 384], P('copy', 'space')
- grad_tokens: bfloat16 [4, 256, 256, 384], P('copy', 'space')
- grad_filter: float32 [2, 256, 256, 384], P(None, None, 'space')
- grad_weight_in: bfloat16 [384, 1536], replicated
- grad_weight_out: bfloat16 [1536, 384], replicated
- grad_gain_one: float32 [384], replicated
- grad_gain_two: float32 [384], replicated
The draws below stay inside these ranges and needn't reach their ends.
All inputs are finite; a program needn't handle non-finite values.
Results may differ from the reference program's by a relative error of at most 0.024.
Values may be sent and summed in bfloat16 or wider, within the bound.
No kernel may reach another device: no remote copies, remote signals or barrier semaphores. Data moves between devices by JAX's collectives and lax.ppermute only.
A program may use at most 320 MiB of HBM per device.

```python
import math
import jax
import jax.numpy as jnp
from jax import lax

C = 384
FF = 1536
H = 256
W = 256
COPIES = 4


def shard_levels(stream_key, dims, shards, least, largest):
    level = 1.0
    for position, shards_of in shards:
        heights = jax.random.uniform(jax.random.fold_in(jax.random.fold_in(stream_key, 6), position), (shards_of,), jnp.float32, least / len(shards), largest / len(shards))
        level = level * jnp.repeat(jnp.exp(heights), dims[position] // shards_of).reshape((-1,) + (1,) * (len(dims) - 1 - position))
    return level


def normal_values(stream_key, dims, deviation, most, shards=(), kind=jnp.bfloat16):
    array = deviation * jax.random.normal(stream_key, dims, jnp.float32)
    if shards:
        array = array * shard_levels(stream_key, dims, shards, -0.22, 0.18)
    return jnp.clip(array, -most, most).astype(kind)


def setup_inputs(seed: int = 0) -> dict:
    arg_keys = jax.random.split(jax.random.key(seed), 8)
    return {
        "noisy_tokens": normal_values(arg_keys[0], (COPIES, H, W, C), 1.0, 6.0, ((0, 4), (1, 8))),
        "grad_out": normal_values(arg_keys[1], (COPIES, H, W, C), 1.0, 6.0, ((0, 4), (1, 8))),
        "filter_weight": normal_values(arg_keys[2], (2, H, W, C), 0.7, 4.0, ((2, 8),)),
        "weight_in": normal_values(arg_keys[3], (C, FF), C ** -0.5, 0.3125),
        "weight_out": normal_values(arg_keys[4], (FF, C), FF ** -0.5, 0.15625),
        "gain_one": jnp.clip(1.0 + 0.18 * jax.random.normal(arg_keys[5], (C,), jnp.float32), 0.1, 1.9),
        "gain_two": jnp.clip(1.0 + 0.18 * jax.random.normal(arg_keys[6], (C,), jnp.float32), 0.1, 1.9),
    }


EPS = 1e-06

def dft_parts(length):
    index = jnp.arange(length, dtype=jnp.int32)
    phase = index[:, None] * index[None, :] % length
    angle = phase.astype(jnp.float32) * (2.0 * math.pi / length)
    factor = 1.0 / math.sqrt(length)
    return ((jnp.cos(angle) * factor).astype(jnp.bfloat16), (jnp.sin(angle) * factor).astype(jnp.bfloat16))

def row_table(length):
    cosine, sine = dft_parts(length)
    return jnp.stack([cosine, -sine])

def column_table(length, direction):
    cosine, sine = dft_parts(length)
    upper = jnp.stack([cosine, direction * sine], axis=1)
    lower = jnp.stack([-direction * sine, cosine], axis=1)
    return jnp.stack([upper, lower])

def layer_norm(values):
    centre = lax.optimization_barrier(jnp.mean(values, axis=-1, keepdims=True))
    centred = values - centre
    variance = lax.optimization_barrier(jnp.mean(centred * centred, axis=-1, keepdims=True))
    rstd_value = lax.rsqrt(variance + EPS)
    return (centred * rstd_value, rstd_value)

def norm_backward(upstream, normed, rstd_value, gain):
    scaled = upstream * gain
    result = (scaled - lax.optimization_barrier(jnp.mean(scaled, axis=-1, keepdims=True)) - normed * lax.optimization_barrier(jnp.mean(scaled * normed, axis=-1, keepdims=True))) * rstd_value
    lead = tuple(range(upstream.ndim - 1))
    return (result, lax.optimization_barrier(jnp.sum(upstream * normed, axis=lead)))

def apply_filter(spectrum, filter_weight, direction):
    real_part = spectrum[0].astype(jnp.float32)
    imag_part = spectrum[1].astype(jnp.float32)
    kernel_real = filter_weight[0].astype(jnp.float32)
    kernel_imag = direction * filter_weight[1].astype(jnp.float32)
    return jnp.stack([kernel_real * real_part - kernel_imag * imag_part, kernel_real * imag_part + kernel_imag * real_part])

def exact_gelu(values):
    return jax.nn.gelu(values, approximate=False)

def spectral(values, filter_weight, direction):
    highest = lax.Precision.HIGHEST
    rows_tab = row_table(W).astype(jnp.float32)
    rows = jnp.einsum('pkw,hwc->phkc', rows_tab, values.astype(jnp.float32), precision=highest).astype(jnp.bfloat16)
    spectrum = jnp.einsum('qmph,phkc->qmkc', column_table(H, 1).astype(jnp.float32), rows.astype(jnp.float32), precision=highest).astype(jnp.bfloat16)
    weighted = apply_filter(spectrum, filter_weight, direction).astype(jnp.bfloat16)
    returned = jnp.einsum('qmph,phkc->qmkc', column_table(H, -1).astype(jnp.float32), weighted.astype(jnp.float32), precision=highest).astype(jnp.bfloat16)
    output = jnp.einsum('pkw,phkc->hwc', rows_tab, returned.astype(jnp.float32), precision=highest)
    return (output, spectrum)

def one_copy(carry, pair):
    noisy, upstream_grad = pair
    filter_weight, weight_in, weight_out, gain_one, gain_two, totals = carry
    inputs = noisy.astype(jnp.float32)
    normed_one, rstd_one = layer_norm(inputs)
    mixed_in = (normed_one * gain_one).astype(jnp.bfloat16)
    spatial, spectrum = spectral(mixed_in, filter_weight, 1)
    normed_two, rstd_two = layer_norm(spatial)
    mlp_in = (normed_two * gain_two).astype(jnp.bfloat16).reshape(-1, C)
    preact = jnp.dot(mlp_in, weight_in, preferred_element_type=jnp.float32)
    activated = exact_gelu(preact).astype(jnp.bfloat16)
    mlp_out = jnp.dot(activated, weight_out, preferred_element_type=jnp.float32)
    block_out = (inputs + mlp_out.reshape(inputs.shape)).astype(jnp.bfloat16)
    upstream = upstream_grad.reshape(-1, C)
    grad_act = jnp.dot(upstream, weight_out.T, preferred_element_type=jnp.float32)
    grad_pre = jax.vjp(exact_gelu, preact)[1](grad_act)[0].astype(jnp.bfloat16)
    sum_out = jnp.dot(activated.T, upstream, preferred_element_type=jnp.float32)
    sum_in = jnp.dot(mlp_in.T, grad_pre, preferred_element_type=jnp.float32)
    grad_mlp = jnp.dot(grad_pre, weight_in.T, preferred_element_type=jnp.float32).reshape(inputs.shape)
    grad_spatial, sum_gain_two = norm_backward(grad_mlp, normed_two, rstd_two, gain_two)
    back_spatial, adjoint = spectral(grad_spatial.astype(jnp.bfloat16), filter_weight, -1)
    spec_f = spectrum.astype(jnp.float32)
    adj_f = adjoint.astype(jnp.float32)
    filter_terms = jnp.stack([adj_f[0] * spec_f[0] + adj_f[1] * spec_f[1], adj_f[1] * spec_f[0] - adj_f[0] * spec_f[1]])
    grad_normed, sum_gain_one = norm_backward(back_spatial, normed_one, rstd_one, gain_one)
    grad_tokens = (upstream_grad.astype(jnp.float32) + grad_normed).astype(jnp.bfloat16)
    new_totals = (totals[0] + filter_terms, totals[1] + sum_in, totals[2] + sum_out, totals[3] + sum_gain_one, totals[4] + sum_gain_two)
    return ((filter_weight, weight_in, weight_out, gain_one, gain_two, new_totals), (block_out, grad_tokens))

def reference(noisy_tokens, grad_out, filter_weight, weight_in, weight_out, gain_one, gain_two):
    totals = (jnp.zeros((2, H, W, C), jnp.float32), jnp.zeros((C, FF), jnp.float32), jnp.zeros((FF, C), jnp.float32), jnp.zeros((C,), jnp.float32), jnp.zeros((C,), jnp.float32))
    carry = (filter_weight, weight_in, weight_out, gain_one, gain_two, totals)
    carry, outputs = lax.scan(one_copy, carry, (noisy_tokens, grad_out))
    totals = carry[5]
    factor = 1.0 / math.sqrt(COPIES * H * W)
    return (outputs[0], outputs[1], totals[0], (totals[1] * factor).astype(jnp.bfloat16), (totals[2] * factor).astype(jnp.bfloat16), totals[3] * factor, totals[4] * factor)
```

```python
import functools
import math

import jax
import jax.numpy as jnp
import ml_dtypes
import numpy as np
from jax import lax
from jax.experimental import pallas as pl
from jax.experimental.pallas import tpu as pltpu
from jax.sharding import PartitionSpec as P

EPS = 1e-06
LANES = 128
VMEM_LIMIT = 60 * 1024 * 1024
BF16 = jnp.bfloat16
F32 = jnp.float32


def dft_pair(length):
    index = np.arange(length, dtype=np.int64)
    angle = (index[:, None] * index[None, :] % length) * (2.0 * math.pi / length)
    factor = 1.0 / math.sqrt(length)
    rounded = lambda a: a.astype(np.float32).astype(ml_dtypes.bfloat16).astype(np.float32)
    return rounded(np.cos(angle) * factor), rounded(np.sin(angle) * factor)


def row_tables(width, n):
    cosine, sine = dft_pair(width)
    own = width // n
    half = own // 2
    forward = np.zeros((n, 2, half, width), np.float32)
    weight = np.full((n, 2, half, 1), 2.0, np.float32)
    for d in range(n):
        first = own * d + (1 if d >= n // 2 else 0)
        forward[d, 0] = cosine[first : first + half]
        forward[d, 1] = -sine[first : first + half]
    forward[0, 1, 0] = cosine[width // 2]
    weight[0, :, 0] = 1.0
    backward = (forward * weight).reshape(width, width).T
    return (
        forward.reshape(width, width).astype(ml_dtypes.bfloat16),
        np.ascontiguousarray(backward).astype(ml_dtypes.bfloat16),
    )


def column_tables(height, n, chunks):
    cosine, sine = dft_pair(height)
    zero = np.zeros_like(cosine)
    rows = height // n // chunks

    def arrange(blocks):
        full = np.stack([np.stack(line, axis=1) for line in blocks])
        full = full.reshape(2 * height, 2, n, chunks, rows)
        return full.transpose(0, 3, 2, 1, 4).reshape(2 * height, 2 * height)

    middle = arrange([[zero, cosine], [zero, -sine]])
    first = arrange([[cosine, zero], [-sine, zero]])
    other = arrange([[cosine, sine], [-sine, cosine]])
    forward = np.stack([middle, first, other])
    backward = np.ascontiguousarray(forward.transpose(0, 2, 1))
    return forward.astype(ml_dtypes.bfloat16), backward.astype(ml_dtypes.bfloat16)


def mirror_table(height):
    table = np.zeros((height, height), np.float32)
    table[np.arange(height), (-np.arange(height)) % height] = 1.0
    return table.astype(ml_dtypes.bfloat16)


def dot(a, b):
    return jnp.dot(a, b, preferred_element_type=F32)


def dot_tn(a, b):
    return lax.dot_general(a, b, (((0,), (0,)), ((), ())), preferred_element_type=F32)


def normalize(values):
    centred = values - jnp.mean(values, axis=-1, keepdims=True)
    variance = jnp.mean(centred * centred, axis=-1, keepdims=True)
    rstd = lax.rsqrt(variance + EPS)
    return centred * rstd, rstd


def norm_backward(upstream, normed, rstd, gain):
    scaled = upstream * gain
    return (
        scaled
        - jnp.mean(scaled, axis=-1, keepdims=True)
        - normed * jnp.mean(scaled * normed, axis=-1, keepdims=True)
    ) * rstd


def gelu_and_slope(v):
    e = jnp.exp(v * v * -0.5)
    d = 1.0 + (0.3275911 / math.sqrt(2.0)) * jnp.abs(v)
    t = pl.reciprocal(d, approx=True)
    t = t * (2.0 - d * t)
    poly = 0.5 * 1.061405429
    for coefficient in (-1.453152027, 1.421413741, -0.284496736, 0.254829592):
        poly = poly * t + 0.5 * coefficient
    tail = poly * t * e
    phi = jnp.where(v < 0.0, tail, 1.0 - tail)
    return v * phi, phi + v * e * (1.0 / math.sqrt(2.0 * math.pi))


def unpack(received, scratch):
    columns, rows, chans = received.shape
    for c in range(chans // LANES):
        part = received[:, :, c * LANES : (c + 1) * LANES].astype(F32)
        scratch[c] = part.reshape(columns * rows, LANES)


def read_row(scratch, row, columns, rows):
    parts = [
        scratch[c, pl.ds(row, columns, stride=rows), :].astype(BF16)
        for c in range(scratch.shape[0])
    ]
    return jnp.concatenate(parts, axis=1)


def write_row(scratch, row, columns, values):
    start = pl.multiple_of(row * columns, columns)
    for c in range(scratch.shape[0]):
        scratch[c, pl.ds(start, columns), :] = values[:, c * LANES : (c + 1) * LANES]


def pack(scratch, outgoing):
    columns, rows, _ = outgoing.shape

    def step(k, carry):
        for c in range(scratch.shape[0]):
            part = scratch[c, pl.ds(k, rows, stride=columns), :]
            outgoing[k, :, c * LANES : (c + 1) * LANES] = part.astype(BF16)
        return carry

    lax.fori_loop(0, columns, step, 0, unroll=8)


def params():
    return pltpu.CompilerParams(vmem_limit_bytes=VMEM_LIMIT)


def resident(shape):
    return pl.BlockSpec(shape, lambda *_: (0,) * len(shape), pipeline_mode=pl.Buffered(1))


def cost(flops, size):
    return pl.CostEstimate(flops=int(flops), bytes_accessed=int(size), transcendentals=0)


def enter_kernel(tokens, gain, table, outgoing, scratch):
    step = pl.program_id(0)
    block, width, _ = tokens.shape
    for r in range(block):
        normed, _ = normalize(tokens[r].astype(F32))
        mixed = (normed * gain[...]).astype(BF16)
        write_row(scratch, step * block + r, width, dot(table[...], mixed))

    @pl.when(step == pl.num_programs(0) - 1)
    def _():
        pack(scratch, outgoing)


def enter(tokens, gain, table, chunk, rows, block):
    _, width, chans = tokens.shape
    steps = rows // block
    return pl.pallas_call(
        enter_kernel,
        grid=(steps,),
        in_specs=[
            pl.BlockSpec((block, width, chans), lambda i: (i + chunk * steps, 0, 0)),
            resident((1, chans)),
            resident((width, width)),
        ],
        out_specs=resident((width, rows, chans)),
        out_shape=jax.ShapeDtypeStruct((width, rows, chans), BF16),
        scratch_shapes=[pltpu.VMEM((chans // LANES, rows * width, LANES), F32)],
        compiler_params=params(),
        cost_estimate=cost(2 * rows * width * width * chans, 4 * rows * width * chans),
        name="enter_rows",
    )(tokens, gain, table)


def mlp_kernel(
    received, tokens, upstream, gain, table_out, table_in, w_in, w_out, w_in_t, w_out_t, *rest
):
    block_out, outgoing, sum_in, sum_out, sum_gain, unpacked, packed = rest[-7:]
    step = pl.program_id(0)
    block, width, chans = tokens.shape
    rows = received.shape[1]
    hidden = w_in.shape[1]
    part = min(512, hidden)

    @pl.when(step == 0)
    def _():
        unpack(received, unpacked)
        sum_in[...] = jnp.zeros_like(sum_in)
        sum_out[...] = jnp.zeros_like(sum_out)
        sum_gain[...] = jnp.zeros_like(sum_gain)

    spatial = jnp.concatenate(
        [
            dot(table_out[...], read_row(unpacked, step * block + r, width, rows))
            for r in range(block)
        ],
        axis=0,
    )
    normed, rstd = normalize(spatial)
    mlp_in = (normed * gain[...]).astype(BF16)
    grad = upstream[...].reshape(block * width, chans)
    out = tokens[...].reshape(block * width, chans).astype(F32)
    grad_mlp = jnp.zeros_like(spatial)
    for f in range(0, hidden, part):
        cols = slice(f, f + part)
        value, slope = gelu_and_slope(dot(mlp_in, w_in[:, cols]))
        activated = value.astype(BF16)
        grad_pre = (dot(grad, w_out_t[:, cols]) * slope).astype(BF16)
        out = out + dot(activated, w_out[cols, :])
        grad_mlp = grad_mlp + dot(grad_pre, w_in_t[cols, :])
        sum_out[:, cols] += dot_tn(grad, activated)
        sum_in[:, cols] += dot_tn(mlp_in, grad_pre)
    block_out[...] = out.astype(BF16).reshape(block, width, chans)
    grad_spatial = norm_backward(grad_mlp, normed, rstd, gain[...])
    sum_gain[0:8] += jnp.sum((grad_mlp * normed).reshape(-1, 8, chans), axis=0)
    sum_gain[8:16] += jnp.sum((grad_spatial * spatial).reshape(-1, 8, chans), axis=0)
    sent = grad_spatial.astype(BF16)
    for r in range(block):
        values = dot(table_in[...], sent[r * width : (r + 1) * width])
        write_row(packed, step * block + r, width, values)

    @pl.when(step == pl.num_programs(0) - 1)
    def _():
        pack(packed, outgoing)


def mlp(received, tokens, upstream, gain, tables, weights, previous, chunk, block):
    width, rows, chans = received.shape
    hidden = weights[0].shape[1]
    steps = rows // block
    by_rows = pl.BlockSpec((block, width, chans), lambda i: (i + chunk * steps, 0, 0))
    operands = [received, tokens, upstream, gain, *tables, *weights]
    in_specs = [
        resident((width, rows, chans)),
        by_rows,
        by_rows,
        resident((1, chans)),
        resident((width, width)),
        resident((width, width)),
        resident((chans, hidden)),
        resident((hidden, chans)),
        resident((hidden, chans)),
        resident((chans, hidden)),
    ]
    aliases = {}
    if previous is not None:
        aliases = {len(operands): 0}
        operands.append(previous)
        in_specs.append(pl.BlockSpec(memory_space=pl.ANY))
    flops = 2 * rows * width * chans * (6 * hidden + 2 * width)
    return pl.pallas_call(
        mlp_kernel,
        grid=(steps,),
        in_specs=in_specs,
        out_specs=[
            by_rows,
            resident((width, rows, chans)),
            resident((chans, hidden)),
            resident((chans, hidden)),
            resident((16, chans)),
        ],
        out_shape=[
            jax.ShapeDtypeStruct(tokens.shape, BF16),
            jax.ShapeDtypeStruct((width, rows, chans), BF16),
            jax.ShapeDtypeStruct((chans, hidden), F32),
            jax.ShapeDtypeStruct((chans, hidden), F32),
            jax.ShapeDtypeStruct((16, chans), F32),
        ],
        scratch_shapes=[
            pltpu.VMEM((chans // LANES, rows * width, LANES), F32),
            pltpu.VMEM((chans // LANES, rows * width, LANES), F32),
        ],
        input_output_aliases=aliases,
        compiler_params=params(),
        cost_estimate=cost(flops, 10 * rows * width * chans),
        name="mlp_rows",
    )(*operands)


def leave_kernel(received, tokens, upstream, gain, table_out, *rest):
    grad_tokens, unpacked = rest[-2:]
    step = pl.program_id(0)
    block, width, _ = tokens.shape
    rows = received.shape[1]

    @pl.when(step == 0)
    def _():
        unpack(received, unpacked)

    for r in range(block):
        back = dot(table_out[...], read_row(unpacked, step * block + r, width, rows))
        normed, rstd = normalize(tokens[r].astype(F32))
        grad = norm_backward(back, normed, rstd, gain[...])
        grad_tokens[r] = (upstream[r].astype(F32) + grad).astype(BF16)


def leave(received, tokens, upstream, gain, table_out, previous, chunk, block):
    width, rows, chans = received.shape
    steps = rows // block
    by_rows = pl.BlockSpec((block, width, chans), lambda i: (i + chunk * steps, 0, 0))
    operands = [received, tokens, upstream, gain, table_out]
    in_specs = [
        resident((width, rows, chans)),
        by_rows,
        by_rows,
        resident((1, chans)),
        resident((width, width)),
    ]
    aliases = {}
    if previous is not None:
        aliases = {len(operands): 0}
        operands.append(previous)
        in_specs.append(pl.BlockSpec(memory_space=pl.ANY))
    return pl.pallas_call(
        leave_kernel,
        grid=(steps,),
        in_specs=in_specs,
        out_specs=by_rows,
        out_shape=jax.ShapeDtypeStruct(tokens.shape, BF16),
        scratch_shapes=[pltpu.VMEM((chans // LANES, rows * width, LANES), F32)],
        input_output_aliases=aliases,
        compiler_params=params(),
        cost_estimate=cost(2 * rows * width * width * chans, 8 * rows * width * chans),
        name="leave_rows",
    )(*operands)


def transform_in(table, received):
    parts = [ref[...].reshape(-1, ref.shape[-1]) for ref in received]
    return dot(table[0], jnp.concatenate(parts, axis=0))


def transform_out(table, weighted, outgoing, carried):
    step = pl.program_id(0)
    result = dot(table[0], weighted)

    @pl.when(step == 0)
    def _():
        carried[...] = result

    result = result + jnp.where(step == 1, carried[...], 0.0)
    size = result.shape[0] // len(outgoing)
    for c, ref in enumerate(outgoing):
        ref[...] = result[c * size : (c + 1) * size].astype(BF16).reshape(ref.shape)


def forward_kernel(chunks, flags, table_f, table_b, kernel, *rest):
    received, outgoing = rest[:chunks], rest[chunks : 2 * chunks]
    spectrum, carried = rest[2 * chunks :]
    height = kernel.shape[2]
    found = transform_in(table_f, received).astype(BF16)
    spectrum[0] = found.reshape(spectrum.shape[1:])
    found = found.astype(F32)
    real, imag = found[:height], found[height:]
    k_real, k_imag = kernel[0, 0].astype(F32), kernel[0, 1].astype(F32)
    weighted = jnp.concatenate(
        [
            (k_real * real - k_imag * imag).astype(BF16),
            (k_real * imag + k_imag * real).astype(BF16),
        ],
        axis=0,
    )
    transform_out(table_b, weighted, outgoing, carried)


def backward_kernel(chunks, flags, table_f, table_b, kernel, spectrum, *rest):
    received, outgoing = rest[:chunks], rest[chunks : 2 * chunks]
    terms, carried = rest[2 * chunks :]
    height = kernel.shape[2]
    found = transform_in(table_f, received).astype(BF16).astype(F32)
    real, imag = found[:height], found[height:]
    s_real, s_imag = spectrum[0, 0].astype(F32), spectrum[0, 1].astype(F32)
    terms[0, 0] = (real * s_real + imag * s_imag).astype(BF16)
    terms[0, 1] = (imag * s_real - real * s_imag).astype(BF16)
    k_real, k_imag = kernel[0, 0].astype(F32), kernel[0, 1].astype(F32)
    weighted = jnp.concatenate(
        [
            (k_real * real + k_imag * imag).astype(BF16),
            (k_real * imag - k_imag * real).astype(BF16),
        ],
        axis=0,
    )
    transform_out(table_b, weighted, outgoing, carried)


def columns(flags, tables, kernel, received, spectrum):
    chunks = len(received)
    n, _, half, rows, chans = received[0].shape
    height = kernel.shape[2]
    column = pl.BlockSpec(
        (n, 2, 1, rows, chans), lambda t, flags: (0, 0, jnp.maximum(t - 1, 0), 0, 0)
    )
    table = pl.BlockSpec(
        (1, 2 * height, 2 * height),
        lambda t, flags: (jnp.where(t == 1, 2 - flags[1], jnp.minimum(t, 1) * 2), 0, 0),
    )
    held = pl.BlockSpec((1, 2, height, chans), lambda t, flags: (t, 0, 0, 0))
    body = forward_kernel if spectrum is None else backward_kernel
    extra = [] if spectrum is None else [spectrum]
    return pl.pallas_call(
        functools.partial(body, chunks),
        grid_spec=pltpu.PrefetchScalarGridSpec(
            num_scalar_prefetch=1,
            grid=(half + 1,),
            in_specs=[table, table, held] + [held] * len(extra) + [column] * chunks,
            out_specs=[column] * chunks + [held],
            scratch_shapes=[pltpu.VMEM((2 * height, chans), F32)],
        ),
        out_shape=[jax.ShapeDtypeStruct(r.shape, BF16) for r in received]
        + [jax.ShapeDtypeStruct(kernel.shape, BF16)],
        compiler_params=params(),
        cost_estimate=cost(
            16 * height * height * chans * (half + 1), 20 * height * chans * (half + 1)
        ),
        name="filter_columns",
    )(flags, *tables, kernel, *extra, *received)


def kernel_part_kernel(copies, flags, mirror, own, *rest):
    mains, extras = rest[:copies], rest[copies : 2 * copies]
    kernel, scr_own, scr_main, scr_extra = rest[2 * copies :]
    part = pl.program_id(0)
    upper, first, me = flags[0], flags[1], flags[2]
    _, height, wide, lanes = own.shape
    half = wide // 2
    share = height // copies
    scr_own[...] = own[0].astype(F32).reshape(height * wide, lanes)
    for i in range(copies):
        owner = jnp.bitwise_xor(me, i)
        at = pl.multiple_of(owner * (share * half), share * half)
        scr_main[pl.ds(at, share * half), :] = (
            mains[i][0].astype(F32).reshape(share * half, lanes)
        )
        at = pl.multiple_of(owner * share, share)
        scr_extra[pl.ds(at, share), :] = extras[i][0].astype(F32)
    sign = jnp.where(part == 0, 0.5, -0.5)
    extra = scr_extra[...]
    middle = 0.5 * extra + sign * dot(mirror[...], extra.astype(BF16))
    kernel[0, 0] = jnp.where(first == 1, middle, 0.0).astype(BF16)
    for j in range(half):
        mine = scr_own[pl.ds(j + upper, height, stride=wide), :]
        index = half - j - upper
        if j == 0:
            other = scr_main[pl.ds(half - 1, height, stride=half), :]
            lower = jnp.where(first == 1, mine, extra)
            other = jnp.where(upper == 1, other, lower)
        else:
            other = scr_main[pl.ds(index, height, stride=half), :]
        turned = dot(mirror[...], other.astype(BF16))
        kernel[j + 1, 0] = (0.5 * mine + sign * turned).astype(BF16)


def kernel_part(flags, mirror, own, mains, extras):
    _, height, wide, chans = own.shape
    copies = len(mains)
    half, share = wide // 2, height // copies
    return pl.pallas_call(
        functools.partial(kernel_part_kernel, copies),
        grid_spec=pltpu.PrefetchScalarGridSpec(
            num_scalar_prefetch=1,
            grid=(2, chans // LANES),
            in_specs=[
                pl.BlockSpec((height, height), lambda p, c, flags: (0, 0)),
                pl.BlockSpec((1, height, wide, LANES), lambda p, c, flags: (p, 0, 0, c)),
            ]
            + [pl.BlockSpec((1, share, half, LANES), lambda p, c, flags: (p, 0, 0, c))] * copies
            + [pl.BlockSpec((1, share, LANES), lambda p, c, flags: (p, 0, c))] * copies,
            out_specs=pl.BlockSpec(
                (half + 1, 1, height, LANES), lambda p, c, flags: (0, p, 0, c)
            ),
            scratch_shapes=[
                pltpu.VMEM((height * wide, LANES), F32),
                pltpu.VMEM((height * half, LANES), F32),
                pltpu.VMEM((height, LANES), F32),
            ],
        ),
        out_shape=jax.ShapeDtypeStruct((half + 1, 2, height, chans), BF16),
        compiler_params=params(),
        cost_estimate=cost(4 * height * height * chans * half, 16 * height * half * chans),
        name="filter_part",
    )(flags, mirror, own, *mains, *extras)


def spread_kernel(copies, flags, mirror, *rest):
    parts, (out, gathered, turned) = rest[:copies], rest[copies:]
    part = pl.program_id(0)
    upper, me = flags[0], flags[2]
    _, height, wide, lanes = out.shape
    half = wide // 2
    share = height // copies
    for i in range(copies):
        owner = jnp.bitwise_xor(me, i)
        at = pl.multiple_of(owner * share, share)
        gathered[:, pl.ds(at, share), :] = parts[i][:, 0]
    sign = jnp.where(part == 0, 1.0, -1.0)
    for k in range(wide):
        if k == 0:
            index, straight = jnp.where(upper == 1, 2 * half, 0), 1 - upper
        elif k < half:
            index, straight = k - upper, 1
        elif k == half:
            index, straight = jnp.where(upper == 1, half - 1, 2 * half - 1), upper
        else:
            index, straight = half + wide - 1 - k + upper, 0
        value = gathered[index]
        if k != 0 and k < half:
            turned[pl.ds(k * height, height), :] = value.astype(F32)
        else:
            other = sign * dot(mirror[...], value)
            if k == 0 or k == half:
                other = jnp.where(straight == 1, value.astype(F32), other)
            turned[pl.ds(k * height, height), :] = other

    def step(m, carry):
        out[0, m] = turned[pl.ds(m, wide, stride=height), :]
        return carry

    lax.fori_loop(0, height, step, 0, unroll=8)


def spread(flags, mirror, parts, height, wide):
    slots, _, share, chans = parts[0].shape
    copies = len(parts)
    return pl.pallas_call(
        functools.partial(spread_kernel, copies),
        grid_spec=pltpu.PrefetchScalarGridSpec(
            num_scalar_prefetch=1,
            grid=(2, chans // LANES),
            in_specs=[pl.BlockSpec((height, height), lambda p, c, flags: (0, 0))]
            + [pl.BlockSpec((slots, 1, share, LANES), lambda p, c, flags: (0, p, 0, c))] * copies,
            out_specs=pl.BlockSpec(
                (1, height, wide, LANES), lambda p, c, flags: (p, 0, 0, c)
            ),
            scratch_shapes=[
                pltpu.VMEM((slots, height, LANES), BF16),
                pltpu.VMEM((wide * height, LANES), F32),
            ],
        ),
        out_shape=jax.ShapeDtypeStruct((2, height, wide, chans), F32),
        compiler_params=params(),
        cost_estimate=cost(2 * height * height * chans * wide, 12 * height * wide * chans),
        name="filter_gradient",
    )(flags, mirror, *parts)


def swap(value, axis, size, partner):
    return lax.ppermute(value, axis, [(i, partner(i)) for i in range(size)])


def gather_copies(value, copies):
    parts = {0: value}
    bit = copies // 2
    while bit:
        for key in list(parts):
            parts[key ^ bit] = swap(parts[key], "copy", copies, lambda i: i ^ bit)
        bit //= 2
    return [parts[i] for i in range(copies)]


def reduce_copies(value, copies, axis):
    me = lax.axis_index("copy")
    bit = 1
    while bit < copies:
        size = value.shape[axis] // 2
        mine = (me // bit) % 2
        kept = lax.dynamic_slice_in_dim(value, mine * size, size, axis)
        sent = lax.dynamic_slice_in_dim(value, (1 - mine) * size, size, axis)
        other = swap(sent, "copy", copies, lambda i: i ^ bit)
        value = (kept.astype(F32) + other.astype(F32)).astype(value.dtype)
        bit *= 2
    return value


def share_index(copies):
    me = lax.axis_index("copy")
    index = 0 * me
    bit = 1
    while bit < copies:
        index = index * 2 + (me // bit) % 2
        bit *= 2
    return index


def exchange(value, n):
    return lax.all_to_all(value, "space", split_axis=0, concat_axis=0, tiled=True)


def body(noisy_tokens, grad_out, filter_weight, weight_in, weight_out, gain_one, gain_two):
    _, rows_dev, width, chans = noisy_tokens.shape
    height = filter_weight.shape[1]
    wide = filter_weight.shape[2]
    half = wide // 2
    n, copies = lax.axis_size("space"), lax.axis_size("copy")
    chunks = 2
    rows = rows_dev // chunks
    block = 2
    tokens = noisy_tokens[0]
    upstream = grad_out[0]
    me, copy = lax.axis_index("space"), lax.axis_index("copy")
    table_in, table_out = (jnp.asarray(t) for t in row_tables(width, n))
    column_tabs = tuple(jnp.asarray(t) for t in column_tables(height, n, chunks))
    mirror = jnp.asarray(mirror_table(height))
    gain_a, gain_b = gain_one.reshape(1, chans), gain_two.reshape(1, chans)

    upper = (me >= n // 2).astype(jnp.int32)
    first = (me == 0).astype(jnp.int32)
    flags_in = jnp.stack([upper, first, copy.astype(jnp.int32)])

    share = height // copies
    mine = lax.dynamic_slice_in_dim(filter_weight, copy * share, share, 1)
    opposite = lambda d: n - 1 - d
    main = swap(mine[:, :, half:], "space", n, opposite)
    to_lower = [(n // 2, 0)] + [(e, n - e) for e in range(n // 2 + 1, n)]
    single = lax.ppermute(mine[:, :, 0], "space", to_lower)
    mains, singles = gather_copies(main, copies), gather_copies(single, copies)

    split = lambda value: value.reshape(n, 2, half, rows, chans)
    join = lambda value: value.reshape(width, rows, chans)

    entered = [enter(tokens, gain_a, table_in, c, rows, block) for c in range(chunks)]
    arrived = [split(exchange(e, n)) for e in entered]
    kernel = kernel_part(flags_in, mirror, filter_weight, mains, singles)
    *returned, spectrum = columns(flags_in, column_tabs, kernel, arrived, None)

    weights = (weight_in, weight_out, weight_in.T, weight_out.T)
    block_out = None
    sums, entered = [], []
    for c in range(chunks):
        received = exchange(join(returned[c]), n)
        block_out, sent, *local = mlp(
            received, tokens, upstream, gain_b, (table_out, table_in), weights, block_out, c, block
        )
        entered.append(sent)
        sums.append(local)
    arrived = [split(exchange(e, n)) for e in entered]
    sum_in, sum_out, sum_gain = (a + b for a, b in zip(*sums))
    sum_two = jnp.sum(sum_gain[:8], axis=0)
    sum_one = jnp.sum(sum_gain[8:], axis=0) / gain_one
    summed = lax.psum((sum_in, sum_out, sum_one, sum_two), ("copy", "space"))

    *returned, terms = columns(flags_in, column_tabs, kernel, arrived, spectrum)
    grad_tokens = None
    for c in range(chunks):
        received = exchange(join(returned[c]), n)
        grad_tokens = leave(
            received, tokens, upstream, gain_a, table_out, grad_tokens, c, block
        )

    reduced = reduce_copies(terms, copies, 2)
    mirrored = swap(reduced[1:], "space", n, opposite)
    to_upper = [(0, n // 2)] + [(d, n - d) for d in range(1, n // 2)]
    single = lax.ppermute(jnp.where(me == 0, reduced[0], reduced[1]), "space", to_upper)
    bundle = jnp.concatenate([reduced[1:], mirrored, single[None]], axis=0)
    flags_out = jnp.stack([upper, first, share_index(copies).astype(jnp.int32)])
    parts = gather_copies(bundle, copies)
    order = [int(format(i, "b").zfill(copies.bit_length() - 1)[::-1], 2) for i in range(copies)]
    parts = [parts[order[i]] for i in range(copies)]
    grad_filter = spread(flags_out, mirror, parts, height, wide)

    total_tokens = copies * rows_dev * n * width
    factor = 1.0 / math.sqrt(total_tokens)
    return (
        block_out[None],
        grad_tokens[None],
        grad_filter,
        (summed[0] * factor).astype(BF16),
        (summed[1].T * factor).astype(BF16),
        summed[2] * factor,
        summed[3] * factor,
    )


def dft_parts(length):
    index = jnp.arange(length, dtype=jnp.int32)
    phase = index[:, None] * index[None, :] % length
    angle = phase.astype(jnp.float32) * (2.0 * math.pi / length)
    factor = 1.0 / math.sqrt(length)
    return (
        (jnp.cos(angle) * factor).astype(jnp.bfloat16),
        (jnp.sin(angle) * factor).astype(jnp.bfloat16),
    )


def row_table(length):
    cosine, sine = dft_parts(length)
    return jnp.stack([cosine, -sine])


def column_table(length, direction):
    cosine, sine = dft_parts(length)
    upper = jnp.stack([cosine, direction * sine], axis=1)
    lower = jnp.stack([-direction * sine, cosine], axis=1)
    return jnp.stack([upper, lower])


def plain_layer_norm(values):
    centre = jnp.mean(values, axis=-1, keepdims=True)
    centred = values - centre
    variance = jnp.mean(centred * centred, axis=-1, keepdims=True)
    rstd_value = lax.rsqrt(variance + EPS)
    return (centred * rstd_value, rstd_value)


def plain_norm_backward(upstream, normed, rstd_value, gain):
    scaled = upstream * gain
    result = (
        scaled
        - jnp.mean(scaled, axis=-1, keepdims=True)
        - normed * jnp.mean(scaled * normed, axis=-1, keepdims=True)
    ) * rstd_value
    lead = tuple(range(upstream.ndim - 1))
    return (result, jnp.sum(upstream * normed, axis=lead))


def apply_filter(spectrum, filter_weight, direction):
    real_part = spectrum[0].astype(jnp.float32)
    imag_part = spectrum[1].astype(jnp.float32)
    kernel_real = filter_weight[0].astype(jnp.float32)
    kernel_imag = direction * filter_weight[1].astype(jnp.float32)
    return jnp.stack(
        [
            kernel_real * real_part - kernel_imag * imag_part,
            kernel_real * imag_part + kernel_imag * real_part,
        ]
    )


def exact_gelu(values):
    return jax.nn.gelu(values, approximate=False)


def spectral(values, filter_weight, direction):
    width = values.shape[2]
    rows_tab = row_table(width)
    rows = jnp.einsum(
        "pkw,bhwc->pbhkc", rows_tab, values, preferred_element_type=jnp.float32
    ).astype(jnp.bfloat16)
    columns = lax.all_to_all(rows, "space", split_axis=3, concat_axis=2, tiled=True)
    height = columns.shape[2]
    spectrum = jnp.einsum(
        "qmph,pbhkc->qbmkc", column_table(height, 1), columns, preferred_element_type=jnp.float32
    ).astype(jnp.bfloat16)
    weighted = apply_filter(spectrum, filter_weight[:, None], direction).astype(jnp.bfloat16)
    returned = jnp.einsum(
        "qmph,pbhkc->qbmkc", column_table(height, -1), weighted, preferred_element_type=jnp.float32
    ).astype(jnp.bfloat16)
    back_rows = lax.all_to_all(returned, "space", split_axis=2, concat_axis=3, tiled=True)
    output = jnp.einsum("pkw,pbhkc->bhwc", rows_tab, back_rows, preferred_element_type=jnp.float32)
    return (output, spectrum)


def plain_body(noisy_tokens, grad_out, filter_weight, weight_in, weight_out, gain_one, gain_two):
    batch, rows_dev, width, chans = noisy_tokens.shape
    inputs = noisy_tokens.astype(jnp.float32)
    normed_one, rstd_one = plain_layer_norm(inputs)
    mixed_in = (normed_one * gain_one).astype(jnp.bfloat16)
    spatial, spectrum = spectral(mixed_in, filter_weight, 1)
    normed_two, rstd_two = plain_layer_norm(spatial)
    mlp_in = (normed_two * gain_two).astype(jnp.bfloat16).reshape(-1, chans)
    preact = jnp.dot(mlp_in, weight_in, preferred_element_type=jnp.float32)
    activated = exact_gelu(preact).astype(jnp.bfloat16)
    mlp_out = jnp.dot(activated, weight_out, preferred_element_type=jnp.float32)
    block_out = (inputs + mlp_out.reshape(inputs.shape)).astype(jnp.bfloat16)
    upstream = grad_out.reshape(-1, chans)
    grad_act = jnp.dot(upstream, weight_out.T, preferred_element_type=jnp.float32)
    grad_pre = jax.vjp(exact_gelu, preact)[1](grad_act)[0].astype(jnp.bfloat16)
    sum_out = jnp.dot(activated.T, upstream, preferred_element_type=jnp.float32)
    sum_in = jnp.dot(mlp_in.T, grad_pre, preferred_element_type=jnp.float32)
    grad_mlp = jnp.dot(grad_pre, weight_in.T, preferred_element_type=jnp.float32).reshape(
        inputs.shape
    )
    grad_spatial, sum_gain_two = plain_norm_backward(grad_mlp, normed_two, rstd_two, gain_two)
    back_spatial, adjoint = spectral(grad_spatial.astype(jnp.bfloat16), filter_weight, -1)
    spec_f = spectrum.astype(jnp.float32)
    adj_f = adjoint.astype(jnp.float32)
    filter_terms = jnp.stack(
        [
            jnp.sum(adj_f[0] * spec_f[0] + adj_f[1] * spec_f[1], axis=0),
            jnp.sum(adj_f[1] * spec_f[0] - adj_f[0] * spec_f[1], axis=0),
        ]
    )
    grad_filter = lax.psum(filter_terms.astype(jnp.bfloat16), "copy").astype(jnp.float32)
    grad_normed, sum_gain_one = plain_norm_backward(back_spatial, normed_one, rstd_one, gain_one)
    grad_tokens = (grad_out.astype(jnp.float32) + grad_normed).astype(jnp.bfloat16)
    local_sums = (sum_in, sum_out, sum_gain_one, sum_gain_two)
    summed = lax.psum(
        (local_sums[0], local_sums[1], local_sums[2], local_sums[3]), ("copy", "space")
    )
    total_tokens = batch * lax.axis_size("copy") * rows_dev * lax.axis_size("space") * width
    factor = 1.0 / math.sqrt(total_tokens)
    return (
        block_out,
        grad_tokens,
        grad_filter,
        (summed[0] * factor).astype(jnp.bfloat16),
        (summed[1] * factor).astype(jnp.bfloat16),
        summed[2] * factor,
        summed[3] * factor,
    )


def solution(mesh):
    def program(*arrays):
        rows_dev, wide = arrays[0].shape[1], arrays[2].shape[2]
        tiled = rows_dev % 32 == 0 and wide % 16 == 0
        return (body if tiled else plain_body)(*arrays)

    return jax.shard_map(
        program,
        mesh=mesh,
        in_specs=(
            P("copy", "space", None, None),
            P("copy", "space", None, None),
            P(None, None, "space", None),
            P(),
            P(),
            P(),
            P(),
        ),
        out_specs=(
            P("copy", "space", None, None),
            P("copy", "space", None, None),
            P(None, None, "space", None),
            P(),
            P(),
            P(),
            P(),
        ),
        check_vma=False,
    )
```

```python
import functools
import math

import jax
import jax.numpy as jnp
import ml_dtypes
import numpy as np
from jax import lax
from jax.experimental import pallas as pl
from jax.experimental.pallas import tpu as pltpu
from jax.sharding import PartitionSpec as P

EPS = 1e-06
LANES = 128
VMEM_LIMIT = 60 * 1024 * 1024
BF16 = jnp.bfloat16
F32 = jnp.float32


def dft_pair(length):
    index = np.arange(length, dtype=np.int64)
    angle = (index[:, None] * index[None, :] % length) * (2.0 * math.pi / length)
    factor = 1.0 / math.sqrt(length)
    rounded = lambda a: a.astype(np.float32).astype(ml_dtypes.bfloat16).astype(np.float32)
    return rounded(np.cos(angle) * factor), rounded(np.sin(angle) * factor)


def row_tables(width, n):
    cosine, sine = dft_pair(width)
    own = width // n
    half = own // 2
    forward = np.zeros((n, 2, half, width), np.float32)
    weight = np.full((n, 2, half, 1), 2.0, np.float32)
    for d in range(n):
        first = own * d + (1 if d >= n // 2 else 0)
        forward[d, 0] = cosine[first : first + half]
        forward[d, 1] = -sine[first : first + half]
    forward[0, 1, 0] = cosine[width // 2]
    weight[0, :, 0] = 1.0
    shape = (n, 2 * half, width)
    return (
        forward.reshape(shape).astype(ml_dtypes.bfloat16),
        (forward * weight).reshape(shape).astype(ml_dtypes.bfloat16),
    )


def column_tables(height, n, chunks):
    cosine, sine = dft_pair(height)
    zero = np.zeros_like(cosine)
    rows = height // n // chunks

    def arrange(blocks):
        full = np.stack([np.stack(line, axis=1) for line in blocks])
        full = full.reshape(2 * height, 2, n, chunks, rows)
        return full.transpose(0, 3, 2, 1, 4).reshape(2 * height, 2 * height)

    middle = arrange([[zero, cosine], [zero, -sine]])
    first = arrange([[cosine, zero], [-sine, zero]])
    other = arrange([[cosine, sine], [-sine, cosine]])
    backward = np.stack([middle, first, other]).transpose(0, 2, 1)
    backward = backward.reshape(3, chunks, n, 2 * rows, 2 * height)
    return backward.astype(ml_dtypes.bfloat16)


def mirror_table(height):
    table = np.zeros((height, height), np.float32)
    table[np.arange(height), (-np.arange(height)) % height] = 1.0
    return table.astype(ml_dtypes.bfloat16)


def dot(a, b):
    return jnp.dot(a, b, preferred_element_type=F32)


def dot_tn(a, b):
    return lax.dot_general(a, b, (((0,), (0,)), ((), ())), preferred_element_type=F32)


def normalize(values):
    centred = values - jnp.mean(values, axis=-1, keepdims=True)
    variance = jnp.mean(centred * centred, axis=-1, keepdims=True)
    rstd = lax.rsqrt(variance + EPS)
    return centred * rstd, rstd


def norm_backward(upstream, normed, rstd, gain):
    scaled = upstream * gain
    return (
        scaled
        - jnp.mean(scaled, axis=-1, keepdims=True)
        - normed * jnp.mean(scaled * normed, axis=-1, keepdims=True)
    ) * rstd


def gelu_and_slope(v):
    e = jnp.exp(v * v * -0.5)
    d = 1.0 + (0.3275911 / math.sqrt(2.0)) * jnp.abs(v)
    t = pl.reciprocal(d, approx=True)
    t = t * (2.0 - d * t)
    poly = 0.5 * 1.061405429
    for coefficient in (-1.453152027, 1.421413741, -0.284496736, 0.254829592):
        poly = poly * t + 0.5 * coefficient
    tail = poly * t * e
    phi = jnp.where(v < 0.0, tail, 1.0 - tail)
    return v * phi, phi + v * e * (1.0 / math.sqrt(2.0 * math.pi))


def spaced(count):
    groups = -(-count // 8)
    return 8 * (groups + 1 - groups % 2)


def lanes(c):
    return slice(c * LANES, (c + 1) * LANES)


def unpack(received, scratch):
    count, rows, chans = received[0].shape
    pitch = spaced(rows)

    def step(k, carry):
        for s, ref in enumerate(received):
            start = pl.multiple_of((s * count + k) * pitch, 8)
            for c in range(chans // LANES):
                scratch[c, pl.ds(start, rows), :] = ref[k, :, lanes(c)].astype(F32)
        return carry

    lax.fori_loop(0, count, step, 0, unroll=2)


def read_row(scratch, row, columns, rows):
    parts = [
        scratch[c, pl.ds(row, columns, stride=spaced(rows)), :].astype(BF16)
        for c in range(scratch.shape[0])
    ]
    return jnp.concatenate(parts, axis=1)


def write_row(scratch, row, columns, values):
    start = pl.multiple_of(row * spaced(columns), 8)
    for c in range(scratch.shape[0]):
        scratch[c, pl.ds(start, columns), :] = values[:, lanes(c)]


def pack(scratch, columns, outgoing):
    count, rows, _ = outgoing[0].shape

    def step(k, carry):
        for s, ref in enumerate(outgoing):
            for c in range(scratch.shape[0]):
                part = scratch[c, pl.ds(s * count + k, rows, stride=spaced(columns)), :]
                ref[k, :, lanes(c)] = part.astype(BF16)
        return carry

    lax.fori_loop(0, count, step, 0, unroll=2)


def params():
    return pltpu.CompilerParams(vmem_limit_bytes=VMEM_LIMIT)


def resident(shape):
    return pl.BlockSpec(shape, lambda *_: (0,) * len(shape), pipeline_mode=pl.Buffered(1))


ANYWHERE = pl.BlockSpec(memory_space=pl.ANY)


def cost(flops, size):
    return pl.CostEstimate(flops=int(flops), bytes_accessed=int(size), transcendentals=0)


def shape_of(shape, dtype=BF16):
    return jax.ShapeDtypeStruct(tuple(shape), dtype)


def enter_kernel(n, tokens, gain, table, *rest):
    outgoing, scratch = rest[:n], rest[n]
    step = pl.program_id(0)
    block, width, _ = tokens.shape
    for r in range(block):
        normed, _ = normalize(tokens[r].astype(F32))
        mixed = (normed * gain[...]).astype(BF16)
        write_row(scratch, step * block + r, width, dot(table[...], mixed))

    @pl.when(step == pl.num_programs(0) - 1)
    def _():
        pack(scratch, width, outgoing)


def enter(tokens, gain, table, n, chunk, rows, block):
    _, width, chans = tokens.shape
    steps = rows // block
    out = (width // n, rows, chans)
    return pl.pallas_call(
        functools.partial(enter_kernel, n),
        grid=(steps,),
        in_specs=[
            pl.BlockSpec((block, width, chans), lambda i: (i + chunk * steps, 0, 0)),
            resident((1, chans)),
            resident((width, width)),
        ],
        out_specs=[resident(out)] * n,
        out_shape=[shape_of(out)] * n,
        scratch_shapes=[pltpu.VMEM((chans // LANES, rows * spaced(width), LANES), F32)],
        compiler_params=params(),
        cost_estimate=cost(2 * rows * width * width * chans, 4 * rows * width * chans),
        name="enter_rows",
    )(tokens, gain, table)


def mlp_kernel(
    n, extra, tokens, upstream, gain, table_out, table_in, w_in, w_out, w_in_t, w_out_t, *rest
):
    received, rest = rest[:n], rest[n + extra :]
    block_out, outgoing, rest = rest[0], rest[1 : n + 1], rest[n + 1 :]
    sum_in, sum_out, sum_gain, unpacked, packed = rest
    step = pl.program_id(0)
    block, width, chans = tokens.shape
    rows = received[0].shape[1]
    hidden = w_in.shape[1]
    part = min(512, hidden)

    @pl.when(step == 0)
    def _():
        unpack(received, unpacked)
        sum_in[...] = jnp.zeros_like(sum_in)
        sum_out[...] = jnp.zeros_like(sum_out)
        sum_gain[...] = jnp.zeros_like(sum_gain)

    spatial = jnp.concatenate(
        [
            dot(table_out[...], read_row(unpacked, step * block + r, width, rows))
            for r in range(block)
        ],
        axis=0,
    )
    normed, rstd = normalize(spatial)
    mlp_in = (normed * gain[...]).astype(BF16)
    grad = upstream[...].reshape(block * width, chans)
    out = tokens[...].reshape(block * width, chans).astype(F32)
    grad_mlp = jnp.zeros_like(spatial)

    def first(cols):
        return dot(mlp_in, w_in[:, cols]), dot(grad, w_out_t[:, cols])

    parts = [slice(f, f + part) for f in range(0, hidden, part)]
    ahead = first(parts[0])
    for f, cols in enumerate(parts):
        preact, grad_act = ahead
        if f + 1 < len(parts):
            ahead = first(parts[f + 1])
        value, slope = gelu_and_slope(preact)
        activated = value.astype(BF16)
        grad_pre = (grad_act * slope).astype(BF16)
        out = out + dot(activated, w_out[cols, :])
        grad_mlp = grad_mlp + dot(grad_pre, w_in_t[cols, :])
        sum_out[:, cols] += dot_tn(grad, activated)
        sum_in[:, cols] += dot_tn(mlp_in, grad_pre)
    block_out[...] = out.astype(BF16).reshape(block, width, chans)
    grad_spatial = norm_backward(grad_mlp, normed, rstd, gain[...])
    sum_gain[0:8] += jnp.sum((grad_mlp * normed).reshape(-1, 8, chans), axis=0)
    sum_gain[8:16] += jnp.sum((grad_spatial * spatial).reshape(-1, 8, chans), axis=0)
    sent = grad_spatial.astype(BF16)
    for r in range(block):
        values = dot(table_in[...], sent[r * width : (r + 1) * width])
        write_row(packed, step * block + r, width, values)

    @pl.when(step == pl.num_programs(0) - 1)
    def _():
        pack(packed, width, outgoing)


def mlp(received, tokens, upstream, gain, tables, weights, previous, chunk, block):
    n = len(received)
    count, rows, chans = received[0].shape
    width = tokens.shape[1]
    hidden = weights[0].shape[1]
    steps = rows // block
    by_rows = pl.BlockSpec((block, width, chans), lambda i: (i + chunk * steps, 0, 0))
    operands = [tokens, upstream, gain, *tables, *weights, *received]
    in_specs = [
        by_rows,
        by_rows,
        resident((1, chans)),
        resident((width, width)),
        resident((width, width)),
        resident((chans, hidden)),
        resident((hidden, chans)),
        resident((hidden, chans)),
        resident((chans, hidden)),
    ] + [resident((count, rows, chans))] * n
    aliases = {}
    if previous is not None:
        aliases = {len(operands): 0}
        operands.append(previous)
        in_specs.append(ANYWHERE)
    flops = 2 * rows * width * chans * (6 * hidden + 2 * width)
    outputs = pl.pallas_call(
        functools.partial(mlp_kernel, n, len(aliases)),
        grid=(steps,),
        in_specs=in_specs,
        out_specs=[by_rows]
        + [resident((count, rows, chans))] * n
        + [resident((chans, hidden)), resident((chans, hidden)), resident((16, chans))],
        out_shape=[shape_of(tokens.shape)]
        + [shape_of((count, rows, chans))] * n
        + [shape_of((chans, hidden), F32)] * 2
        + [shape_of((16, chans), F32)],
        scratch_shapes=[
            pltpu.VMEM((chans // LANES, width * spaced(rows), LANES), F32),
            pltpu.VMEM((chans // LANES, rows * spaced(width), LANES), F32),
        ],
        input_output_aliases=aliases,
        compiler_params=params(),
        cost_estimate=cost(flops, 10 * rows * width * chans),
        name="mlp_rows",
    )(*operands)
    return outputs[0], outputs[1 : n + 1], outputs[n + 1 :]


def leave_kernel(n, tokens, upstream, gain, table_out, *rest):
    received, (grad_tokens, unpacked) = rest[:n], rest[-2:]
    step = pl.program_id(0)
    block, width, _ = tokens.shape
    rows = received[0].shape[1]

    @pl.when(step == 0)
    def _():
        unpack(received, unpacked)

    for r in range(block):
        back = dot(table_out[...], read_row(unpacked, step * block + r, width, rows))
        normed, rstd = normalize(tokens[r].astype(F32))
        grad = norm_backward(back, normed, rstd, gain[...])
        grad_tokens[r] = (upstream[r].astype(F32) + grad).astype(BF16)


def leave(received, tokens, upstream, gain, table_out, previous, chunk, block):
    n = len(received)
    count, rows, chans = received[0].shape
    width = tokens.shape[1]
    steps = rows // block
    by_rows = pl.BlockSpec((block, width, chans), lambda i: (i + chunk * steps, 0, 0))
    operands = [tokens, upstream, gain, table_out, *received]
    in_specs = [by_rows, by_rows, resident((1, chans)), resident((width, width))]
    in_specs += [resident((count, rows, chans))] * n
    aliases = {}
    if previous is not None:
        aliases = {len(operands): 0}
        operands.append(previous)
        in_specs.append(ANYWHERE)
    return pl.pallas_call(
        functools.partial(leave_kernel, n),
        grid=(steps,),
        in_specs=in_specs,
        out_specs=by_rows,
        out_shape=shape_of(tokens.shape),
        scratch_shapes=[pltpu.VMEM((chans // LANES, width * spaced(rows), LANES), F32)],
        input_output_aliases=aliases,
        compiler_params=params(),
        cost_estimate=cost(2 * rows * width * width * chans, 8 * rows * width * chans),
        name="leave_rows",
    )(*operands)


def columns_kernel(count, back, after, flags, table_f, table_b, kernel, *rest):
    spectrum, rest = (rest[0], rest[1:]) if back else (None, rest)
    received, rest = rest[:count], rest[count + after :]
    outgoing, held = rest[:count], rest[count]
    step, last = pl.program_id(0), pl.num_programs(0) - 1
    per, _, height, chans = kernel.shape
    _, _, rows, _ = received[0].shape

    def load(j):
        return jnp.concatenate([ref[:, j].reshape(2 * rows, chans) for ref in received], axis=0)

    def store(j, values):
        values = values.astype(BF16)
        for i, ref in enumerate(outgoing):
            part = values[i * 2 * rows : (i + 1) * 2 * rows]
            ref[:, j] = part.reshape(2, rows, chans)

    def filtered(slot, found):
        found = found.astype(BF16)
        real, imag = found[:height].astype(F32), found[height:].astype(F32)
        k_real, k_imag = kernel[slot, 0].astype(F32), kernel[slot, 1].astype(F32)
        if back:
            s_real, s_imag = spectrum[slot, 0].astype(F32), spectrum[slot, 1].astype(F32)
            held[slot, 0] = (real * s_real + imag * s_imag).astype(BF16)
            held[slot, 1] = (imag * s_real - real * s_imag).astype(BF16)
            k_imag = -k_imag
        else:
            held[slot, 0] = found[:height]
            held[slot, 1] = found[height:]
        upper = (k_real * real - k_imag * imag).astype(BF16)
        lower = (k_real * imag + k_imag * real).astype(BF16)
        return jnp.concatenate([upper, lower], axis=0)

    @pl.when(step < last)
    def _():
        at = [1 + step * per + i for i in range(per)]
        found = dot(table_f[2], jnp.concatenate([load(j) for j in at], axis=1))
        weighted = [filtered(i, found[:, i * chans : (i + 1) * chans]) for i in range(per)]
        result = dot(table_b[2], jnp.concatenate(weighted, axis=1))
        for i, j in enumerate(at):
            store(j, result[:, i * chans : (i + 1) * chans])

    @pl.when(step == last)
    def _():
        values = load(0)
        kind = 2 - flags[1]
        zero = filtered(0, dot(table_f[kind], values))
        middle = filtered(1, dot(table_f[0], values))
        store(0, dot(table_b[kind], zero) + dot(table_b[0], middle))
        for i in range(2, per):
            held[i] = jnp.zeros_like(held[i])


def columns(flags, tables, kernel, received, spectrum, after=()):
    count = len(received)
    _, half, rows, chans = received[0].shape
    slots, _, height, _ = kernel.shape
    per = columns_per_step(half)
    held = pl.BlockSpec((per, 2, height, chans), lambda t, flags: (t, 0, 0, 0))
    table = resident((3, 2 * height, 2 * height))
    back = spectrum is not None
    outputs = pl.pallas_call(
        functools.partial(columns_kernel, count, back, len(after)),
        grid_spec=pltpu.PrefetchScalarGridSpec(
            num_scalar_prefetch=1,
            grid=(slots // per,),
            in_specs=[table, table, held]
            + [held] * back
            + [resident(r.shape) for r in received]
            + [ANYWHERE] * len(after),
            out_specs=[resident(r.shape) for r in received] + [held],
        ),
        out_shape=[shape_of(r.shape) for r in received] + [shape_of(kernel.shape)],
        compiler_params=params(),
        cost_estimate=cost(16 * height * height * chans * slots, 20 * height * chans * slots),
        name="filter_columns",
    )(flags, *tables, kernel, *([spectrum] if back else []), *received, *after)
    return outputs[:count], outputs[count]


def columns_per_step(half):
    return 3 if (half - 1) % 3 == 0 else 2 if (half - 1) % 2 == 0 else 1


def slot_count(half):
    per = max(2, columns_per_step(half))
    return half - 1 + per


def filter_part_kernel(copies, flags, mirror, own, *rest):
    mains, extras = rest[:copies], rest[copies : 2 * copies]
    kernel, scr_own, scr_main, scr_extra = rest[2 * copies :]
    part = pl.program_id(0)
    upper, first, me = flags[0], flags[1], flags[2]
    _, height, wide, _ = own.shape
    half = wide // 2
    share = height // copies
    pitch_own, pitch = spaced(wide), spaced(half)

    def spread_own(m, carry):
        scr_own[pl.ds(pl.multiple_of(m * pitch_own, 8), wide), :] = own[0, m].astype(F32)
        return carry

    lax.fori_loop(0, height, spread_own, 0, unroll=8)
    for i in range(copies):
        owner = jnp.bitwise_xor(me, i)

        def spread_main(m, carry):
            at = pl.multiple_of((owner * share + m) * pitch, 8)
            scr_main[pl.ds(at, half), :] = mains[i][0, m].astype(F32)
            return carry

        lax.fori_loop(0, share, spread_main, 0, unroll=8)
        at = pl.multiple_of(owner * share, share)
        scr_extra[pl.ds(at, share), :] = extras[i][0].astype(F32)
    sign = jnp.where(part == 0, 0.5, -0.5)
    extra = scr_extra[...]
    middle = 0.5 * extra + sign * dot(mirror[...], extra.astype(BF16))
    kernel[half, 0] = jnp.where(first == 1, middle, 0.0).astype(BF16)
    for i in range(half + 1, kernel.shape[0]):
        kernel[i, 0] = jnp.zeros((height, LANES), BF16)
    for j in range(half):
        mine = scr_own[pl.ds(j + upper, height, stride=pitch_own), :]
        if j == 0:
            other = scr_main[pl.ds(half - 1, height, stride=pitch), :]
            lower = jnp.where(first == 1, mine, extra)
            other = jnp.where(upper == 1, other, lower)
        else:
            other = scr_main[pl.ds(half - j - upper, height, stride=pitch), :]
        turned = dot(mirror[...], other.astype(BF16))
        kernel[(j - 1) % half, 0] = (0.5 * mine + sign * turned).astype(BF16)


def filter_part(flags, mirror, own, mains, extras):
    _, height, wide, chans = own.shape
    copies = len(mains)
    half, share = wide // 2, height // copies
    slots = slot_count(half)
    return pl.pallas_call(
        functools.partial(filter_part_kernel, copies),
        grid_spec=pltpu.PrefetchScalarGridSpec(
            num_scalar_prefetch=1,
            grid=(2, chans // LANES),
            in_specs=[
                pl.BlockSpec((height, height), lambda p, c, flags: (0, 0)),
                pl.BlockSpec((1, height, wide, LANES), lambda p, c, flags: (p, 0, 0, c)),
            ]
            + [pl.BlockSpec((1, share, half, LANES), lambda p, c, flags: (p, 0, 0, c))] * copies
            + [pl.BlockSpec((1, share, LANES), lambda p, c, flags: (p, 0, c))] * copies,
            out_specs=pl.BlockSpec((slots, 1, height, LANES), lambda p, c, flags: (0, p, 0, c)),
            scratch_shapes=[
                pltpu.VMEM((height * spaced(wide), LANES), F32),
                pltpu.VMEM((height * spaced(half), LANES), F32),
                pltpu.VMEM((height, LANES), F32),
            ],
        ),
        out_shape=shape_of((slots, 2, height, chans)),
        compiler_params=params(),
        cost_estimate=cost(4 * height * height * chans * half, 16 * height * half * chans),
        name="filter_part",
    )(flags, mirror, own, *mains, *extras)


def filter_gradient_kernel(copies, flags, mirror, *rest):
    mine, theirs = rest[:copies], rest[copies : 2 * copies]
    out, gathered, turned = rest[2 * copies :]
    part = pl.program_id(0)
    upper, me = flags[0], flags[2]
    _, height, wide, _ = out.shape
    half = wide // 2
    share = height // copies
    pitch = spaced(height)
    for i in range(copies):
        at = pl.multiple_of(jnp.bitwise_xor(me, i) * share, share)
        gathered[0:half, pl.ds(at, share), :] = mine[i][:, 0]
        gathered[half:, pl.ds(at, share), :] = theirs[i][:, 0]
    sign = jnp.where(part == 0, 1.0, -1.0)
    for k in range(wide):
        if k == 0:
            index = jnp.where(upper == 1, 2 * half, half - 1)
        elif k < half:
            index = k - 1 - upper
            index = jnp.where(index < 0, half - 1, index)
        elif k == half:
            index = jnp.where(upper == 1, half - 2, 2 * half - 2)
        else:
            index = wide - 2 - k + upper
            index = half + jnp.where(index < 0, half - 1, index)
        value = gathered[index]
        if 0 < k < half:
            value = value.astype(F32)
        else:
            other = sign * dot(mirror[...], value)
            if k == 0:
                other = jnp.where(upper == 1, other, value.astype(F32))
            elif k == half:
                other = jnp.where(upper == 1, value.astype(F32), other)
            value = other
        turned[pl.ds(k * pitch, height), :] = value

    def step(m, carry):
        out[0, m] = turned[pl.ds(m, wide, stride=pitch), :]
        return carry

    lax.fori_loop(0, height, step, 0, unroll=8)


def filter_gradient(flags, mirror, mine, theirs, height, wide):
    _, _, share, chans = mine[0].shape
    copies, half = len(mine), wide // 2
    block = lambda slots: pl.BlockSpec(
        (slots, 1, share, LANES), lambda p, c, flags: (0, p, 0, c)
    )
    return pl.pallas_call(
        functools.partial(filter_gradient_kernel, copies),
        grid_spec=pltpu.PrefetchScalarGridSpec(
            num_scalar_prefetch=1,
            grid=(2, chans // LANES),
            in_specs=[pl.BlockSpec((height, height), lambda p, c, flags: (0, 0))]
            + [block(half)] * copies
            + [block(half + 1)] * copies,
            out_specs=pl.BlockSpec((1, height, wide, LANES), lambda p, c, flags: (p, 0, 0, c)),
            scratch_shapes=[
                pltpu.VMEM((wide + 1, height, LANES), BF16),
                pltpu.VMEM((wide * spaced(height), LANES), F32),
            ],
        ),
        out_shape=shape_of((2, height, wide, chans), F32),
        compiler_params=params(),
        cost_estimate=cost(2 * height * height * chans * wide, 12 * height * wide * chans),
        name="filter_gradient",
    )(flags, mirror, *mine, *theirs)


def swap(value, axis, size, partner):
    return lax.ppermute(value, axis, [(i, partner(i)) for i in range(size)])


def swap_bits(value, axis, size, bits):
    return swap(value, axis, size, lambda i: i ^ bits)


def exchange(blocks):
    n = len(blocks)
    moved = {s: swap_bits(blocks[s], "space", n, s) for s in range(n - 1, 0, -1)}
    return [blocks[0]] + [moved[s] for s in range(1, n)]


def gather_copies(value, copies):
    parts = {0: value}
    bit = copies // 2
    while bit:
        for key in list(parts):
            parts[key ^ bit] = swap_bits(parts[key], "copy", copies, bit)
        bit //= 2
    return [parts[i] for i in range(copies)]


def reduce_copies(value, copies, axis):
    me = lax.axis_index("copy")
    bit = 1
    while bit < copies:
        size = value.shape[axis] // 2
        mine = (me // bit) % 2
        kept = lax.dynamic_slice_in_dim(value, mine * size, size, axis)
        sent = lax.dynamic_slice_in_dim(value, (1 - mine) * size, size, axis)
        other = swap_bits(sent, "copy", copies, bit)
        value = (kept.astype(F32) + other.astype(F32)).astype(value.dtype)
        bit *= 2
    return value


def share_order(copies):
    digits = copies.bit_length() - 1
    return [int(format(i, "b").zfill(digits)[::-1], 2) if digits else 0 for i in range(copies)]


def body(noisy_tokens, grad_out, filter_weight, weight_in, weight_out, gain_one, gain_two):
    _, rows_dev, width, chans = noisy_tokens.shape
    height, wide = filter_weight.shape[1:3]
    hidden = weight_in.shape[1]
    half = wide // 2
    n, copies = lax.axis_size("space"), lax.axis_size("copy")
    chunks = 2
    rows = rows_dev // chunks
    tokens, upstream = noisy_tokens[0], grad_out[0]
    me, copy = lax.axis_index("space"), lax.axis_index("copy")
    order = share_order(copies)

    share = height // copies
    mine = lax.dynamic_slice_in_dim(filter_weight, copy * share, share, 1)
    opposite = lambda d: n - 1 - d
    main = swap(mine[:, :, half:], "space", n, opposite)
    to_lower = [(n // 2, 0)] + [(e, n - e) for e in range(n // 2 + 1, n)]
    single = lax.ppermute(mine[:, :, 0], "space", to_lower)
    mains, singles = gather_copies(main, copies), gather_copies(single, copies)

    others = jnp.bitwise_xor(me, jnp.arange(n, dtype=me.dtype))
    forward, weighted = row_tables(width, n)
    table_in = jnp.take(jnp.asarray(forward), others, axis=0).reshape(width, width)
    table_out = jnp.take(jnp.asarray(weighted), others, axis=0).reshape(width, width).T
    table_b = jnp.take(jnp.asarray(column_tables(height, n, chunks)), others, axis=2)
    table_b = table_b.reshape(3, 2 * height, 2 * height)
    column_tabs = (jnp.swapaxes(table_b, 1, 2), table_b)
    mirror = jnp.asarray(mirror_table(height))
    gain_a, gain_b = gain_one.reshape(1, chans), gain_two.reshape(1, chans)
    upper = (me >= n // 2).astype(jnp.int32)
    first = (me == 0).astype(jnp.int32)

    def flags(index):
        return jnp.stack([upper, first, index.astype(jnp.int32)])

    def split(blocks):
        return [b.reshape(2, half, rows, chans) for b in blocks]

    def join(blocks):
        return [b.reshape(wide, rows, chans) for b in blocks]

    def by_chunk(blocks):
        return [join(blocks[c * n : (c + 1) * n]) for c in range(chunks)]

    arrived = []
    for c in range(chunks):
        arrived += split(exchange(enter(tokens, gain_a, table_in, n, c, rows, 2)))
    kernel = filter_part(flags(copy), mirror, filter_weight, mains, singles)
    returned, spectrum = columns(flags(copy), column_tabs, kernel, arrived, None)

    weights = (weight_in, weight_out, weight_in.T, weight_out.T)
    tables = (table_out, table_in)
    block_out = None
    sums, arrived = [], []
    for c, blocks in enumerate(by_chunk(returned)):
        block_out, sent, local = mlp(
            exchange(blocks), tokens, upstream, gain_b, tables, weights, block_out, c, 4
        )
        arrived += split(exchange(sent))
        sums.append(local)

    sum_in, sum_out, sum_gain = (a + b for a, b in zip(*sums))
    both = reduce_copies(jnp.concatenate([sum_in, sum_out], axis=0), copies, 0)
    gains = jnp.concatenate([jnp.sum(sum_gain[8:], axis=0) / gain_one, jnp.sum(sum_gain[:8], axis=0)])
    bit = 1
    while bit < copies:
        gains = gains + swap_bits(gains, "copy", copies, bit)
        bit *= 2
    gains = jnp.pad(gains[None], ((0, 7), (0, hidden - 2 * chans)))
    local = jnp.concatenate([both, gains], axis=0)

    returned, terms = columns(
        flags(copy), column_tabs, kernel, arrived, spectrum, after=(local,)
    )
    total_tokens = copies * rows_dev * n * width
    summed = lax.psum(local, "space") * (1.0 / math.sqrt(total_tokens))
    size = both.shape[0]
    shares = lax.all_gather(summed[:size].astype(BF16), "copy")
    shares = jnp.concatenate([shares[order.index(i)] for i in range(copies)], axis=0)
    grad_in, grad_out_t = shares[:chans], shares[chans:]

    grad_tokens = None
    for c, blocks in enumerate(by_chunk(returned)):
        grad_tokens = leave(
            exchange(blocks), tokens, upstream, gain_a, table_out, grad_tokens, c, 2
        )

    reduced = reduce_copies(terms[: half + 1], copies, 2)
    mirrored = swap(reduced[:half], "space", n, opposite)
    to_upper = [(0, n // 2)] + [(d, n - d) for d in range(1, n // 2)]
    single = lax.ppermute(
        jnp.where(me == 0, reduced[half], reduced[half - 1]), "space", to_upper
    )
    mine = gather_copies(reduced[:half], copies)
    theirs = gather_copies(jnp.concatenate([mirrored, single[None]], axis=0), copies)
    index = jnp.asarray(order, jnp.int32)[copy]
    grad_filter = filter_gradient(
        flags(index),
        mirror,
        [mine[order[i]] for i in range(copies)],
        [theirs[order[i]] for i in range(copies)],
        height,
        wide,
    )
    return (
        block_out[None],
        grad_tokens[None],
        grad_filter,
        grad_in,
        grad_out_t.T,
        summed[size, :chans],
        summed[size, chans : 2 * chans],
    )


def dft_parts(length):
    index = jnp.arange(length, dtype=jnp.int32)
    phase = index[:, None] * index[None, :] % length
    angle = phase.astype(jnp.float32) * (2.0 * math.pi / length)
    factor = 1.0 / math.sqrt(length)
    return (
        (jnp.cos(angle) * factor).astype(jnp.bfloat16),
        (jnp.sin(angle) * factor).astype(jnp.bfloat16),
    )


def row_table(length):
    cosine, sine = dft_parts(length)
    return jnp.stack([cosine, -sine])


def column_table(length, direction):
    cosine, sine = dft_parts(length)
    upper = jnp.stack([cosine, direction * sine], axis=1)
    lower = jnp.stack([-direction * sine, cosine], axis=1)
    return jnp.stack([upper, lower])


def plain_layer_norm(values):
    centre = jnp.mean(values, axis=-1, keepdims=True)
    centred = values - centre
    variance = jnp.mean(centred * centred, axis=-1, keepdims=True)
    rstd_value = lax.rsqrt(variance + EPS)
    return (centred * rstd_value, rstd_value)


def plain_norm_backward(upstream, normed, rstd_value, gain):
    scaled = upstream * gain
    result = (
        scaled
        - jnp.mean(scaled, axis=-1, keepdims=True)
        - normed * jnp.mean(scaled * normed, axis=-1, keepdims=True)
    ) * rstd_value
    lead = tuple(range(upstream.ndim - 1))
    return (result, jnp.sum(upstream * normed, axis=lead))


def apply_filter(spectrum, filter_weight, direction):
    real_part = spectrum[0].astype(jnp.float32)
    imag_part = spectrum[1].astype(jnp.float32)
    kernel_real = filter_weight[0].astype(jnp.float32)
    kernel_imag = direction * filter_weight[1].astype(jnp.float32)
    return jnp.stack(
        [
            kernel_real * real_part - kernel_imag * imag_part,
            kernel_real * imag_part + kernel_imag * real_part,
        ]
    )


def exact_gelu(values):
    return jax.nn.gelu(values, approximate=False)


def spectral(values, filter_weight, direction):
    width = values.shape[2]
    rows_tab = row_table(width)
    rows = jnp.einsum(
        "pkw,bhwc->pbhkc", rows_tab, values, preferred_element_type=jnp.float32
    ).astype(jnp.bfloat16)
    columns = lax.all_to_all(rows, "space", split_axis=3, concat_axis=2, tiled=True)
    height = columns.shape[2]
    spectrum = jnp.einsum(
        "qmph,pbhkc->qbmkc", column_table(height, 1), columns, preferred_element_type=jnp.float32
    ).astype(jnp.bfloat16)
    weighted = apply_filter(spectrum, filter_weight[:, None], direction).astype(jnp.bfloat16)
    returned = jnp.einsum(
        "qmph,pbhkc->qbmkc", column_table(height, -1), weighted, preferred_element_type=jnp.float32
    ).astype(jnp.bfloat16)
    back_rows = lax.all_to_all(returned, "space", split_axis=2, concat_axis=3, tiled=True)
    output = jnp.einsum("pkw,pbhkc->bhwc", rows_tab, back_rows, preferred_element_type=jnp.float32)
    return (output, spectrum)


def plain_body(noisy_tokens, grad_out, filter_weight, weight_in, weight_out, gain_one, gain_two):
    batch, rows_dev, width, chans = noisy_tokens.shape
    inputs = noisy_tokens.astype(jnp.float32)
    normed_one, rstd_one = plain_layer_norm(inputs)
    mixed_in = (normed_one * gain_one).astype(jnp.bfloat16)
    spatial, spectrum = spectral(mixed_in, filter_weight, 1)
    normed_two, rstd_two = plain_layer_norm(spatial)
    mlp_in = (normed_two * gain_two).astype(jnp.bfloat16).reshape(-1, chans)
    preact = jnp.dot(mlp_in, weight_in, preferred_element_type=jnp.float32)
    activated = exact_gelu(preact).astype(jnp.bfloat16)
    mlp_out = jnp.dot(activated, weight_out, preferred_element_type=jnp.float32)
    block_out = (inputs + mlp_out.reshape(inputs.shape)).astype(jnp.bfloat16)
    upstream = grad_out.reshape(-1, chans)
    grad_act = jnp.dot(upstream, weight_out.T, preferred_element_type=jnp.float32)
    grad_pre = jax.vjp(exact_gelu, preact)[1](grad_act)[0].astype(jnp.bfloat16)
    sum_out = jnp.dot(activated.T, upstream, preferred_element_type=jnp.float32)
    sum_in = jnp.dot(mlp_in.T, grad_pre, preferred_element_type=jnp.float32)
    grad_mlp = jnp.dot(grad_pre, weight_in.T, preferred_element_type=jnp.float32).reshape(
        inputs.shape
    )
    grad_spatial, sum_gain_two = plain_norm_backward(grad_mlp, normed_two, rstd_two, gain_two)
    back_spatial, adjoint = spectral(grad_spatial.astype(jnp.bfloat16), filter_weight, -1)
    spec_f = spectrum.astype(jnp.float32)
    adj_f = adjoint.astype(jnp.float32)
    filter_terms = jnp.stack(
        [
            jnp.sum(adj_f[0] * spec_f[0] + adj_f[1] * spec_f[1], axis=0),
            jnp.sum(adj_f[1] * spec_f[0] - adj_f[0] * spec_f[1], axis=0),
        ]
    )
    grad_filter = lax.psum(filter_terms.astype(jnp.bfloat16), "copy").astype(jnp.float32)
    grad_normed, sum_gain_one = plain_norm_backward(back_spatial, normed_one, rstd_one, gain_one)
    grad_tokens = (grad_out.astype(jnp.float32) + grad_normed).astype(jnp.bfloat16)
    local_sums = (sum_in, sum_out, sum_gain_one, sum_gain_two)
    summed = lax.psum(
        (local_sums[0], local_sums[1], local_sums[2], local_sums[3]), ("copy", "space")
    )
    total_tokens = batch * lax.axis_size("copy") * rows_dev * lax.axis_size("space") * width
    factor = 1.0 / math.sqrt(total_tokens)
    return (
        block_out,
        grad_tokens,
        grad_filter,
        (summed[0] * factor).astype(jnp.bfloat16),
        (summed[1] * factor).astype(jnp.bfloat16),
        summed[2] * factor,
        summed[3] * factor,
    )


def solution(mesh):
    def program(*arrays):
        rows_dev, wide = arrays[0].shape[1], arrays[2].shape[2]
        n = lax.axis_size("space")
        tiled = rows_dev % 32 == 0 and wide % 32 == 0 and n & (n - 1) == 0
        return (body if tiled else plain_body)(*arrays)

    return jax.shard_map(
        program,
        mesh=mesh,
        in_specs=(
            P("copy", "space", None, None),
            P("copy", "space", None, None),
            P(None, None, "space", None),
            P(),
            P(),
            P(),
            P(),
        ),
        out_specs=(
            P("copy", "space", None, None),
            P("copy", "space", None, None),
            P(None, None, "space", None),
            P(),
            P(),
            P(),
            P(),
        ),
        check_vma=False,
    )
```

```python
import functools
import math

import jax
import jax.numpy as jnp
import ml_dtypes
import numpy as np
from jax import lax
from jax.experimental import pallas as pl
from jax.experimental.pallas import tpu as pltpu
from jax.sharding import PartitionSpec as P

EPS = 1e-06
LANES = 128
VMEM_LIMIT = 60 * 1024 * 1024
BF16 = jnp.bfloat16
F32 = jnp.float32


def dft_pair(length):
    index = np.arange(length, dtype=np.int64)
    angle = (index[:, None] * index[None, :] % length) * (2.0 * math.pi / length)
    factor = 1.0 / math.sqrt(length)
    rounded = lambda a: a.astype(np.float32).astype(ml_dtypes.bfloat16).astype(np.float32)
    return rounded(np.cos(angle) * factor), rounded(np.sin(angle) * factor)


def row_tables(width, n):
    cosine, sine = dft_pair(width)
    own = width // n
    half = own // 2
    forward = np.zeros((n, 2, half, width), np.float32)
    weight = np.full((n, 2, half, 1), 2.0, np.float32)
    for d in range(n):
        first = own * d + (1 if d >= n // 2 else 0)
        forward[d, 0] = cosine[first : first + half]
        forward[d, 1] = -sine[first : first + half]
    forward[0, 1, 0] = cosine[width // 2]
    weight[0, :, 0] = 1.0
    shape = (n, 2 * half, width)
    return (
        forward.reshape(shape).astype(ml_dtypes.bfloat16),
        (forward * weight).reshape(shape).astype(ml_dtypes.bfloat16),
    )


def column_tables(height, n, chunks):
    cosine, sine = dft_pair(height)
    zero = np.zeros_like(cosine)
    rows = height // n // chunks

    def arrange(blocks):
        full = np.stack([np.stack(line, axis=1) for line in blocks])
        full = full.reshape(2 * height, 2, n, chunks, rows)
        return full.transpose(0, 3, 2, 1, 4).reshape(2 * height, 2 * height)

    middle = arrange([[zero, cosine], [zero, -sine]])
    first = arrange([[cosine, zero], [-sine, zero]])
    other = arrange([[cosine, sine], [-sine, cosine]])
    backward = np.stack([middle, first, other]).transpose(0, 2, 1)
    backward = backward.reshape(3, chunks, n, 2 * rows, 2 * height)
    return backward.astype(ml_dtypes.bfloat16)


def mirror_table(height):
    table = np.zeros((height, height), np.float32)
    table[np.arange(height), (-np.arange(height)) % height] = 1.0
    return table.astype(ml_dtypes.bfloat16)


def dot(a, b):
    return jnp.dot(a, b, preferred_element_type=F32)


def dot_tn(a, b):
    return lax.dot_general(a, b, (((0,), (0,)), ((), ())), preferred_element_type=F32)


def normalize(values):
    centred = values - jnp.mean(values, axis=-1, keepdims=True)
    variance = jnp.mean(centred * centred, axis=-1, keepdims=True)
    rstd = lax.rsqrt(variance + EPS)
    return centred * rstd, rstd


def norm_backward(upstream, normed, rstd, gain):
    scaled = upstream * gain
    return (
        scaled
        - jnp.mean(scaled, axis=-1, keepdims=True)
        - normed * jnp.mean(scaled * normed, axis=-1, keepdims=True)
    ) * rstd


def gelu_and_slope(v):
    e = jnp.exp(v * v * -0.5)
    d = 1.0 + (0.3275911 / math.sqrt(2.0)) * jnp.abs(v)
    t = pl.reciprocal(d, approx=True)
    t = t * (2.0 - d * t)
    poly = 0.5 * 1.061405429
    for coefficient in (-1.453152027, 1.421413741, -0.284496736, 0.254829592):
        poly = poly * t + 0.5 * coefficient
    tail = poly * t * e
    phi = jnp.where(v < 0.0, tail, 1.0 - tail)
    return v * phi, phi + v * e * (1.0 / math.sqrt(2.0 * math.pi))


def spaced(count):
    groups = -(-count // 8)
    return 8 * (groups + 1 - groups % 2)


def lanes(c):
    return slice(c * LANES, (c + 1) * LANES)


def unpack(received, scratch):
    count, rows, chans = received[0].shape
    pitch = spaced(rows)

    def step(k, carry):
        for s, ref in enumerate(received):
            start = pl.multiple_of((s * count + k) * pitch, 8)
            for c in range(chans // LANES):
                scratch[c, pl.ds(start, rows), :] = ref[k, :, lanes(c)].astype(F32)
        return carry

    lax.fori_loop(0, count, step, 0, unroll=2)


def read_row(scratch, row, columns, rows):
    parts = [
        scratch[c, pl.ds(row, columns, stride=spaced(rows)), :].astype(BF16)
        for c in range(scratch.shape[0])
    ]
    return jnp.concatenate(parts, axis=1)


def write_row(scratch, row, columns, values):
    start = pl.multiple_of(row * spaced(columns), 8)
    for c in range(scratch.shape[0]):
        scratch[c, pl.ds(start, columns), :] = values[:, lanes(c)]


def pack(scratch, columns, outgoing):
    count, rows, _ = outgoing[0].shape

    def step(k, carry):
        for s, ref in enumerate(outgoing):
            for c in range(scratch.shape[0]):
                part = scratch[c, pl.ds(s * count + k, rows, stride=spaced(columns)), :]
                ref[k, :, lanes(c)] = part.astype(BF16)
        return carry

    lax.fori_loop(0, count, step, 0, unroll=2)


def params():
    return pltpu.CompilerParams(vmem_limit_bytes=VMEM_LIMIT)


def resident(shape):
    return pl.BlockSpec(shape, lambda *_: (0,) * len(shape), pipeline_mode=pl.Buffered(1))


ANYWHERE = pl.BlockSpec(memory_space=pl.ANY)


def cost(flops, size):
    return pl.CostEstimate(flops=int(flops), bytes_accessed=int(size), transcendentals=0)


def shape_of(shape, dtype=BF16):
    return jax.ShapeDtypeStruct(tuple(shape), dtype)


def enter_kernel(tokens, gain, table, *rest):
    outgoing, scratch = rest[-2:-1], rest[-1]
    step = pl.program_id(0)
    block, width, _ = tokens.shape
    for r in range(block):
        normed, _ = normalize(tokens[r].astype(F32))
        mixed = (normed * gain[...]).astype(BF16)
        write_row(scratch, step * block + r, width, dot(table[...], mixed))

    @pl.when(step == pl.num_programs(0) - 1)
    def _():
        pack(scratch, width, outgoing)


def enter(tokens, gain, table, chunk, rows, block, after):
    _, width, chans = tokens.shape
    steps = rows // block
    out = (width, rows, chans)
    return pl.pallas_call(
        enter_kernel,
        grid=(steps,),
        in_specs=[
            pl.BlockSpec((block, width, chans), lambda i: (i + chunk * steps, 0, 0)),
            resident((1, chans)),
            resident((width, width)),
        ]
        + [ANYWHERE] * len(after),
        out_specs=resident(out),
        out_shape=shape_of(out),
        scratch_shapes=[pltpu.VMEM((chans // LANES, rows * spaced(width), LANES), F32)],
        compiler_params=params(),
        cost_estimate=cost(2 * rows * width * width * chans, 4 * rows * width * chans),
        name="enter_rows",
    )(tokens, gain, table, *after)


def mlp_kernel(
    n, extra, tokens, upstream, gain, table_out, table_in, w_in, w_out, w_in_t, w_out_t, *rest
):
    received, rest = rest[:n], rest[n + extra :]
    block_out, outgoing, rest = rest[0], rest[1 : n + 1], rest[n + 1 :]
    sum_in, sum_out, sum_gain, unpacked, packed = rest
    step = pl.program_id(0)
    block, width, chans = tokens.shape
    rows = received[0].shape[1]
    hidden = w_in.shape[1]
    part = min(512, hidden)

    @pl.when(step == 0)
    def _():
        unpack(received, unpacked)
        sum_in[...] = jnp.zeros_like(sum_in)
        sum_out[...] = jnp.zeros_like(sum_out)
        sum_gain[...] = jnp.zeros_like(sum_gain)

    spatial = jnp.concatenate(
        [
            dot(table_out[...], read_row(unpacked, step * block + r, width, rows))
            for r in range(block)
        ],
        axis=0,
    )
    normed, rstd = normalize(spatial)
    mlp_in = (normed * gain[...]).astype(BF16)
    grad = upstream[...].reshape(block * width, chans)
    out = tokens[...].reshape(block * width, chans).astype(F32)
    grad_mlp = jnp.zeros_like(spatial)

    def first(cols):
        return dot(mlp_in, w_in[:, cols]), dot(grad, w_out_t[:, cols])

    parts = [slice(f, f + part) for f in range(0, hidden, part)]
    ahead = first(parts[0])
    for f, cols in enumerate(parts):
        preact, grad_act = ahead
        if f + 1 < len(parts):
            ahead = first(parts[f + 1])
        value, slope = gelu_and_slope(preact)
        activated = value.astype(BF16)
        grad_pre = (grad_act * slope).astype(BF16)
        out = out + dot(activated, w_out[cols, :])
        grad_mlp = grad_mlp + dot(grad_pre, w_in_t[cols, :])
        sum_out[:, cols] += dot_tn(grad, activated)
        sum_in[:, cols] += dot_tn(mlp_in, grad_pre)
    block_out[...] = out.astype(BF16).reshape(block, width, chans)
    grad_spatial = norm_backward(grad_mlp, normed, rstd, gain[...])
    sum_gain[0:8] += jnp.sum((grad_mlp * normed).reshape(-1, 8, chans), axis=0)
    sum_gain[8:16] += jnp.sum((grad_spatial * spatial).reshape(-1, 8, chans), axis=0)
    sent = grad_spatial.astype(BF16)
    for r in range(block):
        values = dot(table_in[...], sent[r * width : (r + 1) * width])
        write_row(packed, step * block + r, width, values)

    @pl.when(step == pl.num_programs(0) - 1)
    def _():
        pack(packed, width, outgoing)


def mlp(received, tokens, upstream, gain, tables, weights, previous, chunk, block):
    n = len(received)
    count, rows, chans = received[0].shape
    width = tokens.shape[1]
    hidden = weights[0].shape[1]
    steps = rows // block
    by_rows = pl.BlockSpec((block, width, chans), lambda i: (i + chunk * steps, 0, 0))
    operands = [tokens, upstream, gain, *tables, *weights, *received]
    in_specs = [
        by_rows,
        by_rows,
        resident((1, chans)),
        resident((width, width)),
        resident((width, width)),
        resident((chans, hidden)),
        resident((hidden, chans)),
        resident((hidden, chans)),
        resident((chans, hidden)),
    ] + [resident((count, rows, chans))] * n
    aliases = {}
    if previous is not None:
        aliases = {len(operands): 0}
        operands.append(previous)
        in_specs.append(ANYWHERE)
    flops = 2 * rows * width * chans * (6 * hidden + 2 * width)
    outputs = pl.pallas_call(
        functools.partial(mlp_kernel, n, len(aliases)),
        grid=(steps,),
        in_specs=in_specs,
        out_specs=[by_rows]
        + [resident((count, rows, chans))] * n
        + [resident((chans, hidden)), resident((chans, hidden)), resident((16, chans))],
        out_shape=[shape_of(tokens.shape)]
        + [shape_of((count, rows, chans))] * n
        + [shape_of((chans, hidden), F32)] * 2
        + [shape_of((16, chans), F32)],
        scratch_shapes=[
            pltpu.VMEM((chans // LANES, width * spaced(rows), LANES), F32),
            pltpu.VMEM((chans // LANES, rows * spaced(width), LANES), F32),
        ],
        input_output_aliases=aliases,
        compiler_params=params(),
        cost_estimate=cost(flops, 10 * rows * width * chans),
        name="mlp_rows",
    )(*operands)
    return outputs[0], outputs[1 : n + 1], outputs[n + 1 :]


def leave_kernel(n, tokens, upstream, gain, table_out, *rest):
    received, (grad_tokens, unpacked) = rest[:n], rest[-2:]
    step = pl.program_id(0)
    block, width, _ = tokens.shape
    rows = received[0].shape[1]

    @pl.when(step == 0)
    def _():
        unpack(received, unpacked)

    for r in range(block):
        back = dot(table_out[...], read_row(unpacked, step * block + r, width, rows))
        normed, rstd = normalize(tokens[r].astype(F32))
        grad = norm_backward(back, normed, rstd, gain[...])
        grad_tokens[r] = (upstream[r].astype(F32) + grad).astype(BF16)


def leave(received, tokens, upstream, gain, table_out, previous, chunk, block, after):
    n = len(received)
    count, rows, chans = received[0].shape
    width = tokens.shape[1]
    steps = rows // block
    by_rows = pl.BlockSpec((block, width, chans), lambda i: (i + chunk * steps, 0, 0))
    operands = [tokens, upstream, gain, table_out, *received]
    in_specs = [by_rows, by_rows, resident((1, chans)), resident((width, width))]
    in_specs += [resident((count, rows, chans))] * n
    aliases = {}
    if previous is not None:
        aliases = {len(operands): 0}
        operands.append(previous)
        in_specs.append(ANYWHERE)
    operands += after
    in_specs += [ANYWHERE] * len(after)
    return pl.pallas_call(
        functools.partial(leave_kernel, n),
        grid=(steps,),
        in_specs=in_specs,
        out_specs=by_rows,
        out_shape=shape_of(tokens.shape),
        scratch_shapes=[pltpu.VMEM((chans // LANES, width * spaced(rows), LANES), F32)],
        input_output_aliases=aliases,
        compiler_params=params(),
        cost_estimate=cost(2 * rows * width * width * chans, 8 * rows * width * chans),
        name="leave_rows",
    )(*operands)


def columns_kernel(count, back, flags, table_f, table_b, kernel, *rest):
    spectrum, rest = (rest[0], rest[1:]) if back else (None, rest)
    received, rest = rest[:count], rest[count:]
    outgoing, held = rest[:count], rest[count]
    step, last = pl.program_id(0), pl.num_programs(0) - 1
    per, _, height, chans = kernel.shape

    def load(j):
        return jnp.concatenate([ref[:, :, j].reshape(-1, chans) for ref in received], axis=0)

    def store(j, values):
        values = values.astype(BF16)
        size = values.shape[0] // len(outgoing)
        for i, ref in enumerate(outgoing):
            n, _, _, rows, _ = ref.shape
            ref[:, :, j] = values[i * size : (i + 1) * size].reshape(n, 2, rows, chans)

    def filtered(slot, found):
        found = found.astype(BF16)
        real, imag = found[:height].astype(F32), found[height:].astype(F32)
        k_real, k_imag = kernel[slot, 0].astype(F32), kernel[slot, 1].astype(F32)
        if back:
            s_real, s_imag = spectrum[slot, 0].astype(F32), spectrum[slot, 1].astype(F32)
            held[slot, 0] = (real * s_real + imag * s_imag).astype(BF16)
            held[slot, 1] = (imag * s_real - real * s_imag).astype(BF16)
            k_imag = -k_imag
        else:
            held[slot, 0] = found[:height]
            held[slot, 1] = found[height:]
        upper = (k_real * real - k_imag * imag).astype(BF16)
        lower = (k_real * imag + k_imag * real).astype(BF16)
        return jnp.concatenate([upper, lower], axis=0)

    @pl.when(step < last)
    def _():
        at = [1 + step * per + i for i in range(per)]
        found = dot(table_f[2], jnp.concatenate([load(j) for j in at], axis=1))
        weighted = [filtered(i, found[:, i * chans : (i + 1) * chans]) for i in range(per)]
        result = dot(table_b[2], jnp.concatenate(weighted, axis=1))
        for i, j in enumerate(at):
            store(j, result[:, i * chans : (i + 1) * chans])

    @pl.when(step == last)
    def _():
        values = load(0)
        kind = 2 - flags[1]
        zero = filtered(0, dot(table_f[kind], values))
        middle = filtered(1, dot(table_f[0], values))
        store(0, dot(table_b[kind], zero) + dot(table_b[0], middle))
        for i in range(2, per):
            held[i] = jnp.zeros_like(held[i])


def columns(flags, tables, kernel, received, spectrum):
    count = len(received)
    _, _, half, _, chans = received[0].shape
    slots, _, height, _ = kernel.shape
    per = columns_per_step(half)
    held = pl.BlockSpec((per, 2, height, chans), lambda t, flags: (t, 0, 0, 0))
    table = resident((3, 2 * height, 2 * height))
    back = spectrum is not None
    outputs = pl.pallas_call(
        functools.partial(columns_kernel, count, back),
        grid_spec=pltpu.PrefetchScalarGridSpec(
            num_scalar_prefetch=1,
            grid=(slots // per,),
            in_specs=[table, table, held]
            + [held] * back
            + [resident(r.shape) for r in received],
            out_specs=[resident(r.shape) for r in received] + [held],
        ),
        out_shape=[shape_of(r.shape) for r in received] + [shape_of(kernel.shape)],
        compiler_params=params(),
        cost_estimate=cost(16 * height * height * chans * slots, 20 * height * chans * slots),
        name="filter_columns",
    )(flags, *tables, kernel, *([spectrum] if back else []), *received)
    return outputs[:count], outputs[count]


def columns_per_step(half):
    return 3 if (half - 1) % 3 == 0 else 2 if (half - 1) % 2 == 0 else 1


def slot_count(half):
    per = max(2, columns_per_step(half))
    return half - 1 + per


def filter_part_kernel(copies, flags, mirror, own, *rest):
    mains, extras = rest[:copies], rest[copies : 2 * copies]
    kernel, scr_own, scr_main, scr_extra = rest[2 * copies :]
    part = pl.program_id(0)
    upper, first, me = flags[0], flags[1], flags[2]
    _, height, wide, _ = own.shape
    half = wide // 2
    share = height // copies
    pitch_own, pitch = spaced(wide), spaced(half)

    def spread_own(m, carry):
        scr_own[pl.ds(pl.multiple_of(m * pitch_own, 8), wide), :] = own[0, m].astype(F32)
        return carry

    lax.fori_loop(0, height, spread_own, 0, unroll=8)
    for i in range(copies):
        owner = jnp.bitwise_xor(me, i)

        def spread_main(m, carry):
            at = pl.multiple_of((owner * share + m) * pitch, 8)
            scr_main[pl.ds(at, half), :] = mains[i][0, m].astype(F32)
            return carry

        lax.fori_loop(0, share, spread_main, 0, unroll=8)
        at = pl.multiple_of(owner * share, share)
        scr_extra[pl.ds(at, share), :] = extras[i][0].astype(F32)
    sign = jnp.where(part == 0, 0.5, -0.5)
    extra = scr_extra[...]
    middle = 0.5 * extra + sign * dot(mirror[...], extra.astype(BF16))
    kernel[half, 0] = jnp.where(first == 1, middle, 0.0).astype(BF16)
    for i in range(half + 1, kernel.shape[0]):
        kernel[i, 0] = jnp.zeros((height, LANES), BF16)
    for j in range(half):
        mine = scr_own[pl.ds(j + upper, height, stride=pitch_own), :]
        if j == 0:
            other = scr_main[pl.ds(half - 1, height, stride=pitch), :]
            lower = jnp.where(first == 1, mine, extra)
            other = jnp.where(upper == 1, other, lower)
        else:
            other = scr_main[pl.ds(half - j - upper, height, stride=pitch), :]
        turned = dot(mirror[...], other.astype(BF16))
        kernel[(j - 1) % half, 0] = (0.5 * mine + sign * turned).astype(BF16)


def filter_part(flags, mirror, own, mains, extras):
    _, height, wide, chans = own.shape
    copies = len(mains)
    half, share = wide // 2, height // copies
    slots = slot_count(half)
    return pl.pallas_call(
        functools.partial(filter_part_kernel, copies),
        grid_spec=pltpu.PrefetchScalarGridSpec(
            num_scalar_prefetch=1,
            grid=(2, chans // LANES),
            in_specs=[
                pl.BlockSpec((height, height), lambda p, c, flags: (0, 0)),
                pl.BlockSpec((1, height, wide, LANES), lambda p, c, flags: (p, 0, 0, c)),
            ]
            + [pl.BlockSpec((1, share, half, LANES), lambda p, c, flags: (p, 0, 0, c))] * copies
            + [pl.BlockSpec((1, share, LANES), lambda p, c, flags: (p, 0, c))] * copies,
            out_specs=pl.BlockSpec((slots, 1, height, LANES), lambda p, c, flags: (0, p, 0, c)),
            scratch_shapes=[
                pltpu.VMEM((height * spaced(wide), LANES), F32),
                pltpu.VMEM((height * spaced(half), LANES), F32),
                pltpu.VMEM((height, LANES), F32),
            ],
        ),
        out_shape=shape_of((slots, 2, height, chans)),
        compiler_params=params(),
        cost_estimate=cost(4 * height * height * chans * half, 16 * height * half * chans),
        name="filter_part",
    )(flags, mirror, own, *mains, *extras)


def filter_gradient_kernel(copies, flags, mirror, *rest):
    mine, theirs = rest[:copies], rest[copies : 2 * copies]
    out, gathered, turned = rest[2 * copies :]
    part = pl.program_id(0)
    upper, me = flags[0], flags[2]
    _, height, wide, _ = out.shape
    half = wide // 2
    share = height // copies
    pitch = spaced(height)
    for i in range(copies):
        at = pl.multiple_of(jnp.bitwise_xor(me, i) * share, share)
        gathered[0:half, pl.ds(at, share), :] = mine[i][:, 0]
        gathered[half:, pl.ds(at, share), :] = theirs[i][:, 0]
    sign = jnp.where(part == 0, 1.0, -1.0)
    for k in range(wide):
        if k == 0:
            index = jnp.where(upper == 1, 2 * half, half - 1)
        elif k < half:
            index = k - 1 - upper
            index = jnp.where(index < 0, half - 1, index)
        elif k == half:
            index = jnp.where(upper == 1, half - 2, 2 * half - 2)
        else:
            index = wide - 2 - k + upper
            index = half + jnp.where(index < 0, half - 1, index)
        value = gathered[index]
        if 0 < k < half:
            value = value.astype(F32)
        else:
            other = sign * dot(mirror[...], value)
            if k == 0:
                other = jnp.where(upper == 1, other, value.astype(F32))
            elif k == half:
                other = jnp.where(upper == 1, value.astype(F32), other)
            value = other
        turned[pl.ds(k * pitch, height), :] = value

    def step(m, carry):
        out[0, m] = turned[pl.ds(m, wide, stride=pitch), :]
        return carry

    lax.fori_loop(0, height, step, 0, unroll=8)


def filter_gradient(flags, mirror, mine, theirs, height, wide):
    _, _, share, chans = mine[0].shape
    copies, half = len(mine), wide // 2
    block = lambda slots: pl.BlockSpec(
        (slots, 1, share, LANES), lambda p, c, flags: (0, p, 0, c)
    )
    return pl.pallas_call(
        functools.partial(filter_gradient_kernel, copies),
        grid_spec=pltpu.PrefetchScalarGridSpec(
            num_scalar_prefetch=1,
            grid=(2, chans // LANES),
            in_specs=[pl.BlockSpec((height, height), lambda p, c, flags: (0, 0))]
            + [block(half)] * copies
            + [block(half + 1)] * copies,
            out_specs=pl.BlockSpec((1, height, wide, LANES), lambda p, c, flags: (p, 0, 0, c)),
            scratch_shapes=[
                pltpu.VMEM((wide + 1, height, LANES), BF16),
                pltpu.VMEM((wide * spaced(height), LANES), F32),
            ],
        ),
        out_shape=shape_of((2, height, wide, chans), F32),
        compiler_params=params(),
        cost_estimate=cost(2 * height * height * chans * wide, 12 * height * wide * chans),
        name="filter_gradient",
    )(flags, mirror, *mine, *theirs)


def swap(value, axis, size, partner):
    return lax.ppermute(value, axis, [(i, partner(i)) for i in range(size)])


def swap_bits(value, axis, size, bits):
    return swap(value, axis, size, lambda i: i ^ bits)


def exchange(value):
    return lax.all_to_all(value, "space", split_axis=0, concat_axis=0, tiled=True)


def gather_copies(value, copies):
    parts = {0: value}
    bit = copies // 2
    while bit:
        for key in list(parts):
            parts[key ^ bit] = swap_bits(parts[key], "copy", copies, bit)
        bit //= 2
    return [parts[i] for i in range(copies)]


def reduce_copies(value, copies, axis):
    me = lax.axis_index("copy")
    bit = 1
    while bit < copies:
        size = value.shape[axis] // 2
        mine = (me // bit) % 2
        kept = lax.dynamic_slice_in_dim(value, mine * size, size, axis)
        sent = lax.dynamic_slice_in_dim(value, (1 - mine) * size, size, axis)
        other = swap_bits(sent, "copy", copies, bit)
        value = (kept.astype(F32) + other.astype(F32)).astype(value.dtype)
        bit *= 2
    return value


def share_order(copies):
    digits = copies.bit_length() - 1
    return [int(format(i, "b").zfill(digits)[::-1], 2) if digits else 0 for i in range(copies)]


def body(noisy_tokens, grad_out, filter_weight, weight_in, weight_out, gain_one, gain_two):
    _, rows_dev, width, chans = noisy_tokens.shape
    height, wide = filter_weight.shape[1:3]
    hidden = weight_in.shape[1]
    half = wide // 2
    n, copies = lax.axis_size("space"), lax.axis_size("copy")
    chunks = 2
    rows = rows_dev // chunks
    tokens, upstream = noisy_tokens[0], grad_out[0]
    me, copy = lax.axis_index("space"), lax.axis_index("copy")
    order = share_order(copies)

    share = height // copies
    at = copy * share
    opposite = lambda d: n - 1 - d
    main = lax.dynamic_slice(filter_weight, (0, at, half, 0), (2, share, half, chans))
    main = swap(main, "space", n, opposite)
    to_lower = [(n // 2, 0)] + [(e, n - e) for e in range(n // 2 + 1, n)]
    single = lax.dynamic_slice(filter_weight, (0, at, 0, 0), (2, share, 1, chans))
    single = lax.ppermute(single.reshape(2, share, chans), "space", to_lower)

    forward, weighted = row_tables(width, n)
    table_in = jnp.asarray(forward.reshape(width, width))
    table_out = jnp.asarray(np.ascontiguousarray(weighted.reshape(width, width).T))
    table_b = column_tables(height, n, chunks).reshape(3, 2 * height, 2 * height)
    table_f = np.ascontiguousarray(table_b.transpose(0, 2, 1))
    column_tabs = (jnp.asarray(table_f), jnp.asarray(table_b))
    mirror = jnp.asarray(mirror_table(height))
    gain_a, gain_b = gain_one.reshape(1, chans), gain_two.reshape(1, chans)
    upper = (me >= n // 2).astype(jnp.int32)
    first = (me == 0).astype(jnp.int32)

    def flags(index):
        return jnp.stack([upper, first, index.astype(jnp.int32)])

    def split(value):
        return value.reshape(n, 2, half, rows, chans)

    def join(value):
        return value.reshape(width, rows, chans)

    arrived = []
    for c in range(chunks):
        after = (main, single) if c else ()
        arrived.append(split(exchange(enter(tokens, gain_a, table_in, c, rows, 2, after))))
    mains, singles = gather_copies(main, copies), gather_copies(single, copies)
    kernel = filter_part(flags(copy), mirror, filter_weight, mains, singles)
    returned, spectrum = columns(flags(copy), column_tabs, kernel, arrived, None)

    weights = (weight_in, weight_out, weight_in.T, weight_out.T)
    tables = (table_out, table_in)
    block_out = None
    sums, arrived = [], []
    for c in range(chunks):
        received = exchange(join(returned[c]))
        block_out, sent, local = mlp(
            [received], tokens, upstream, gain_b, tables, weights, block_out, c, 4
        )
        arrived.append(split(exchange(sent[0])))
        sums.append(local)

    sum_in, sum_out, sum_gain = (a + b for a, b in zip(*sums))
    both = reduce_copies(jnp.concatenate([sum_in, sum_out], axis=0), copies, 0)
    gains = jnp.concatenate([jnp.sum(sum_gain[8:], axis=0) / gain_one, jnp.sum(sum_gain[:8], axis=0)])
    bit = 1
    while bit < copies:
        gains = gains + swap_bits(gains, "copy", copies, bit)
        bit *= 2
    gains = jnp.pad(gains[None], ((0, 7), (0, hidden - 2 * chans)))
    total_tokens = copies * rows_dev * n * width
    summed = lax.psum(jnp.concatenate([both, gains], axis=0), "space")
    summed = summed * (1.0 / math.sqrt(total_tokens))
    size = both.shape[0]
    shares = lax.all_gather(summed[:size].astype(BF16), "copy")
    grads = jnp.concatenate([shares[order.index(i)] for i in range(copies)], axis=0)
    grad_in, grad_out_t = grads[:chans], grads[chans:]

    returned, terms = columns(flags(copy), column_tabs, kernel, arrived, spectrum)
    grad_tokens = None
    for c in range(chunks):
        grad_tokens = leave(
            [exchange(join(returned[c]))],
            tokens,
            upstream,
            gain_a,
            table_out,
            grad_tokens,
            c,
            2,
            (shares,) if c else (summed,),
        )

    reduced = reduce_copies(terms[: half + 1], copies, 2)
    mirrored = swap(reduced[:half], "space", n, opposite)
    to_upper = [(0, n // 2)] + [(d, n - d) for d in range(1, n // 2)]
    single = lax.ppermute(
        jnp.where(me == 0, reduced[half], reduced[half - 1]), "space", to_upper
    )
    mine = gather_copies(reduced[:half], copies)
    theirs = gather_copies(jnp.concatenate([mirrored, single[None]], axis=0), copies)
    index = jnp.asarray(order, jnp.int32)[copy]
    grad_filter = filter_gradient(
        flags(index),
        mirror,
        [mine[order[i]] for i in range(copies)],
        [theirs[order[i]] for i in range(copies)],
        height,
        wide,
    )
    return (
        block_out[None],
        grad_tokens[None],
        grad_filter,
        grad_in,
        grad_out_t.T,
        summed[size, :chans],
        summed[size, chans : 2 * chans],
    )


def dft_parts(length):
    index = jnp.arange(length, dtype=jnp.int32)
    phase = index[:, None] * index[None, :] % length
    angle = phase.astype(jnp.float32) * (2.0 * math.pi / length)
    factor = 1.0 / math.sqrt(length)
    return (
        (jnp.cos(angle) * factor).astype(jnp.bfloat16),
        (jnp.sin(angle) * factor).astype(jnp.bfloat16),
    )


def row_table(length):
    cosine, sine = dft_parts(length)
    return jnp.stack([cosine, -sine])


def column_table(length, direction):
    cosine, sine = dft_parts(length)
    upper = jnp.stack([cosine, direction * sine], axis=1)
    lower = jnp.stack([-direction * sine, cosine], axis=1)
    return jnp.stack([upper, lower])


def plain_layer_norm(values):
    centre = jnp.mean(values, axis=-1, keepdims=True)
    centred = values - centre
    variance = jnp.mean(centred * centred, axis=-1, keepdims=True)
    rstd_value = lax.rsqrt(variance + EPS)
    return (centred * rstd_value, rstd_value)


def plain_norm_backward(upstream, normed, rstd_value, gain):
    scaled = upstream * gain
    result = (
        scaled
        - jnp.mean(scaled, axis=-1, keepdims=True)
        - normed * jnp.mean(scaled * normed, axis=-1, keepdims=True)
    ) * rstd_value
    lead = tuple(range(upstream.ndim - 1))
    return (result, jnp.sum(upstream * normed, axis=lead))


def apply_filter(spectrum, filter_weight, direction):
    real_part = spectrum[0].astype(jnp.float32)
    imag_part = spectrum[1].astype(jnp.float32)
    kernel_real = filter_weight[0].astype(jnp.float32)
    kernel_imag = direction * filter_weight[1].astype(jnp.float32)
    return jnp.stack(
        [
            kernel_real * real_part - kernel_imag * imag_part,
            kernel_real * imag_part + kernel_imag * real_part,
        ]
    )


def exact_gelu(values):
    return jax.nn.gelu(values, approximate=False)


def spectral(values, filter_weight, direction):
    width = values.shape[2]
    rows_tab = row_table(width)
    rows = jnp.einsum(
        "pkw,bhwc->pbhkc", rows_tab, values, preferred_element_type=jnp.float32
    ).astype(jnp.bfloat16)
    columns = lax.all_to_all(rows, "space", split_axis=3, concat_axis=2, tiled=True)
    height = columns.shape[2]
    spectrum = jnp.einsum(
        "qmph,pbhkc->qbmkc", column_table(height, 1), columns, preferred_element_type=jnp.float32
    ).astype(jnp.bfloat16)
    weighted = apply_filter(spectrum, filter_weight[:, None], direction).astype(jnp.bfloat16)
    returned = jnp.einsum(
        "qmph,pbhkc->qbmkc", column_table(height, -1), weighted, preferred_element_type=jnp.float32
    ).astype(jnp.bfloat16)
    back_rows = lax.all_to_all(returned, "space", split_axis=2, concat_axis=3, tiled=True)
    output = jnp.einsum("pkw,pbhkc->bhwc", rows_tab, back_rows, preferred_element_type=jnp.float32)
    return (output, spectrum)


def plain_body(noisy_tokens, grad_out, filter_weight, weight_in, weight_out, gain_one, gain_two):
    batch, rows_dev, width, chans = noisy_tokens.shape
    inputs = noisy_tokens.astype(jnp.float32)
    normed_one, rstd_one = plain_layer_norm(inputs)
    mixed_in = (normed_one * gain_one).astype(jnp.bfloat16)
    spatial, spectrum = spectral(mixed_in, filter_weight, 1)
    normed_two, rstd_two = plain_layer_norm(spatial)
    mlp_in = (normed_two * gain_two).astype(jnp.bfloat16).reshape(-1, chans)
    preact = jnp.dot(mlp_in, weight_in, preferred_element_type=jnp.float32)
    activated = exact_gelu(preact).astype(jnp.bfloat16)
    mlp_out = jnp.dot(activated, weight_out, preferred_element_type=jnp.float32)
    block_out = (inputs + mlp_out.reshape(inputs.shape)).astype(jnp.bfloat16)
    upstream = grad_out.reshape(-1, chans)
    grad_act = jnp.dot(upstream, weight_out.T, preferred_element_type=jnp.float32)
    grad_pre = jax.vjp(exact_gelu, preact)[1](grad_act)[0].astype(jnp.bfloat16)
    sum_out = jnp.dot(activated.T, upstream, preferred_element_type=jnp.float32)
    sum_in = jnp.dot(mlp_in.T, grad_pre, preferred_element_type=jnp.float32)
    grad_mlp = jnp.dot(grad_pre, weight_in.T, preferred_element_type=jnp.float32).reshape(
        inputs.shape
    )
    grad_spatial, sum_gain_two = plain_norm_backward(grad_mlp, normed_two, rstd_two, gain_two)
    back_spatial, adjoint = spectral(grad_spatial.astype(jnp.bfloat16), filter_weight, -1)
    spec_f = spectrum.astype(jnp.float32)
    adj_f = adjoint.astype(jnp.float32)
    filter_terms = jnp.stack(
        [
            jnp.sum(adj_f[0] * spec_f[0] + adj_f[1] * spec_f[1], axis=0),
            jnp.sum(adj_f[1] * spec_f[0] - adj_f[0] * spec_f[1], axis=0),
        ]
    )
    grad_filter = lax.psum(filter_terms.astype(jnp.bfloat16), "copy").astype(jnp.float32)
    grad_normed, sum_gain_one = plain_norm_backward(back_spatial, normed_one, rstd_one, gain_one)
    grad_tokens = (grad_out.astype(jnp.float32) + grad_normed).astype(jnp.bfloat16)
    local_sums = (sum_in, sum_out, sum_gain_one, sum_gain_two)
    summed = lax.psum(
        (local_sums[0], local_sums[1], local_sums[2], local_sums[3]), ("copy", "space")
    )
    total_tokens = batch * lax.axis_size("copy") * rows_dev * lax.axis_size("space") * width
    factor = 1.0 / math.sqrt(total_tokens)
    return (
        block_out,
        grad_tokens,
        grad_filter,
        (summed[0] * factor).astype(jnp.bfloat16),
        (summed[1] * factor).astype(jnp.bfloat16),
        summed[2] * factor,
        summed[3] * factor,
    )


def solution(mesh):
    def program(*arrays):
        rows_dev, wide = arrays[0].shape[1], arrays[2].shape[2]
        tiled = rows_dev % 32 == 0 and wide % 32 == 0
        return (body if tiled else plain_body)(*arrays)

    return jax.shard_map(
        program,
        mesh=mesh,
        in_specs=(
            P("copy", "space", None, None),
            P("copy", "space", None, None),
            P(None, None, "space", None),
            P(),
            P(),
            P(),
            P(),
        ),
        out_specs=(
            P("copy", "space", None, None),
            P("copy", "space", None, None),
            P(None, None, "space", None),
            P(),
            P(),
            P(),
            P(),
        ),
        check_vma=False,
    )
```

```python
import functools
import math

import jax
import jax.numpy as jnp
import ml_dtypes
import numpy as np
from jax import lax
from jax.experimental import pallas as pl
from jax.experimental.pallas import tpu as pltpu
from jax.sharding import PartitionSpec as P

EPS = 1e-06
LANES = 128
VMEM_LIMIT = 60 * 1024 * 1024
BF16 = jnp.bfloat16
F32 = jnp.float32


def dft_pair(length):
    index = np.arange(length, dtype=np.int64)
    angle = (index[:, None] * index[None, :] % length) * (2.0 * math.pi / length)
    factor = 1.0 / math.sqrt(length)
    rounded = lambda a: a.astype(np.float32).astype(ml_dtypes.bfloat16).astype(np.float32)
    return rounded(np.cos(angle) * factor), rounded(np.sin(angle) * factor)


def row_tables(width, n):
    cosine, sine = dft_pair(width)
    own = width // n
    half = own // 2
    forward = np.zeros((n, 2, half, width), np.float32)
    weight = np.full((n, 2, half, 1), 2.0, np.float32)
    for d in range(n):
        first = own * d + (1 if d >= n // 2 else 0)
        forward[d, 0] = cosine[first : first + half]
        forward[d, 1] = -sine[first : first + half]
    forward[0, 1, 0] = cosine[width // 2]
    weight[0, :, 0] = 1.0
    shape = (n, 2 * half, width)
    return (
        forward.reshape(shape).astype(ml_dtypes.bfloat16),
        (forward * weight).reshape(shape).astype(ml_dtypes.bfloat16),
    )


def column_tables(height, n, chunks):
    cosine, sine = dft_pair(height)
    zero = np.zeros_like(cosine)
    rows = height // n // chunks

    def arrange(blocks):
        full = np.stack([np.stack(line, axis=1) for line in blocks])
        full = full.reshape(2 * height, 2, n, chunks, rows)
        return full.transpose(0, 3, 2, 1, 4).reshape(2 * height, 2 * height)

    middle = arrange([[zero, cosine], [zero, -sine]])
    first = arrange([[cosine, zero], [-sine, zero]])
    other = arrange([[cosine, sine], [-sine, cosine]])
    backward = np.stack([middle, first, other]).transpose(0, 2, 1)
    backward = backward.reshape(3, chunks, n, 2 * rows, 2 * height)
    return backward.astype(ml_dtypes.bfloat16)


def mirror_table(height):
    table = np.zeros((height, height), np.float32)
    table[np.arange(height), (-np.arange(height)) % height] = 1.0
    return table.astype(ml_dtypes.bfloat16)


def dot(a, b):
    return jnp.dot(a, b, preferred_element_type=F32)


def dot_tn(a, b):
    return lax.dot_general(a, b, (((0,), (0,)), ((), ())), preferred_element_type=F32)


def normalize(values):
    centred = values - jnp.mean(values, axis=-1, keepdims=True)
    variance = jnp.mean(centred * centred, axis=-1, keepdims=True)
    rstd = lax.rsqrt(variance + EPS)
    return centred * rstd, rstd


def norm_backward(upstream, normed, rstd, gain):
    scaled = upstream * gain
    return (
        scaled
        - jnp.mean(scaled, axis=-1, keepdims=True)
        - normed * jnp.mean(scaled * normed, axis=-1, keepdims=True)
    ) * rstd


def gelu_and_slope(v):
    e = jnp.exp(v * v * -0.5)
    d = 1.0 + (0.3275911 / math.sqrt(2.0)) * jnp.abs(v)
    t = pl.reciprocal(d, approx=True)
    t = t * (2.0 - d * t)
    poly = 0.5 * 1.061405429
    for coefficient in (-1.453152027, 1.421413741, -0.284496736, 0.254829592):
        poly = poly * t + 0.5 * coefficient
    tail = poly * t * e
    phi = jnp.where(v < 0.0, tail, 1.0 - tail)
    return v * phi, phi + v * e * (1.0 / math.sqrt(2.0 * math.pi))


def spaced(count):
    groups = -(-count // 8)
    return 8 * (groups + 1 - groups % 2)


def lanes(c):
    return slice(c * LANES, (c + 1) * LANES)


def unpack(received, scratch):
    count, rows, chans = received[0].shape
    pitch = spaced(rows)

    def step(k, carry):
        for s, ref in enumerate(received):
            start = pl.multiple_of((s * count + k) * pitch, 8)
            for c in range(chans // LANES):
                scratch[c, pl.ds(start, rows), :] = ref[k, :, lanes(c)].astype(F32)
        return carry

    lax.fori_loop(0, count, step, 0, unroll=2)


def read_row(scratch, row, columns, rows):
    parts = [
        scratch[c, pl.ds(row, columns, stride=spaced(rows)), :].astype(BF16)
        for c in range(scratch.shape[0])
    ]
    return jnp.concatenate(parts, axis=1)


def write_row(scratch, row, columns, values):
    start = pl.multiple_of(row * spaced(columns), 8)
    for c in range(scratch.shape[0]):
        scratch[c, pl.ds(start, columns), :] = values[:, lanes(c)]


def pack(scratch, columns, outgoing):
    count, rows, _ = outgoing[0].shape

    def step(k, carry):
        for s, ref in enumerate(outgoing):
            for c in range(scratch.shape[0]):
                part = scratch[c, pl.ds(s * count + k, rows, stride=spaced(columns)), :]
                ref[k, :, lanes(c)] = part.astype(BF16)
        return carry

    lax.fori_loop(0, count, step, 0, unroll=2)


def params():
    return pltpu.CompilerParams(vmem_limit_bytes=VMEM_LIMIT)


def resident(shape):
    return pl.BlockSpec(shape, lambda *_: (0,) * len(shape), pipeline_mode=pl.Buffered(1))


ANYWHERE = pl.BlockSpec(memory_space=pl.ANY)


def cost(flops, size):
    return pl.CostEstimate(flops=int(flops), bytes_accessed=int(size), transcendentals=0)


def shape_of(shape, dtype=BF16):
    return jax.ShapeDtypeStruct(tuple(shape), dtype)


def hold(value, after):
    return pl.pallas_call(
        lambda *refs: None,
        in_specs=[ANYWHERE] * (1 + len(after)),
        out_specs=ANYWHERE,
        out_shape=shape_of(value.shape, value.dtype),
        input_output_aliases={0: 0},
        compiler_params=params(),
        cost_estimate=cost(0, 0),
        name="hold",
    )(value, *after)


def enter_kernel(tokens, gain, table, *rest):
    outgoing, scratch = rest[-2:-1], rest[-1]
    step = pl.program_id(0)
    block, width, _ = tokens.shape
    for r in range(block):
        normed, _ = normalize(tokens[r].astype(F32))
        mixed = (normed * gain[...]).astype(BF16)
        write_row(scratch, step * block + r, width, dot(table[...], mixed))

    @pl.when(step == pl.num_programs(0) - 1)
    def _():
        pack(scratch, width, outgoing)


def enter(tokens, gain, table, block):
    rows, width, chans = tokens.shape
    steps = rows // block
    out = (width, rows, chans)
    return pl.pallas_call(
        enter_kernel,
        grid=(steps,),
        in_specs=[
            pl.BlockSpec((block, width, chans), lambda i: (i, 0, 0)),
            resident((1, chans)),
            resident((width, width)),
        ],
        out_specs=resident(out),
        out_shape=shape_of(out),
        scratch_shapes=[pltpu.VMEM((chans // LANES, rows * spaced(width), LANES), F32)],
        compiler_params=params(),
        cost_estimate=cost(2 * rows * width * width * chans, 4 * rows * width * chans),
        name="enter_rows",
    )(tokens, gain, table)


def mlp_kernel(
    n, extra, tokens, upstream, gain, table_out, table_in, w_in, w_out, w_in_t, w_out_t, *rest
):
    received, rest = rest[:n], rest[n + extra :]
    block_out, outgoing, rest = rest[0], rest[1 : n + 1], rest[n + 1 :]
    sum_in, sum_out, sum_gain, unpacked, packed = rest
    step = pl.program_id(0)
    block, width, chans = tokens.shape
    rows = received[0].shape[1]
    hidden = w_in.shape[1]
    part = min(512, hidden)

    @pl.when(step == 0)
    def _():
        unpack(received, unpacked)
        sum_in[...] = jnp.zeros_like(sum_in)
        sum_out[...] = jnp.zeros_like(sum_out)
        sum_gain[...] = jnp.zeros_like(sum_gain)

    spatial = jnp.concatenate(
        [
            dot(table_out[...], read_row(unpacked, step * block + r, width, rows))
            for r in range(block)
        ],
        axis=0,
    )
    normed, rstd = normalize(spatial)
    mlp_in = (normed * gain[...]).astype(BF16)
    grad = upstream[...].reshape(block * width, chans)
    out = tokens[...].reshape(block * width, chans).astype(F32)
    grad_mlp = jnp.zeros_like(spatial)

    def first(cols):
        return dot(mlp_in, w_in[:, cols]), dot(grad, w_out_t[:, cols])

    parts = [slice(f, f + part) for f in range(0, hidden, part)]
    ahead = first(parts[0])
    for f, cols in enumerate(parts):
        preact, grad_act = ahead
        if f + 1 < len(parts):
            ahead = first(parts[f + 1])
        value, slope = gelu_and_slope(preact)
        activated = value.astype(BF16)
        grad_pre = (grad_act * slope).astype(BF16)
        out = out + dot(activated, w_out[cols, :])
        grad_mlp = grad_mlp + dot(grad_pre, w_in_t[cols, :])
        sum_out[:, cols] += dot_tn(grad, activated)
        sum_in[:, cols] += dot_tn(mlp_in, grad_pre)
    block_out[...] = out.astype(BF16).reshape(block, width, chans)
    grad_spatial = norm_backward(grad_mlp, normed, rstd, gain[...])
    sum_gain[0:8] += jnp.sum((grad_mlp * normed).reshape(-1, 8, chans), axis=0)
    sum_gain[8:16] += jnp.sum((grad_spatial * spatial).reshape(-1, 8, chans), axis=0)
    sent = grad_spatial.astype(BF16)
    for r in range(block):
        values = dot(table_in[...], sent[r * width : (r + 1) * width])
        write_row(packed, step * block + r, width, values)

    @pl.when(step == pl.num_programs(0) - 1)
    def _():
        pack(packed, width, outgoing)


def mlp(received, tokens, upstream, gain, tables, weights, previous, chunk, block):
    n = len(received)
    count, rows, chans = received[0].shape
    width = tokens.shape[1]
    hidden = weights[0].shape[1]
    steps = rows // block
    by_rows = pl.BlockSpec((block, width, chans), lambda i: (i + chunk * steps, 0, 0))
    operands = [tokens, upstream, gain, *tables, *weights, *received]
    in_specs = [
        by_rows,
        by_rows,
        resident((1, chans)),
        resident((width, width)),
        resident((width, width)),
        resident((chans, hidden)),
        resident((hidden, chans)),
        resident((hidden, chans)),
        resident((chans, hidden)),
    ] + [resident((count, rows, chans))] * n
    aliases = {}
    if previous is not None:
        aliases = {len(operands): 0}
        operands.append(previous)
        in_specs.append(ANYWHERE)
    flops = 2 * rows * width * chans * (6 * hidden + 2 * width)
    outputs = pl.pallas_call(
        functools.partial(mlp_kernel, n, len(aliases)),
        grid=(steps,),
        in_specs=in_specs,
        out_specs=[by_rows]
        + [resident((count, rows, chans))] * n
        + [resident((chans, hidden)), resident((chans, hidden)), resident((16, chans))],
        out_shape=[shape_of(tokens.shape)]
        + [shape_of((count, rows, chans))] * n
        + [shape_of((chans, hidden), F32)] * 2
        + [shape_of((16, chans), F32)],
        scratch_shapes=[
            pltpu.VMEM((chans // LANES, width * spaced(rows), LANES), F32),
            pltpu.VMEM((chans // LANES, rows * spaced(width), LANES), F32),
        ],
        input_output_aliases=aliases,
        compiler_params=params(),
        cost_estimate=cost(flops, 10 * rows * width * chans),
        name="mlp_rows",
    )(*operands)
    return outputs[0], outputs[1 : n + 1], outputs[n + 1 :]


def leave_kernel(n, tokens, upstream, gain, table_out, *rest):
    received, (grad_tokens, unpacked) = rest[:n], rest[-2:]
    step = pl.program_id(0)
    block, width, _ = tokens.shape
    rows = received[0].shape[1]

    @pl.when(step == 0)
    def _():
        unpack(received, unpacked)

    for r in range(block):
        back = dot(table_out[...], read_row(unpacked, step * block + r, width, rows))
        normed, rstd = normalize(tokens[r].astype(F32))
        grad = norm_backward(back, normed, rstd, gain[...])
        grad_tokens[r] = (upstream[r].astype(F32) + grad).astype(BF16)


def leave(received, tokens, upstream, gain, table_out, previous, chunk, block, after):
    n = len(received)
    count, rows, chans = received[0].shape
    width = tokens.shape[1]
    steps = rows // block
    by_rows = pl.BlockSpec((block, width, chans), lambda i: (i + chunk * steps, 0, 0))
    operands = [tokens, upstream, gain, table_out, *received]
    in_specs = [by_rows, by_rows, resident((1, chans)), resident((width, width))]
    in_specs += [resident((count, rows, chans))] * n
    aliases = {}
    if previous is not None:
        aliases = {len(operands): 0}
        operands.append(previous)
        in_specs.append(ANYWHERE)
    operands += after
    in_specs += [ANYWHERE] * len(after)
    return pl.pallas_call(
        functools.partial(leave_kernel, n),
        grid=(steps,),
        in_specs=in_specs,
        out_specs=by_rows,
        out_shape=shape_of(tokens.shape),
        scratch_shapes=[pltpu.VMEM((chans // LANES, width * spaced(rows), LANES), F32)],
        input_output_aliases=aliases,
        compiler_params=params(),
        cost_estimate=cost(2 * rows * width * width * chans, 8 * rows * width * chans),
        name="leave_rows",
    )(*operands)


def columns_kernel(count, outs, back, flags, table_f, table_b, kernel, *rest):
    spectrum, rest = (rest[0], rest[1:]) if back else (None, rest)
    received, (*outgoing, held) = rest[:count], rest[-outs - 1 :]
    step, last = pl.program_id(0), pl.num_programs(0) - 1
    per, _, height, chans = kernel.shape

    def load(j):
        return jnp.concatenate([ref[:, :, j].reshape(-1, chans) for ref in received], axis=0)

    def store(j, values):
        values = values.astype(BF16)
        size = values.shape[0] // len(outgoing)
        for i, ref in enumerate(outgoing):
            n, _, _, rows, _ = ref.shape
            ref[:, :, j] = values[i * size : (i + 1) * size].reshape(n, 2, rows, chans)

    def filtered(slot, found):
        found = found.astype(BF16)
        real, imag = found[:height].astype(F32), found[height:].astype(F32)
        k_real, k_imag = kernel[slot, 0].astype(F32), kernel[slot, 1].astype(F32)
        if back:
            s_real, s_imag = spectrum[slot, 0].astype(F32), spectrum[slot, 1].astype(F32)
            held[slot, 0] = (real * s_real + imag * s_imag).astype(BF16)
            held[slot, 1] = (imag * s_real - real * s_imag).astype(BF16)
            k_imag = -k_imag
        else:
            held[slot, 0] = found[:height]
            held[slot, 1] = found[height:]
        upper = (k_real * real - k_imag * imag).astype(BF16)
        lower = (k_real * imag + k_imag * real).astype(BF16)
        return jnp.concatenate([upper, lower], axis=0)

    @pl.when(step < last)
    def _():
        at = [1 + step * per + i for i in range(per)]
        found = dot(table_f[2], jnp.concatenate([load(j) for j in at], axis=1))
        weighted = [filtered(i, found[:, i * chans : (i + 1) * chans]) for i in range(per)]
        result = dot(table_b[2], jnp.concatenate(weighted, axis=1))
        for i, j in enumerate(at):
            store(j, result[:, i * chans : (i + 1) * chans])

    @pl.when(step == last)
    def _():
        values = load(0)
        kind = 2 - flags[1]
        zero = filtered(0, dot(table_f[kind], values))
        middle = filtered(1, dot(table_f[0], values))
        store(0, dot(table_b[kind], zero) + dot(table_b[0], middle))
        for i in range(2, per):
            held[i] = jnp.zeros_like(held[i])


def columns(flags, tables, kernel, received, outs, spectrum=None, after=()):
    count = len(received)
    n, _, half, rows, chans = received[0].shape
    sent = (n, 2, half, count * rows // outs, chans)
    slots, _, height, _ = kernel.shape
    per = columns_per_step(half)
    held = pl.BlockSpec((per, 2, height, chans), lambda t, flags: (t, 0, 0, 0))
    table = resident((3, 2 * height, 2 * height))
    back = spectrum is not None
    outputs = pl.pallas_call(
        functools.partial(columns_kernel, count, outs, back),
        grid_spec=pltpu.PrefetchScalarGridSpec(
            num_scalar_prefetch=1,
            grid=(slots // per,),
            in_specs=[table, table, held]
            + [held] * back
            + [resident(r.shape) for r in received]
            + [ANYWHERE] * len(after),
            out_specs=[resident(sent)] * outs + [held],
        ),
        out_shape=[shape_of(sent)] * outs + [shape_of(kernel.shape)],
        compiler_params=params(),
        cost_estimate=cost(16 * height * height * chans * slots, 20 * height * chans * slots),
        name="filter_columns",
    )(flags, *tables, kernel, *([spectrum] if back else []), *received, *after)
    return outputs[:outs], outputs[outs]


def columns_per_step(half):
    return 3 if (half - 1) % 3 == 0 else 2 if (half - 1) % 2 == 0 else 1


def slot_count(half):
    per = max(2, columns_per_step(half))
    return half - 1 + per


def filter_part_kernel(copies, flags, mirror, own, *rest):
    mains, extras = rest[:copies], rest[copies : 2 * copies]
    kernel, scr_own, scr_main, scr_extra = rest[2 * copies :]
    part = pl.program_id(0)
    upper, first, me = flags[0], flags[1], flags[2]
    _, height, wide, _ = own.shape
    half = wide // 2
    share = height // copies
    pitch_own, pitch = spaced(wide), spaced(half)

    def spread_own(m, carry):
        scr_own[pl.ds(pl.multiple_of(m * pitch_own, 8), wide), :] = own[0, m].astype(F32)
        return carry

    lax.fori_loop(0, height, spread_own, 0, unroll=8)
    for i in range(copies):
        owner = jnp.bitwise_xor(me, i)

        def spread_main(m, carry):
            at = pl.multiple_of((owner * share + m) * pitch, 8)
            scr_main[pl.ds(at, half), :] = mains[i][0, m].astype(F32)
            return carry

        lax.fori_loop(0, share, spread_main, 0, unroll=8)
        at = pl.multiple_of(owner * share, share)
        scr_extra[pl.ds(at, share), :] = extras[i][0].astype(F32)
    sign = jnp.where(part == 0, 0.5, -0.5)
    extra = scr_extra[...]
    middle = 0.5 * extra + sign * dot(mirror[...], extra.astype(BF16))
    kernel[half, 0] = jnp.where(first == 1, middle, 0.0).astype(BF16)
    for i in range(half + 1, kernel.shape[0]):
        kernel[i, 0] = jnp.zeros((height, LANES), BF16)
    for j in range(half):
        mine = scr_own[pl.ds(j + upper, height, stride=pitch_own), :]
        if j == 0:
            other = scr_main[pl.ds(half - 1, height, stride=pitch), :]
            lower = jnp.where(first == 1, mine, extra)
            other = jnp.where(upper == 1, other, lower)
        else:
            other = scr_main[pl.ds(half - j - upper, height, stride=pitch), :]
        turned = dot(mirror[...], other.astype(BF16))
        kernel[(j - 1) % half, 0] = (0.5 * mine + sign * turned).astype(BF16)


def filter_part(flags, mirror, own, mains, extras):
    _, height, wide, chans = own.shape
    copies = len(mains)
    half, share = wide // 2, height // copies
    slots = slot_count(half)
    return pl.pallas_call(
        functools.partial(filter_part_kernel, copies),
        grid_spec=pltpu.PrefetchScalarGridSpec(
            num_scalar_prefetch=1,
            grid=(2, chans // LANES),
            in_specs=[
                pl.BlockSpec((height, height), lambda p, c, flags: (0, 0)),
                pl.BlockSpec((1, height, wide, LANES), lambda p, c, flags: (p, 0, 0, c)),
            ]
            + [pl.BlockSpec((1, share, half, LANES), lambda p, c, flags: (p, 0, 0, c))] * copies
            + [pl.BlockSpec((1, share, LANES), lambda p, c, flags: (p, 0, c))] * copies,
            out_specs=pl.BlockSpec((slots, 1, height, LANES), lambda p, c, flags: (0, p, 0, c)),
            scratch_shapes=[
                pltpu.VMEM((height * spaced(wide), LANES), F32),
                pltpu.VMEM((height * spaced(half), LANES), F32),
                pltpu.VMEM((height, LANES), F32),
            ],
        ),
        out_shape=shape_of((slots, 2, height, chans)),
        compiler_params=params(),
        cost_estimate=cost(4 * height * height * chans * half, 16 * height * half * chans),
        name="filter_part",
    )(flags, mirror, own, *mains, *extras)


def filter_gradient_kernel(copies, flags, mirror, *rest):
    mine, theirs = rest[:copies], rest[copies : 2 * copies]
    out, gathered, turned = rest[-3:]
    part = pl.program_id(0)
    upper, me = flags[0], flags[2]
    _, height, wide, _ = out.shape
    half = wide // 2
    share = height // copies
    pitch = spaced(height)
    for i in range(copies):
        at = pl.multiple_of(jnp.bitwise_xor(me, i) * share, share)
        gathered[0:half, pl.ds(at, share), :] = mine[i][:, 0]
        gathered[half:, pl.ds(at, share), :] = theirs[i][:, 0]
    sign = jnp.where(part == 0, 1.0, -1.0)
    for k in range(wide):
        if k == 0:
            index = jnp.where(upper == 1, 2 * half, half - 1)
        elif k < half:
            index = k - 1 - upper
            index = jnp.where(index < 0, half - 1, index)
        elif k == half:
            index = jnp.where(upper == 1, half - 2, 2 * half - 2)
        else:
            index = wide - 2 - k + upper
            index = half + jnp.where(index < 0, half - 1, index)
        value = gathered[index]
        if 0 < k < half:
            value = value.astype(F32)
        else:
            other = sign * dot(mirror[...], value)
            if k == 0:
                other = jnp.where(upper == 1, other, value.astype(F32))
            elif k == half:
                other = jnp.where(upper == 1, value.astype(F32), other)
            value = other
        turned[pl.ds(k * pitch, height), :] = value

    def step(m, carry):
        out[0, m] = turned[pl.ds(m, wide, stride=pitch), :]
        return carry

    lax.fori_loop(0, height, step, 0, unroll=8)


def filter_gradient(flags, mirror, mine, theirs, height, wide, after):
    _, _, share, chans = mine[0].shape
    copies, half = len(mine), wide // 2
    block = lambda slots: pl.BlockSpec(
        (slots, 1, share, LANES), lambda p, c, flags: (0, p, 0, c)
    )
    return pl.pallas_call(
        functools.partial(filter_gradient_kernel, copies),
        grid_spec=pltpu.PrefetchScalarGridSpec(
            num_scalar_prefetch=1,
            grid=(2, chans // LANES),
            in_specs=[pl.BlockSpec((height, height), lambda p, c, flags: (0, 0))]
            + [block(half)] * copies
            + [block(half + 1)] * copies
            + [ANYWHERE] * len(after),
            out_specs=pl.BlockSpec((1, height, wide, LANES), lambda p, c, flags: (p, 0, 0, c)),
            scratch_shapes=[
                pltpu.VMEM((wide + 1, height, LANES), BF16),
                pltpu.VMEM((wide * spaced(height), LANES), F32),
            ],
        ),
        out_shape=shape_of((2, height, wide, chans), F32),
        compiler_params=params(),
        cost_estimate=cost(2 * height * height * chans * wide, 12 * height * wide * chans),
        name="filter_gradient",
    )(flags, mirror, *mine, *theirs, *after)


def swap(value, axis, size, partner):
    return lax.ppermute(value, axis, [(i, partner(i)) for i in range(size)])


def swap_bits(value, axis, size, bits):
    return swap(value, axis, size, lambda i: i ^ bits)


def exchange(value):
    return lax.all_to_all(value, "space", split_axis=0, concat_axis=0, tiled=True)


def gather_copies(value, copies):
    parts = {0: value}
    bit = copies // 2
    while bit:
        for key in list(parts):
            parts[key ^ bit] = swap_bits(parts[key], "copy", copies, bit)
        bit //= 2
    return [parts[i] for i in range(copies)]


def reduce_copies(value, copies, axis):
    me = lax.axis_index("copy")
    bit = 1
    while bit < copies:
        size = value.shape[axis] // 2
        mine = (me // bit) % 2
        kept = lax.dynamic_slice_in_dim(value, mine * size, size, axis)
        sent = lax.dynamic_slice_in_dim(value, (1 - mine) * size, size, axis)
        other = swap_bits(sent, "copy", copies, bit)
        value = (kept.astype(F32) + other.astype(F32)).astype(value.dtype)
        bit *= 2
    return value


def share_order(copies):
    digits = copies.bit_length() - 1
    return [int(format(i, "b").zfill(digits)[::-1], 2) if digits else 0 for i in range(copies)]


def body(noisy_tokens, grad_out, filter_weight, weight_in, weight_out, gain_one, gain_two):
    _, rows_dev, width, chans = noisy_tokens.shape
    height, wide = filter_weight.shape[1:3]
    hidden = weight_in.shape[1]
    half = wide // 2
    n, copies = lax.axis_size("space"), lax.axis_size("copy")
    chunks = 2
    rows = rows_dev // chunks
    tokens, upstream = noisy_tokens[0], grad_out[0]
    me, copy = lax.axis_index("space"), lax.axis_index("copy")
    order = share_order(copies)

    share = height // copies
    at = copy * share
    opposite = lambda d: n - 1 - d
    main = lax.dynamic_slice(filter_weight, (0, at, half, 0), (2, share, half, chans))
    main = swap(main, "space", n, opposite)
    to_lower = [(n // 2, 0)] + [(e, n - e) for e in range(n // 2 + 1, n)]
    single = lax.dynamic_slice(filter_weight, (0, at, 0, 0), (2, share, 1, chans))
    single = lax.ppermute(single.reshape(2, share, chans), "space", to_lower)

    forward, weighted = row_tables(width, n)
    table_in = jnp.asarray(forward.reshape(width, width))
    table_out = jnp.asarray(np.ascontiguousarray(weighted.reshape(width, width).T))
    whole, cut = (
        column_tables(height, n, c).reshape(3, 2 * height, 2 * height) for c in (1, chunks)
    )
    forward_in, backward_in = (
        jnp.asarray(np.ascontiguousarray(t.transpose(0, 2, 1))) for t in (whole, cut)
    )
    out_tabs = jnp.asarray(cut)
    mirror = jnp.asarray(mirror_table(height))
    gain_a, gain_b = gain_one.reshape(1, chans), gain_two.reshape(1, chans)
    upper = (me >= n // 2).astype(jnp.int32)
    first = (me == 0).astype(jnp.int32)

    def flags(index):
        return jnp.stack([upper, first, index.astype(jnp.int32)])

    def split(value):
        return value.reshape(n, 2, half, -1, chans)

    def join(value):
        return value.reshape(width, -1, chans)

    entered = hold(enter(tokens, gain_a, table_in, 2), (main, single))
    arrived = [split(exchange(entered))]
    mains, singles = gather_copies(main, copies), gather_copies(single, copies)
    kernel = filter_part(flags(copy), mirror, filter_weight, mains, singles)
    returned, spectrum = columns(flags(copy), (forward_in, out_tabs), kernel, arrived, chunks)

    weights = (weight_in, weight_out, weight_in.T, weight_out.T)
    tables = (table_out, table_in)
    block_out = None
    sums, arrived = [], []
    for c in range(chunks):
        received = exchange(join(returned[c]))
        block_out, sent, local = mlp(
            [received], tokens, upstream, gain_b, tables, weights, block_out, c, 4
        )
        arrived.append(split(exchange(sent[0])))
        sums.append(local)

    sum_in, sum_out, sum_gain = (a + b for a, b in zip(*sums))
    both = reduce_copies(jnp.concatenate([sum_in, sum_out], axis=0), copies, 0)
    gains = jnp.concatenate([jnp.sum(sum_gain[8:], axis=0) / gain_one, jnp.sum(sum_gain[:8], axis=0)])
    bit = 1
    while bit < copies:
        gains = gains + swap_bits(gains, "copy", copies, bit)
        bit *= 2
    gains = jnp.pad(gains[None], ((0, 7), (0, hidden - 2 * chans)))
    total_tokens = copies * rows_dev * n * width
    local = jnp.concatenate([both, gains], axis=0)
    summed = lax.psum(local, "space")
    summed = summed * (1.0 / math.sqrt(total_tokens))
    size = both.shape[0]
    shares = lax.all_gather(summed[:size].astype(BF16), "copy")
    grads = jnp.concatenate([shares[order.index(i)] for i in range(copies)], axis=0)
    grad_in, grad_out_t = grads[:chans], grads[chans:]

    returned, terms = columns(
        flags(copy), (backward_in, out_tabs), kernel, arrived, chunks, spectrum, (local,)
    )
    sent = [exchange(join(r)) for r in returned]
    grad_tokens = leave([sent[0]], tokens, upstream, gain_a, table_out, None, 0, 2, ())

    reduced = reduce_copies(terms[: half + 1], copies, 2)
    mirrored = swap(reduced[:half], "space", n, opposite)
    to_upper = [(0, n // 2)] + [(d, n - d) for d in range(1, n // 2)]
    single = lax.ppermute(
        jnp.where(me == 0, reduced[half], reduced[half - 1]), "space", to_upper
    )
    mine = gather_copies(reduced[:half], copies)
    theirs = jnp.concatenate([mirrored, single[None]], axis=0)
    theirs = gather_copies(hold(theirs, (grad_tokens,)), copies)
    grad_tokens = leave(
        [sent[1]], tokens, upstream, gain_a, table_out, grad_tokens, 1, 2, (summed,)
    )
    index = jnp.asarray(order, jnp.int32)[copy]
    grad_filter = filter_gradient(
        flags(index),
        mirror,
        [mine[order[i]] for i in range(copies)],
        [theirs[order[i]] for i in range(copies)],
        height,
        wide,
        (shares, grad_tokens),
    )
    return (
        block_out[None],
        grad_tokens[None],
        grad_filter,
        grad_in,
        grad_out_t.T,
        summed[size, :chans],
        summed[size, chans : 2 * chans],
    )


def dft_parts(length):
    index = jnp.arange(length, dtype=jnp.int32)
    phase = index[:, None] * index[None, :] % length
    angle = phase.astype(jnp.float32) * (2.0 * math.pi / length)
    factor = 1.0 / math.sqrt(length)
    return (
        (jnp.cos(angle) * factor).astype(jnp.bfloat16),
        (jnp.sin(angle) * factor).astype(jnp.bfloat16),
    )


def row_table(length):
    cosine, sine = dft_parts(length)
    return jnp.stack([cosine, -sine])


def column_table(length, direction):
    cosine, sine = dft_parts(length)
    upper = jnp.stack([cosine, direction * sine], axis=1)
    lower = jnp.stack([-direction * sine, cosine], axis=1)
    return jnp.stack([upper, lower])


def plain_layer_norm(values):
    centre = jnp.mean(values, axis=-1, keepdims=True)
    centred = values - centre
    variance = jnp.mean(centred * centred, axis=-1, keepdims=True)
    rstd_value = lax.rsqrt(variance + EPS)
    return (centred * rstd_value, rstd_value)


def plain_norm_backward(upstream, normed, rstd_value, gain):
    scaled = upstream * gain
    result = (
        scaled
        - jnp.mean(scaled, axis=-1, keepdims=True)
        - normed * jnp.mean(scaled * normed, axis=-1, keepdims=True)
    ) * rstd_value
    lead = tuple(range(upstream.ndim - 1))
    return (result, jnp.sum(upstream * normed, axis=lead))


def apply_filter(spectrum, filter_weight, direction):
    real_part = spectrum[0].astype(jnp.float32)
    imag_part = spectrum[1].astype(jnp.float32)
    kernel_real = filter_weight[0].astype(jnp.float32)
    kernel_imag = direction * filter_weight[1].astype(jnp.float32)
    return jnp.stack(
        [
            kernel_real * real_part - kernel_imag * imag_part,
            kernel_real * imag_part + kernel_imag * real_part,
        ]
    )


def exact_gelu(values):
    return jax.nn.gelu(values, approximate=False)


def spectral(values, filter_weight, direction):
    width = values.shape[2]
    rows_tab = row_table(width)
    rows = jnp.einsum(
        "pkw,bhwc->pbhkc", rows_tab, values, preferred_element_type=jnp.float32
    ).astype(jnp.bfloat16)
    columns = lax.all_to_all(rows, "space", split_axis=3, concat_axis=2, tiled=True)
    height = columns.shape[2]
    spectrum = jnp.einsum(
        "qmph,pbhkc->qbmkc", column_table(height, 1), columns, preferred_element_type=jnp.float32
    ).astype(jnp.bfloat16)
    weighted = apply_filter(spectrum, filter_weight[:, None], direction).astype(jnp.bfloat16)
    returned = jnp.einsum(
        "qmph,pbhkc->qbmkc", column_table(height, -1), weighted, preferred_element_type=jnp.float32
    ).astype(jnp.bfloat16)
    back_rows = lax.all_to_all(returned, "space", split_axis=2, concat_axis=3, tiled=True)
    output = jnp.einsum("pkw,pbhkc->bhwc", rows_tab, back_rows, preferred_element_type=jnp.float32)
    return (output, spectrum)


def plain_body(noisy_tokens, grad_out, filter_weight, weight_in, weight_out, gain_one, gain_two):
    batch, rows_dev, width, chans = noisy_tokens.shape
    inputs = noisy_tokens.astype(jnp.float32)
    normed_one, rstd_one = plain_layer_norm(inputs)
    mixed_in = (normed_one * gain_one).astype(jnp.bfloat16)
    spatial, spectrum = spectral(mixed_in, filter_weight, 1)
    normed_two, rstd_two = plain_layer_norm(spatial)
    mlp_in = (normed_two * gain_two).astype(jnp.bfloat16).reshape(-1, chans)
    preact = jnp.dot(mlp_in, weight_in, preferred_element_type=jnp.float32)
    activated = exact_gelu(preact).astype(jnp.bfloat16)
    mlp_out = jnp.dot(activated, weight_out, preferred_element_type=jnp.float32)
    block_out = (inputs + mlp_out.reshape(inputs.shape)).astype(jnp.bfloat16)
    upstream = grad_out.reshape(-1, chans)
    grad_act = jnp.dot(upstream, weight_out.T, preferred_element_type=jnp.float32)
    grad_pre = jax.vjp(exact_gelu, preact)[1](grad_act)[0].astype(jnp.bfloat16)
    sum_out = jnp.dot(activated.T, upstream, preferred_element_type=jnp.float32)
    sum_in = jnp.dot(mlp_in.T, grad_pre, preferred_element_type=jnp.float32)
    grad_mlp = jnp.dot(grad_pre, weight_in.T, preferred_element_type=jnp.float32).reshape(
        inputs.shape
    )
    grad_spatial, sum_gain_two = plain_norm_backward(grad_mlp, normed_two, rstd_two, gain_two)
    back_spatial, adjoint = spectral(grad_spatial.astype(jnp.bfloat16), filter_weight, -1)
    spec_f = spectrum.astype(jnp.float32)
    adj_f = adjoint.astype(jnp.float32)
    filter_terms = jnp.stack(
        [
            jnp.sum(adj_f[0] * spec_f[0] + adj_f[1] * spec_f[1], axis=0),
            jnp.sum(adj_f[1] * spec_f[0] - adj_f[0] * spec_f[1], axis=0),
        ]
    )
    grad_filter = lax.psum(filter_terms.astype(jnp.bfloat16), "copy").astype(jnp.float32)
    grad_normed, sum_gain_one = plain_norm_backward(back_spatial, normed_one, rstd_one, gain_one)
    grad_tokens = (grad_out.astype(jnp.float32) + grad_normed).astype(jnp.bfloat16)
    local_sums = (sum_in, sum_out, sum_gain_one, sum_gain_two)
    summed = lax.psum(
        (local_sums[0], local_sums[1], local_sums[2], local_sums[3]), ("copy", "space")
    )
    total_tokens = batch * lax.axis_size("copy") * rows_dev * lax.axis_size("space") * width
    factor = 1.0 / math.sqrt(total_tokens)
    return (
        block_out,
        grad_tokens,
        grad_filter,
        (summed[0] * factor).astype(jnp.bfloat16),
        (summed[1] * factor).astype(jnp.bfloat16),
        summed[2] * factor,
        summed[3] * factor,
    )


def solution(mesh):
    def program(*arrays):
        rows_dev, wide = arrays[0].shape[1], arrays[2].shape[2]
        tiled = rows_dev % 32 == 0 and wide % 32 == 0
        return (body if tiled else plain_body)(*arrays)

    return jax.shard_map(
        program,
        mesh=mesh,
        in_specs=(
            P("copy", "space", None, None),
            P("copy", "space", None, None),
            P(None, None, "space", None),
            P(),
            P(),
            P(),
            P(),
        ),
        out_specs=(
            P("copy", "space", None, None),
            P("copy", "space", None, None),
            P(None, None, "space", None),
            P(),
            P(),
            P(),
            P(),
        ),
        check_vma=False,
    )
```

```python
import functools
import math

import jax
import jax.numpy as jnp
import ml_dtypes
import numpy as np
from jax import lax
from jax.experimental import pallas as pl
from jax.experimental.pallas import tpu as pltpu
from jax.sharding import PartitionSpec as P

EPS = 1e-06
LANES = 128
VMEM_LIMIT = 60 * 1024 * 1024
BF16 = jnp.bfloat16
F32 = jnp.float32


def dft_pair(length):
    index = np.arange(length, dtype=np.int64)
    angle = (index[:, None] * index[None, :] % length) * (2.0 * math.pi / length)
    factor = 1.0 / math.sqrt(length)
    rounded = lambda a: a.astype(np.float32).astype(ml_dtypes.bfloat16).astype(np.float32)
    return rounded(np.cos(angle) * factor), rounded(np.sin(angle) * factor)


def row_tables(width, n):
    cosine, sine = dft_pair(width)
    own = width // n
    half = own // 2
    forward = np.zeros((n, 2, half, width), np.float32)
    weight = np.full((n, 2, half, 1), 2.0, np.float32)
    for d in range(n):
        first = own * d + (1 if d >= n // 2 else 0)
        forward[d, 0] = cosine[first : first + half]
        forward[d, 1] = -sine[first : first + half]
    forward[0, 1, 0] = cosine[width // 2]
    weight[0, :, 0] = 1.0
    shape = (n, 2 * half, width)
    return (
        forward.reshape(shape).astype(ml_dtypes.bfloat16),
        (forward * weight).reshape(shape).astype(ml_dtypes.bfloat16),
    )


def column_tables(height, n, chunks):
    cosine, sine = dft_pair(height)
    zero = np.zeros_like(cosine)
    rows = height // n // chunks

    def arrange(blocks):
        full = np.stack([np.stack(line, axis=1) for line in blocks])
        full = full.reshape(2 * height, 2, n, chunks, rows)
        return full.transpose(0, 3, 2, 1, 4).reshape(2 * height, 2 * height)

    middle = arrange([[zero, cosine], [zero, -sine]])
    first = arrange([[cosine, zero], [-sine, zero]])
    other = arrange([[cosine, sine], [-sine, cosine]])
    backward = np.stack([middle, first, other]).transpose(0, 2, 1)
    backward = backward.reshape(3, chunks, n, 2 * rows, 2 * height)
    return backward.astype(ml_dtypes.bfloat16)


def mirror_table(height):
    table = np.zeros((height, height), np.float32)
    table[np.arange(height), (-np.arange(height)) % height] = 1.0
    return table.astype(ml_dtypes.bfloat16)


def dot(a, b):
    return jnp.dot(a, b, preferred_element_type=F32)


def dot_tn(a, b):
    return lax.dot_general(a, b, (((0,), (0,)), ((), ())), preferred_element_type=F32)


def normalize(values):
    centred = values - jnp.mean(values, axis=-1, keepdims=True)
    variance = jnp.mean(centred * centred, axis=-1, keepdims=True)
    rstd = lax.rsqrt(variance + EPS)
    return centred * rstd, rstd


def norm_backward(upstream, normed, rstd, gain):
    scaled = upstream * gain
    return (
        scaled
        - jnp.mean(scaled, axis=-1, keepdims=True)
        - normed * jnp.mean(scaled * normed, axis=-1, keepdims=True)
    ) * rstd


def gelu_and_slope(v):
    e = jnp.exp(v * v * -0.5)
    d = 1.0 + (0.3275911 / math.sqrt(2.0)) * jnp.abs(v)
    t = pl.reciprocal(d, approx=True)
    t = t * (2.0 - d * t)
    poly = 0.5 * 1.061405429
    for coefficient in (-1.453152027, 1.421413741, -0.284496736, 0.254829592):
        poly = poly * t + 0.5 * coefficient
    tail = poly * t * e
    phi = jnp.where(v < 0.0, tail, 1.0 - tail)
    return v * phi, phi + v * e * (1.0 / math.sqrt(2.0 * math.pi))


def spaced(count):
    groups = -(-count // 8)
    return 8 * (groups + 1 - groups % 2)


def lanes(c):
    return slice(c * LANES, (c + 1) * LANES)


def unpack(received, scratch):
    count, rows, chans = received[0].shape
    pitch = spaced(rows)

    def step(k, carry):
        for s, ref in enumerate(received):
            start = pl.multiple_of((s * count + k) * pitch, 8)
            for c in range(chans // LANES):
                scratch[c, pl.ds(start, rows), :] = ref[k, :, lanes(c)].astype(F32)
        return carry

    lax.fori_loop(0, count, step, 0, unroll=2)


def read_row(scratch, row, columns, rows):
    parts = [
        scratch[c, pl.ds(row, columns, stride=spaced(rows)), :].astype(BF16)
        for c in range(scratch.shape[0])
    ]
    return jnp.concatenate(parts, axis=1)


def write_row(scratch, row, columns, values):
    start = pl.multiple_of(row * spaced(columns), 8)
    for c in range(scratch.shape[0]):
        scratch[c, pl.ds(start, columns), :] = values[:, lanes(c)]


def pack(scratch, columns, outgoing):
    count, rows, _ = outgoing[0].shape

    def step(k, carry):
        for s, ref in enumerate(outgoing):
            for c in range(scratch.shape[0]):
                part = scratch[c, pl.ds(s * count + k, rows, stride=spaced(columns)), :]
                ref[k, :, lanes(c)] = part.astype(BF16)
        return carry

    lax.fori_loop(0, count, step, 0, unroll=2)


def params():
    return pltpu.CompilerParams(vmem_limit_bytes=VMEM_LIMIT)


def resident(shape):
    return pl.BlockSpec(shape, lambda *_: (0,) * len(shape), pipeline_mode=pl.Buffered(1))


ANYWHERE = pl.BlockSpec(memory_space=pl.ANY)


def cost(flops, size):
    return pl.CostEstimate(flops=int(flops), bytes_accessed=int(size), transcendentals=0)


def shape_of(shape, dtype=BF16):
    return jax.ShapeDtypeStruct(tuple(shape), dtype)


def hold(value, after):
    return pl.pallas_call(
        lambda *refs: None,
        in_specs=[ANYWHERE] * (1 + len(after)),
        out_specs=ANYWHERE,
        out_shape=shape_of(value.shape, value.dtype),
        input_output_aliases={0: 0},
        compiler_params=params(),
        cost_estimate=cost(0, 0),
        name="hold",
    )(value, *after)


def enter_kernel(tokens, gain, table, *rest):
    outgoing, scratch = rest[-2:-1], rest[-1]
    step = pl.program_id(0)
    block, width, _ = tokens.shape
    for r in range(block):
        normed, _ = normalize(tokens[r].astype(F32))
        mixed = (normed * gain[...]).astype(BF16)
        write_row(scratch, step * block + r, width, dot(table[...], mixed))

    @pl.when(step == pl.num_programs(0) - 1)
    def _():
        pack(scratch, width, outgoing)


def enter(tokens, gain, table, block):
    rows, width, chans = tokens.shape
    steps = rows // block
    out = (width, rows, chans)
    return pl.pallas_call(
        enter_kernel,
        grid=(steps,),
        in_specs=[
            pl.BlockSpec((block, width, chans), lambda i: (i, 0, 0)),
            resident((1, chans)),
            resident((width, width)),
        ],
        out_specs=resident(out),
        out_shape=shape_of(out),
        scratch_shapes=[pltpu.VMEM((chans // LANES, rows * spaced(width), LANES), F32)],
        compiler_params=params(),
        cost_estimate=cost(2 * rows * width * width * chans, 4 * rows * width * chans),
        name="enter_rows",
    )(tokens, gain, table)


def mlp_kernel(
    n, later, tokens, upstream, gain, table_out, table_in, w_in, w_out, w_in_t, w_out_t, *rest
):
    received, rest = rest[:n], rest[n:]
    if later:
        (_, *before), rest = rest[:4], rest[4:]
    block_out, outgoing, rest = rest[0], rest[1 : n + 1], rest[n + 1 :]
    sum_in, sum_out, sum_gain, unpacked, packed = rest
    step = pl.program_id(0)
    block, width, chans = tokens.shape
    rows = received[0].shape[1]
    hidden = w_in.shape[1]
    part = min(512, hidden)

    @pl.when(step == 0)
    def _():
        unpack(received, unpacked)
        for i, ref in enumerate((sum_in, sum_out, sum_gain)):
            ref[...] = before[i][...] if later else jnp.zeros_like(ref)

    spatial = jnp.concatenate(
        [
            dot(table_out[...], read_row(unpacked, step * block + r, width, rows))
            for r in range(block)
        ],
        axis=0,
    )
    normed, rstd = normalize(spatial)
    mlp_in = (normed * gain[...]).astype(BF16)
    grad = upstream[...].reshape(block * width, chans)
    out = tokens[...].reshape(block * width, chans).astype(F32)
    grad_mlp = jnp.zeros_like(spatial)

    def first(cols):
        return dot(mlp_in, w_in[:, cols]), dot(grad, w_out_t[:, cols])

    parts = [slice(f, f + part) for f in range(0, hidden, part)]
    ahead = first(parts[0])
    for f, cols in enumerate(parts):
        preact, grad_act = ahead
        if f + 1 < len(parts):
            ahead = first(parts[f + 1])
        value, slope = gelu_and_slope(preact)
        activated = value.astype(BF16)
        grad_pre = (grad_act * slope).astype(BF16)
        out = out + dot(activated, w_out[cols, :])
        grad_mlp = grad_mlp + dot(grad_pre, w_in_t[cols, :])
        sum_out[:, cols] += dot_tn(grad, activated)
        sum_in[:, cols] += dot_tn(mlp_in, grad_pre)
    block_out[...] = out.astype(BF16).reshape(block, width, chans)
    grad_spatial = norm_backward(grad_mlp, normed, rstd, gain[...])
    sum_gain[0:8] += jnp.sum((grad_mlp * normed).reshape(-1, 8, chans), axis=0)
    sum_gain[8:16] += jnp.sum((grad_spatial * spatial).reshape(-1, 8, chans), axis=0)
    sent = grad_spatial.astype(BF16)
    for r in range(block):
        values = dot(table_in[...], sent[r * width : (r + 1) * width])
        write_row(packed, step * block + r, width, values)

    @pl.when(step == pl.num_programs(0) - 1)
    def _():
        pack(packed, width, outgoing)


def mlp(received, tokens, upstream, gain, tables, weights, previous, chunk, block):
    n = len(received)
    count, rows, chans = received[0].shape
    width = tokens.shape[1]
    hidden = weights[0].shape[1]
    steps = rows // block
    by_rows = pl.BlockSpec((block, width, chans), lambda i: (i + chunk * steps, 0, 0))
    operands = [tokens, upstream, gain, *tables, *weights, *received]
    in_specs = [
        by_rows,
        by_rows,
        resident((1, chans)),
        resident((width, width)),
        resident((width, width)),
        resident((chans, hidden)),
        resident((hidden, chans)),
        resident((hidden, chans)),
        resident((chans, hidden)),
    ] + [resident((count, rows, chans))] * n
    aliases = {}
    if previous is not None:
        aliases = {len(operands): 0}
        operands += previous
        in_specs += [ANYWHERE] + [resident(p.shape) for p in previous[1:]]
    flops = 2 * rows * width * chans * (6 * hidden + 2 * width)
    outputs = pl.pallas_call(
        functools.partial(mlp_kernel, n, previous is not None),
        grid=(steps,),
        in_specs=in_specs,
        out_specs=[by_rows]
        + [resident((count, rows, chans))] * n
        + [resident((chans, hidden)), resident((chans, hidden)), resident((16, chans))],
        out_shape=[shape_of(tokens.shape)]
        + [shape_of((count, rows, chans))] * n
        + [shape_of((chans, hidden), F32)] * 2
        + [shape_of((16, chans), F32)],
        scratch_shapes=[
            pltpu.VMEM((chans // LANES, width * spaced(rows), LANES), F32),
            pltpu.VMEM((chans // LANES, rows * spaced(width), LANES), F32),
        ],
        input_output_aliases=aliases,
        compiler_params=params(),
        cost_estimate=cost(flops, 10 * rows * width * chans),
        name="mlp_rows",
    )(*operands)
    return outputs[0], outputs[1 : n + 1], outputs[n + 1 :]


def leave_kernel(n, tokens, upstream, gain, table_out, *rest):
    received, (grad_tokens, unpacked) = rest[:n], rest[-2:]
    step = pl.program_id(0)
    block, width, _ = tokens.shape
    rows = received[0].shape[1]

    @pl.when(step == 0)
    def _():
        unpack(received, unpacked)

    for r in range(block):
        back = dot(table_out[...], read_row(unpacked, step * block + r, width, rows))
        normed, rstd = normalize(tokens[r].astype(F32))
        grad = norm_backward(back, normed, rstd, gain[...])
        grad_tokens[r] = (upstream[r].astype(F32) + grad).astype(BF16)


def leave(received, tokens, upstream, gain, table_out, previous, chunk, block, after):
    n = len(received)
    count, rows, chans = received[0].shape
    width = tokens.shape[1]
    steps = rows // block
    by_rows = pl.BlockSpec((block, width, chans), lambda i: (i + chunk * steps, 0, 0))
    operands = [tokens, upstream, gain, table_out, *received]
    in_specs = [by_rows, by_rows, resident((1, chans)), resident((width, width))]
    in_specs += [resident((count, rows, chans))] * n
    aliases = {}
    if previous is not None:
        aliases = {len(operands): 0}
        operands.append(previous)
        in_specs.append(ANYWHERE)
    operands += after
    in_specs += [ANYWHERE] * len(after)
    return pl.pallas_call(
        functools.partial(leave_kernel, n),
        grid=(steps,),
        in_specs=in_specs,
        out_specs=by_rows,
        out_shape=shape_of(tokens.shape),
        scratch_shapes=[pltpu.VMEM((chans // LANES, width * spaced(rows), LANES), F32)],
        input_output_aliases=aliases,
        compiler_params=params(),
        cost_estimate=cost(2 * rows * width * width * chans, 8 * rows * width * chans),
        name="leave_rows",
    )(*operands)


def columns_kernel(count, outs, back, flags, table_f, table_b, kernel, *rest):
    spectrum, rest = (rest[0], rest[1:]) if back else (None, rest)
    received, (*outgoing, held) = rest[:count], rest[-outs - 1 :]
    step, last = pl.program_id(0), pl.num_programs(0) - 1
    per, _, height, chans = kernel.shape

    def load(j):
        return jnp.concatenate([ref[:, :, j].reshape(-1, chans) for ref in received], axis=0)

    def store(j, values):
        values = values.astype(BF16)
        size = values.shape[0] // len(outgoing)
        for i, ref in enumerate(outgoing):
            n, _, _, rows, _ = ref.shape
            ref[:, :, j] = values[i * size : (i + 1) * size].reshape(n, 2, rows, chans)

    def filtered(slot, found):
        found = found.astype(BF16)
        real, imag = found[:height].astype(F32), found[height:].astype(F32)
        k_real, k_imag = kernel[slot, 0].astype(F32), kernel[slot, 1].astype(F32)
        if back:
            s_real, s_imag = spectrum[slot, 0].astype(F32), spectrum[slot, 1].astype(F32)
            held[slot, 0] = (real * s_real + imag * s_imag).astype(BF16)
            held[slot, 1] = (imag * s_real - real * s_imag).astype(BF16)
            k_imag = -k_imag
        else:
            held[slot, 0] = found[:height]
            held[slot, 1] = found[height:]
        upper = (k_real * real - k_imag * imag).astype(BF16)
        lower = (k_real * imag + k_imag * real).astype(BF16)
        return jnp.concatenate([upper, lower], axis=0)

    @pl.when(step < last)
    def _():
        at = [1 + step * per + i for i in range(per)]
        found = dot(table_f[2], jnp.concatenate([load(j) for j in at], axis=1))
        weighted = [filtered(i, found[:, i * chans : (i + 1) * chans]) for i in range(per)]
        result = dot(table_b[2], jnp.concatenate(weighted, axis=1))
        for i, j in enumerate(at):
            store(j, result[:, i * chans : (i + 1) * chans])

    @pl.when(step == last)
    def _():
        values = load(0)
        kind = 2 - flags[1]
        zero = filtered(0, dot(table_f[kind], values))
        middle = filtered(1, dot(table_f[0], values))
        store(0, dot(table_b[kind], zero) + dot(table_b[0], middle))
        for i in range(2, per):
            held[i] = jnp.zeros_like(held[i])


def columns(flags, tables, kernel, received, outs, spectrum=None, after=()):
    count = len(received)
    n, _, half, rows, chans = received[0].shape
    sent = (n, 2, half, count * rows // outs, chans)
    slots, _, height, _ = kernel.shape
    per = columns_per_step(half)
    held = pl.BlockSpec((per, 2, height, chans), lambda t, flags: (t, 0, 0, 0))
    table = resident((3, 2 * height, 2 * height))
    back = spectrum is not None
    outputs = pl.pallas_call(
        functools.partial(columns_kernel, count, outs, back),
        grid_spec=pltpu.PrefetchScalarGridSpec(
            num_scalar_prefetch=1,
            grid=(slots // per,),
            in_specs=[table, table, held]
            + [held] * back
            + [resident(r.shape) for r in received]
            + [ANYWHERE] * len(after),
            out_specs=[resident(sent)] * outs + [held],
        ),
        out_shape=[shape_of(sent)] * outs + [shape_of(kernel.shape)],
        compiler_params=params(),
        cost_estimate=cost(16 * height * height * chans * slots, 20 * height * chans * slots),
        name="filter_columns",
    )(flags, *tables, kernel, *([spectrum] if back else []), *received, *after)
    return outputs[:outs], outputs[outs]


def columns_per_step(half):
    return 3 if (half - 1) % 3 == 0 else 2 if (half - 1) % 2 == 0 else 1


def slot_count(half):
    per = max(2, columns_per_step(half))
    return half - 1 + per


def filter_part_kernel(copies, flags, mirror, own, *rest):
    mains, extras = rest[:copies], rest[copies : 2 * copies]
    kernel, scr_own, scr_main, scr_extra = rest[-4:]
    part = pl.program_id(0)
    upper, first, me = flags[0], flags[1], flags[2]
    _, height, wide, _ = own.shape
    half = wide // 2
    share = height // copies
    pitch_own, pitch = spaced(wide), spaced(half)

    def spread_own(m, carry):
        scr_own[pl.ds(pl.multiple_of(m * pitch_own, 8), wide), :] = own[0, m].astype(F32)
        return carry

    lax.fori_loop(0, height, spread_own, 0, unroll=8)
    for i in range(copies):
        owner = jnp.bitwise_xor(me, i)

        def spread_main(m, carry):
            at = pl.multiple_of((owner * share + m) * pitch, 8)
            scr_main[pl.ds(at, half), :] = mains[i][0, m].astype(F32)
            return carry

        lax.fori_loop(0, share, spread_main, 0, unroll=8)
        at = pl.multiple_of(owner * share, share)
        scr_extra[pl.ds(at, share), :] = extras[i][0].astype(F32)
    sign = jnp.where(part == 0, 0.5, -0.5)
    extra = scr_extra[...]
    middle = 0.5 * extra + sign * dot(mirror[...], extra.astype(BF16))
    kernel[half, 0] = jnp.where(first == 1, middle, 0.0).astype(BF16)
    for i in range(half + 1, kernel.shape[0]):
        kernel[i, 0] = jnp.zeros((height, LANES), BF16)
    for j in range(half):
        mine = scr_own[pl.ds(j + upper, height, stride=pitch_own), :]
        if j == 0:
            other = scr_main[pl.ds(half - 1, height, stride=pitch), :]
            lower = jnp.where(first == 1, mine, extra)
            other = jnp.where(upper == 1, other, lower)
        else:
            other = scr_main[pl.ds(half - j - upper, height, stride=pitch), :]
        turned = dot(mirror[...], other.astype(BF16))
        kernel[(j - 1) % half, 0] = (0.5 * mine + sign * turned).astype(BF16)


def filter_part(flags, mirror, own, mains, extras, after):
    _, height, wide, chans = own.shape
    copies = len(mains)
    half, share = wide // 2, height // copies
    slots = slot_count(half)
    return pl.pallas_call(
        functools.partial(filter_part_kernel, copies),
        grid_spec=pltpu.PrefetchScalarGridSpec(
            num_scalar_prefetch=1,
            grid=(2, chans // LANES),
            in_specs=[
                pl.BlockSpec((height, height), lambda p, c, flags: (0, 0)),
                pl.BlockSpec((1, height, wide, LANES), lambda p, c, flags: (p, 0, 0, c)),
            ]
            + [pl.BlockSpec((1, share, half, LANES), lambda p, c, flags: (p, 0, 0, c))] * copies
            + [pl.BlockSpec((1, share, LANES), lambda p, c, flags: (p, 0, c))] * copies
            + [ANYWHERE] * len(after),
            out_specs=pl.BlockSpec((slots, 1, height, LANES), lambda p, c, flags: (0, p, 0, c)),
            scratch_shapes=[
                pltpu.VMEM((height * spaced(wide), LANES), F32),
                pltpu.VMEM((height * spaced(half), LANES), F32),
                pltpu.VMEM((height, LANES), F32),
            ],
        ),
        out_shape=shape_of((slots, 2, height, chans)),
        compiler_params=params(),
        cost_estimate=cost(4 * height * height * chans * half, 16 * height * half * chans),
        name="filter_part",
    )(flags, mirror, own, *mains, *extras, *after)


def filter_gradient_kernel(copies, flags, mirror, *rest):
    mine, theirs = rest[:copies], rest[copies : 2 * copies]
    out, gathered, turned = rest[-3:]
    part = pl.program_id(0)
    upper, me = flags[0], flags[2]
    _, height, wide, _ = out.shape
    half = wide // 2
    share = height // copies
    pitch = spaced(height)
    for i in range(copies):
        at = pl.multiple_of(jnp.bitwise_xor(me, i) * share, share)
        gathered[0:half, pl.ds(at, share), :] = mine[i][:, 0]
        gathered[half:, pl.ds(at, share), :] = theirs[i][:, 0]
    sign = jnp.where(part == 0, 1.0, -1.0)
    for k in range(wide):
        if k == 0:
            index = jnp.where(upper == 1, 2 * half, half - 1)
        elif k < half:
            index = k - 1 - upper
            index = jnp.where(index < 0, half - 1, index)
        elif k == half:
            index = jnp.where(upper == 1, half - 2, 2 * half - 2)
        else:
            index = wide - 2 - k + upper
            index = half + jnp.where(index < 0, half - 1, index)
        value = gathered[index]
        if 0 < k < half:
            value = value.astype(F32)
        else:
            other = sign * dot(mirror[...], value)
            if k == 0:
                other = jnp.where(upper == 1, other, value.astype(F32))
            elif k == half:
                other = jnp.where(upper == 1, value.astype(F32), other)
            value = other
        turned[pl.ds(k * pitch, height), :] = value

    def step(m, carry):
        out[0, m] = turned[pl.ds(m, wide, stride=pitch), :]
        return carry

    lax.fori_loop(0, height, step, 0, unroll=8)


def filter_gradient(flags, mirror, mine, theirs, height, wide, after):
    _, _, share, chans = mine[0].shape
    copies, half = len(mine), wide // 2
    block = lambda slots: pl.BlockSpec(
        (slots, 1, share, LANES), lambda p, c, flags: (0, p, 0, c)
    )
    return pl.pallas_call(
        functools.partial(filter_gradient_kernel, copies),
        grid_spec=pltpu.PrefetchScalarGridSpec(
            num_scalar_prefetch=1,
            grid=(2, chans // LANES),
            in_specs=[pl.BlockSpec((height, height), lambda p, c, flags: (0, 0))]
            + [block(half)] * copies
            + [block(half + 1)] * copies
            + [ANYWHERE] * len(after),
            out_specs=pl.BlockSpec((1, height, wide, LANES), lambda p, c, flags: (p, 0, 0, c)),
            scratch_shapes=[
                pltpu.VMEM((wide + 1, height, LANES), BF16),
                pltpu.VMEM((wide * spaced(height), LANES), F32),
            ],
        ),
        out_shape=shape_of((2, height, wide, chans), F32),
        compiler_params=params(),
        cost_estimate=cost(2 * height * height * chans * wide, 12 * height * wide * chans),
        name="filter_gradient",
    )(flags, mirror, *mine, *theirs, *after)


def swap(value, axis, size, partner):
    return lax.ppermute(value, axis, [(i, partner(i)) for i in range(size)])


def swap_bits(value, axis, size, bits):
    return swap(value, axis, size, lambda i: i ^ bits)


def exchange(value):
    return lax.all_to_all(value, "space", split_axis=0, concat_axis=0, tiled=True)


def gather_copies(value, copies):
    parts = {0: value}
    bit = copies // 2
    while bit:
        for key in list(parts):
            parts[key ^ bit] = swap_bits(parts[key], "copy", copies, bit)
        bit //= 2
    return [parts[i] for i in range(copies)]


def reduce_shares(value, axes, extra=None):
    places, place = [], 0
    for name in axes:
        digits = lax.axis_size(name).bit_length() - 1
        places += [(name, bit, place + digits - 1 - bit) for bit in range(digits)]
        place += digits
    for name, bit, place in places:
        size, own = lax.axis_size(name), (lax.axis_index(name) >> bit) & 1
        kept = lax.dynamic_index_in_dim(value, own, place, keepdims=True)
        sent = lax.dynamic_index_in_dim(value, 1 - own, place, keepdims=True)
        other = swap_bits(sent, name, size, 1 << bit)
        value = (kept.astype(F32) + other.astype(F32)).astype(value.dtype)
        if extra is not None:
            extra = extra + swap_bits(extra, name, size, 1 << bit)
    return value, extra


def body(noisy_tokens, grad_out, filter_weight, weight_in, weight_out, gain_one, gain_two):
    _, rows_dev, width, chans = noisy_tokens.shape
    height, wide = filter_weight.shape[1:3]
    digits = (2,) * (lax.axis_size("copy").bit_length() - 1)
    hidden = weight_in.shape[1]
    half = wide // 2
    n, copies = lax.axis_size("space"), lax.axis_size("copy")
    chunks = 2
    rows = rows_dev // chunks
    tokens, upstream = noisy_tokens[0], grad_out[0]
    me, copy = lax.axis_index("space"), lax.axis_index("copy")

    share = height // copies
    at = copy * share
    opposite = lambda d: n - 1 - d
    main = lax.dynamic_slice(filter_weight, (0, at, half, 0), (2, share, half, chans))
    main = swap(main, "space", n, opposite)
    to_lower = [(n // 2, 0)] + [(e, n - e) for e in range(n // 2 + 1, n)]
    single = lax.dynamic_slice(filter_weight, (0, at, 0, 0), (2, share, 1, chans))
    single = lax.ppermute(single.reshape(2, share, chans), "space", to_lower)

    forward, weighted = row_tables(width, n)
    table_in = jnp.asarray(forward.reshape(width, width))
    table_out = jnp.asarray(np.ascontiguousarray(weighted.reshape(width, width).T))
    whole, cut = (
        column_tables(height, n, c).reshape(3, 2 * height, 2 * height) for c in (1, chunks)
    )
    forward_in, backward_in = (
        jnp.asarray(np.ascontiguousarray(t.transpose(0, 2, 1))) for t in (whole, cut)
    )
    out_tabs = jnp.asarray(cut)
    mirror = jnp.asarray(mirror_table(height))
    gain_a, gain_b = gain_one.reshape(1, chans), gain_two.reshape(1, chans)
    upper = (me >= n // 2).astype(jnp.int32)
    first = (me == 0).astype(jnp.int32)

    def flags(index):
        return jnp.stack([upper, first, index.astype(jnp.int32)])

    def split(value):
        return value.reshape(n, 2, half, -1, chans)

    def join(value):
        return value.reshape(width, -1, chans)

    entered = hold(enter(tokens, gain_a, table_in, 2), (main, single))
    arrived = [split(exchange(entered))]
    mains, singles = gather_copies(main, copies), gather_copies(single, copies)
    weights = (weight_in, weight_out, weight_in.T, weight_out.T)
    kernel = filter_part(flags(copy), mirror, filter_weight, mains, singles, weights[2:])
    returned, spectrum = columns(flags(copy), (forward_in, out_tabs), kernel, arrived, chunks)

    tables = (table_out, table_in)
    arrived = []
    previous = None
    for c in range(chunks):
        received = exchange(join(returned[c]))
        block_out, sent, sums = mlp(
            [received], tokens, upstream, gain_b, tables, weights, previous, c, 4
        )
        arrived.append(split(exchange(sent[0])))
        previous = [block_out, *sums]

    axes = ("copy", "space")
    sum_in, sum_out, sum_gain = sums
    both = jnp.concatenate([sum_in, sum_out], axis=0).astype(BF16)
    both = both.reshape((2,) * ((copies * n).bit_length() - 1) + (-1, hidden))
    gains = jnp.stack([jnp.sum(sum_gain[8:], axis=0) / gain_one, jnp.sum(sum_gain[:8], axis=0)])
    part, gains = reduce_shares(both, axes, gains)
    factor = 1.0 / math.sqrt(copies * rows_dev * n * width)
    part = (part.reshape(-1, hidden).astype(F32) * factor).astype(BF16)
    gains = gains * factor

    returned, terms = columns(
        flags(copy), (backward_in, out_tabs), kernel, arrived, chunks, spectrum, (part,)
    )
    grads = lax.all_gather(part, axes, tiled=True)
    received = exchange(join(returned[0]))
    grad_tokens = leave([received], tokens, upstream, gain_a, table_out, None, 0, 2, ())

    terms = terms.reshape(terms.shape[:2] + digits + (share, chans))
    terms = jnp.moveaxis(terms, range(2, 2 + len(digits)), range(len(digits)))
    reduced, _ = reduce_shares(terms, ("copy",))
    reduced = reduced.reshape(-1, 2, share, chans)
    mirrored = swap(reduced[:half], "space", n, opposite)
    to_upper = [(0, n // 2)] + [(d, n - d) for d in range(1, n // 2)]
    single = lax.ppermute(
        jnp.where(me == 0, reduced[half], reduced[half - 1]), "space", to_upper
    )
    mine = gather_copies(reduced[:half], copies)
    received = exchange(hold(join(returned[1]), (mirrored, single)))
    theirs = gather_copies(jnp.concatenate([mirrored, single[None]], axis=0), copies)
    grad_filter = filter_gradient(
        flags(copy), mirror, mine, theirs, height, wide, (grad_tokens,)
    )
    grad_tokens = leave(
        [received], tokens, upstream, gain_a, table_out, grad_tokens, 1, 2, (grad_filter,)
    )
    return (
        block_out[None],
        grad_tokens[None],
        grad_filter,
        grads[:chans],
        grads[chans:].T,
        gains[0],
        gains[1],
    )


def dft_parts(length):
    index = jnp.arange(length, dtype=jnp.int32)
    phase = index[:, None] * index[None, :] % length
    angle = phase.astype(jnp.float32) * (2.0 * math.pi / length)
    factor = 1.0 / math.sqrt(length)
    return (
        (jnp.cos(angle) * factor).astype(jnp.bfloat16),
        (jnp.sin(angle) * factor).astype(jnp.bfloat16),
    )


def row_table(length):
    cosine, sine = dft_parts(length)
    return jnp.stack([cosine, -sine])


def column_table(length, direction):
    cosine, sine = dft_parts(length)
    upper = jnp.stack([cosine, direction * sine], axis=1)
    lower = jnp.stack([-direction * sine, cosine], axis=1)
    return jnp.stack([upper, lower])


def plain_layer_norm(values):
    centre = jnp.mean(values, axis=-1, keepdims=True)
    centred = values - centre
    variance = jnp.mean(centred * centred, axis=-1, keepdims=True)
    rstd_value = lax.rsqrt(variance + EPS)
    return (centred * rstd_value, rstd_value)


def plain_norm_backward(upstream, normed, rstd_value, gain):
    scaled = upstream * gain
    result = (
        scaled
        - jnp.mean(scaled, axis=-1, keepdims=True)
        - normed * jnp.mean(scaled * normed, axis=-1, keepdims=True)
    ) * rstd_value
    lead = tuple(range(upstream.ndim - 1))
    return (result, jnp.sum(upstream * normed, axis=lead))


def apply_filter(spectrum, filter_weight, direction):
    real_part = spectrum[0].astype(jnp.float32)
    imag_part = spectrum[1].astype(jnp.float32)
    kernel_real = filter_weight[0].astype(jnp.float32)
    kernel_imag = direction * filter_weight[1].astype(jnp.float32)
    return jnp.stack(
        [
            kernel_real * real_part - kernel_imag * imag_part,
            kernel_real * imag_part + kernel_imag * real_part,
        ]
    )


def exact_gelu(values):
    return jax.nn.gelu(values, approximate=False)


def spectral(values, filter_weight, direction):
    width = values.shape[2]
    rows_tab = row_table(width)
    rows = jnp.einsum(
        "pkw,bhwc->pbhkc", rows_tab, values, preferred_element_type=jnp.float32
    ).astype(jnp.bfloat16)
    columns = lax.all_to_all(rows, "space", split_axis=3, concat_axis=2, tiled=True)
    height = columns.shape[2]
    spectrum = jnp.einsum(
        "qmph,pbhkc->qbmkc", column_table(height, 1), columns, preferred_element_type=jnp.float32
    ).astype(jnp.bfloat16)
    weighted = apply_filter(spectrum, filter_weight[:, None], direction).astype(jnp.bfloat16)
    returned = jnp.einsum(
        "qmph,pbhkc->qbmkc", column_table(height, -1), weighted, preferred_element_type=jnp.float32
    ).astype(jnp.bfloat16)
    back_rows = lax.all_to_all(returned, "space", split_axis=2, concat_axis=3, tiled=True)
    output = jnp.einsum("pkw,pbhkc->bhwc", rows_tab, back_rows, preferred_element_type=jnp.float32)
    return (output, spectrum)


def plain_body(noisy_tokens, grad_out, filter_weight, weight_in, weight_out, gain_one, gain_two):
    batch, rows_dev, width, chans = noisy_tokens.shape
    inputs = noisy_tokens.astype(jnp.float32)
    normed_one, rstd_one = plain_layer_norm(inputs)
    mixed_in = (normed_one * gain_one).astype(jnp.bfloat16)
    spatial, spectrum = spectral(mixed_in, filter_weight, 1)
    normed_two, rstd_two = plain_layer_norm(spatial)
    mlp_in = (normed_two * gain_two).astype(jnp.bfloat16).reshape(-1, chans)
    preact = jnp.dot(mlp_in, weight_in, preferred_element_type=jnp.float32)
    activated = exact_gelu(preact).astype(jnp.bfloat16)
    mlp_out = jnp.dot(activated, weight_out, preferred_element_type=jnp.float32)
    block_out = (inputs + mlp_out.reshape(inputs.shape)).astype(jnp.bfloat16)
    upstream = grad_out.reshape(-1, chans)
    grad_act = jnp.dot(upstream, weight_out.T, preferred_element_type=jnp.float32)
    grad_pre = jax.vjp(exact_gelu, preact)[1](grad_act)[0].astype(jnp.bfloat16)
    sum_out = jnp.dot(activated.T, upstream, preferred_element_type=jnp.float32)
    sum_in = jnp.dot(mlp_in.T, grad_pre, preferred_element_type=jnp.float32)
    grad_mlp = jnp.dot(grad_pre, weight_in.T, preferred_element_type=jnp.float32).reshape(
        inputs.shape
    )
    grad_spatial, sum_gain_two = plain_norm_backward(grad_mlp, normed_two, rstd_two, gain_two)
    back_spatial, adjoint = spectral(grad_spatial.astype(jnp.bfloat16), filter_weight, -1)
    spec_f = spectrum.astype(jnp.float32)
    adj_f = adjoint.astype(jnp.float32)
    filter_terms = jnp.stack(
        [
            jnp.sum(adj_f[0] * spec_f[0] + adj_f[1] * spec_f[1], axis=0),
            jnp.sum(adj_f[1] * spec_f[0] - adj_f[0] * spec_f[1], axis=0),
        ]
    )
    grad_filter = lax.psum(filter_terms.astype(jnp.bfloat16), "copy").astype(jnp.float32)
    grad_normed, sum_gain_one = plain_norm_backward(back_spatial, normed_one, rstd_one, gain_one)
    grad_tokens = (grad_out.astype(jnp.float32) + grad_normed).astype(jnp.bfloat16)
    local_sums = (sum_in, sum_out, sum_gain_one, sum_gain_two)
    summed = lax.psum(
        (local_sums[0], local_sums[1], local_sums[2], local_sums[3]), ("copy", "space")
    )
    total_tokens = batch * lax.axis_size("copy") * rows_dev * lax.axis_size("space") * width
    factor = 1.0 / math.sqrt(total_tokens)
    return (
        block_out,
        grad_tokens,
        grad_filter,
        (summed[0] * factor).astype(jnp.bfloat16),
        (summed[1] * factor).astype(jnp.bfloat16),
        summed[2] * factor,
        summed[3] * factor,
    )


def solution(mesh):
    def program(*arrays):
        rows_dev, wide = arrays[0].shape[1], arrays[2].shape[2]
        n = lax.axis_size("space")
        tiled = rows_dev % 32 == 0 and wide % 32 == 0 and n & (n - 1) == 0
        return (body if tiled else plain_body)(*arrays)

    return jax.shard_map(
        program,
        mesh=mesh,
        in_specs=(
            P("copy", "space", None, None),
            P("copy", "space", None, None),
            P(None, None, "space", None),
            P(),
            P(),
            P(),
            P(),
        ),
        out_specs=(
            P("copy", "space", None, None),
            P("copy", "space", None, None),
            P(None, None, "space", None),
            P(),
            P(),
            P(),
            P(),
        ),
        check_vma=False,
    )
```

```python
import functools
import math

import jax
import jax.numpy as jnp
import ml_dtypes
import numpy as np
from jax import lax
from jax.experimental import pallas as pl
from jax.experimental.pallas import tpu as pltpu
from jax.sharding import PartitionSpec as P

EPS = 1e-06
LANES = 128
VMEM_LIMIT = 60 * 1024 * 1024
BF16 = jnp.bfloat16
F32 = jnp.float32


def dft_pair(length):
    index = np.arange(length, dtype=np.int64)
    angle = (index[:, None] * index[None, :] % length) * (2.0 * math.pi / length)
    factor = 1.0 / math.sqrt(length)
    rounded = lambda a: a.astype(np.float32).astype(ml_dtypes.bfloat16).astype(np.float32)
    return rounded(np.cos(angle) * factor), rounded(np.sin(angle) * factor)


def row_tables(width, n):
    cosine, sine = dft_pair(width)
    own = width // n
    half = own // 2
    forward = np.zeros((n, 2, half, width), np.float32)
    weight = np.full((n, 2, half, 1), 2.0, np.float32)
    for d in range(n):
        first = own * d + (1 if d >= n // 2 else 0)
        forward[d, 0] = cosine[first : first + half]
        forward[d, 1] = -sine[first : first + half]
    forward[0, 1, 0] = cosine[width // 2]
    weight[0, :, 0] = 1.0
    shape = (n, 2 * half, width)
    return (
        forward.reshape(shape).astype(ml_dtypes.bfloat16),
        (forward * weight).reshape(shape).astype(ml_dtypes.bfloat16),
    )


def column_tables(height, n, chunks):
    cosine, sine = dft_pair(height)
    zero = np.zeros_like(cosine)
    rows = height // n // chunks

    def arrange(blocks):
        full = np.stack([np.stack(line, axis=1) for line in blocks])
        full = full.reshape(2 * height, 2, n, chunks, rows)
        return full.transpose(0, 3, 2, 1, 4).reshape(2 * height, 2 * height)

    middle = arrange([[zero, cosine], [zero, -sine]])
    first = arrange([[cosine, zero], [-sine, zero]])
    other = arrange([[cosine, sine], [-sine, cosine]])
    backward = np.stack([middle, first, other]).transpose(0, 2, 1)
    backward = backward.reshape(3, chunks, n, 2 * rows, 2 * height)
    return backward.astype(ml_dtypes.bfloat16)


def mirror_table(height):
    table = np.zeros((height, height), np.float32)
    table[np.arange(height), (-np.arange(height)) % height] = 1.0
    return table.astype(ml_dtypes.bfloat16)


def dot(a, b):
    return jnp.dot(a, b, preferred_element_type=F32)


def dot_tn(a, b):
    return lax.dot_general(a, b, (((0,), (0,)), ((), ())), preferred_element_type=F32)


def normalize(values):
    centred = values - jnp.mean(values, axis=-1, keepdims=True)
    variance = jnp.mean(centred * centred, axis=-1, keepdims=True)
    rstd = lax.rsqrt(variance + EPS)
    return centred * rstd, rstd


def norm_backward(upstream, normed, rstd, gain):
    scaled = upstream * gain
    return (
        scaled
        - jnp.mean(scaled, axis=-1, keepdims=True)
        - normed * jnp.mean(scaled * normed, axis=-1, keepdims=True)
    ) * rstd


def gelu_and_slope(v):
    e = jnp.exp(v * v * -0.5)
    d = 1.0 + (0.3275911 / math.sqrt(2.0)) * jnp.abs(v)
    t = pl.reciprocal(d, approx=True)
    t = t * (2.0 - d * t)
    poly = 0.5 * 1.061405429
    for coefficient in (-1.453152027, 1.421413741, -0.284496736, 0.254829592):
        poly = poly * t + 0.5 * coefficient
    tail = poly * t * e
    phi = jnp.where(v < 0.0, tail, 1.0 - tail)
    return v * phi, phi + v * e * (1.0 / math.sqrt(2.0 * math.pi))


def spaced(count):
    groups = -(-count // 8)
    return 8 * (groups + 1 - groups % 2)


def lanes(c):
    return slice(c * LANES, (c + 1) * LANES)


def unpack(received, scratch):
    count, rows, chans = received[0].shape
    pitch = spaced(rows)

    def step(k, carry):
        for s, ref in enumerate(received):
            start = pl.multiple_of((s * count + k) * pitch, 8)
            for c in range(chans // LANES):
                scratch[c, pl.ds(start, rows), :] = ref[k, :, lanes(c)].astype(F32)
        return carry

    lax.fori_loop(0, count, step, 0, unroll=2)


def read_row(scratch, row, columns, rows):
    parts = [
        scratch[c, pl.ds(row, columns, stride=spaced(rows)), :].astype(BF16)
        for c in range(scratch.shape[0])
    ]
    return jnp.concatenate(parts, axis=1)


def write_row(scratch, row, columns, values):
    start = pl.multiple_of(row * spaced(columns), 8)
    for c in range(scratch.shape[0]):
        scratch[c, pl.ds(start, columns), :] = values[:, lanes(c)]


def pack(scratch, columns, outgoing):
    count, rows, _ = outgoing[0].shape

    def step(k, carry):
        for s, ref in enumerate(outgoing):
            for c in range(scratch.shape[0]):
                part = scratch[c, pl.ds(s * count + k, rows, stride=spaced(columns)), :]
                ref[k, :, lanes(c)] = part.astype(BF16)
        return carry

    lax.fori_loop(0, count, step, 0, unroll=2)


def params():
    return pltpu.CompilerParams(vmem_limit_bytes=VMEM_LIMIT)


def resident(shape):
    return pl.BlockSpec(shape, lambda *_: (0,) * len(shape), pipeline_mode=pl.Buffered(1))


ANYWHERE = pl.BlockSpec(memory_space=pl.ANY)


def cost(flops, size):
    return pl.CostEstimate(flops=int(flops), bytes_accessed=int(size), transcendentals=0)


def shape_of(shape, dtype=BF16):
    return jax.ShapeDtypeStruct(tuple(shape), dtype)


def hold(value, after):
    return pl.pallas_call(
        lambda *refs: None,
        in_specs=[ANYWHERE] * (1 + len(after)),
        out_specs=ANYWHERE,
        out_shape=shape_of(value.shape, value.dtype),
        input_output_aliases={0: 0},
        compiler_params=params(),
        cost_estimate=cost(0, 0),
        name="hold",
    )(value, *after)


def enter_kernel(tokens, gain, table, *rest):
    outgoing, scratch = rest[-2:-1], rest[-1]
    step = pl.program_id(0)
    block, width, _ = tokens.shape
    for r in range(block):
        normed, _ = normalize(tokens[r].astype(F32))
        mixed = (normed * gain[...]).astype(BF16)
        write_row(scratch, step * block + r, width, dot(table[...], mixed))

    @pl.when(step == pl.num_programs(0) - 1)
    def _():
        pack(scratch, width, outgoing)


def enter(tokens, gain, table, block):
    rows, width, chans = tokens.shape
    steps = rows // block
    out = (width, rows, chans)
    return pl.pallas_call(
        enter_kernel,
        grid=(steps,),
        in_specs=[
            pl.BlockSpec((block, width, chans), lambda i: (i, 0, 0)),
            resident((1, chans)),
            resident((width, width)),
        ],
        out_specs=resident(out),
        out_shape=shape_of(out),
        scratch_shapes=[pltpu.VMEM((chans // LANES, rows * spaced(width), LANES), F32)],
        compiler_params=params(),
        cost_estimate=cost(2 * rows * width * width * chans, 4 * rows * width * chans),
        name="enter_rows",
    )(tokens, gain, table)


def mlp_kernel(
    n, later, tokens, upstream, gain, table_out, table_in, w_in, w_out, w_in_t, w_out_t, *rest
):
    received, rest = rest[:n], rest[n:]
    if later:
        (_, *before), rest = rest[:4], rest[4:]
    block_out, outgoing, rest = rest[0], rest[1 : n + 1], rest[n + 1 :]
    sum_in, sum_out, sum_gain, unpacked, packed = rest
    step = pl.program_id(0)
    block, width, chans = tokens.shape
    rows = received[0].shape[1]
    hidden = w_in.shape[1]
    part = min(512, hidden)

    @pl.when(step == 0)
    def _():
        unpack(received, unpacked)
        for i, ref in enumerate((sum_in, sum_out, sum_gain)):
            ref[...] = before[i][...] if later else jnp.zeros_like(ref)

    spatial = jnp.concatenate(
        [
            dot(table_out[...], read_row(unpacked, step * block + r, width, rows))
            for r in range(block)
        ],
        axis=0,
    )
    normed, rstd = normalize(spatial)
    mlp_in = (normed * gain[...]).astype(BF16)
    grad = upstream[...].reshape(block * width, chans)
    out = tokens[...].reshape(block * width, chans).astype(F32)
    grad_mlp = jnp.zeros_like(spatial)

    def first(cols):
        return dot(mlp_in, w_in[:, cols]), dot(grad, w_out_t[:, cols])

    parts = [slice(f, f + part) for f in range(0, hidden, part)]
    ahead = first(parts[0])
    for f, cols in enumerate(parts):
        preact, grad_act = ahead
        if f + 1 < len(parts):
            ahead = first(parts[f + 1])
        value, slope = gelu_and_slope(preact)
        activated = value.astype(BF16)
        grad_pre = (grad_act * slope).astype(BF16)
        out = out + dot(activated, w_out[cols, :])
        grad_mlp = grad_mlp + dot(grad_pre, w_in_t[cols, :])
        sum_out[:, cols] += dot_tn(grad, activated)
        sum_in[:, cols] += dot_tn(mlp_in, grad_pre)
    block_out[...] = out.astype(BF16).reshape(block, width, chans)
    grad_spatial = norm_backward(grad_mlp, normed, rstd, gain[...])
    sum_gain[0:8] += jnp.sum((grad_mlp * normed).reshape(-1, 8, chans), axis=0)
    sum_gain[8:16] += jnp.sum((grad_spatial * spatial).reshape(-1, 8, chans), axis=0)
    sent = grad_spatial.astype(BF16)
    for r in range(block):
        values = dot(table_in[...], sent[r * width : (r + 1) * width])
        write_row(packed, step * block + r, width, values)

    @pl.when(step == pl.num_programs(0) - 1)
    def _():
        pack(packed, width, outgoing)


def mlp(received, tokens, upstream, gain, tables, weights, previous, chunk, block):
    n = len(received)
    count, rows, chans = received[0].shape
    width = tokens.shape[1]
    hidden = weights[0].shape[1]
    steps = rows // block
    by_rows = pl.BlockSpec((block, width, chans), lambda i: (i + chunk * steps, 0, 0))
    operands = [tokens, upstream, gain, *tables, *weights, *received]
    in_specs = [
        by_rows,
        by_rows,
        resident((1, chans)),
        resident((width, width)),
        resident((width, width)),
        resident((chans, hidden)),
        resident((hidden, chans)),
        resident((hidden, chans)),
        resident((chans, hidden)),
    ] + [resident((count, rows, chans))] * n
    aliases = {}
    if previous is not None:
        aliases = {len(operands): 0}
        operands += previous
        in_specs += [ANYWHERE] + [resident(p.shape) for p in previous[1:]]
    flops = 2 * rows * width * chans * (6 * hidden + 2 * width)
    outputs = pl.pallas_call(
        functools.partial(mlp_kernel, n, previous is not None),
        grid=(steps,),
        in_specs=in_specs,
        out_specs=[by_rows]
        + [resident((count, rows, chans))] * n
        + [resident((chans, hidden)), resident((chans, hidden)), resident((16, chans))],
        out_shape=[shape_of(tokens.shape)]
        + [shape_of((count, rows, chans))] * n
        + [shape_of((chans, hidden), F32)] * 2
        + [shape_of((16, chans), F32)],
        scratch_shapes=[
            pltpu.VMEM((chans // LANES, width * spaced(rows), LANES), F32),
            pltpu.VMEM((chans // LANES, rows * spaced(width), LANES), F32),
        ],
        input_output_aliases=aliases,
        compiler_params=params(),
        cost_estimate=cost(flops, 10 * rows * width * chans),
        name="mlp_rows",
    )(*operands)
    return outputs[0], outputs[1 : n + 1], outputs[n + 1 :]


def leave_kernel(n, tokens, upstream, gain, table_out, *rest):
    received, (grad_tokens, unpacked) = rest[:n], rest[-2:]
    step = pl.program_id(0)
    block, width, _ = tokens.shape
    rows = received[0].shape[1]

    @pl.when(step == 0)
    def _():
        unpack(received, unpacked)

    for r in range(block):
        back = dot(table_out[...], read_row(unpacked, step * block + r, width, rows))
        normed, rstd = normalize(tokens[r].astype(F32))
        grad = norm_backward(back, normed, rstd, gain[...])
        grad_tokens[r] = (upstream[r].astype(F32) + grad).astype(BF16)


def leave(received, tokens, upstream, gain, table_out, previous, chunk, block, after):
    n = len(received)
    count, rows, chans = received[0].shape
    width = tokens.shape[1]
    steps = rows // block
    by_rows = pl.BlockSpec((block, width, chans), lambda i: (i + chunk * steps, 0, 0))
    operands = [tokens, upstream, gain, table_out, *received]
    in_specs = [by_rows, by_rows, resident((1, chans)), resident((width, width))]
    in_specs += [resident((count, rows, chans))] * n
    aliases = {}
    if previous is not None:
        aliases = {len(operands): 0}
        operands.append(previous)
        in_specs.append(ANYWHERE)
    operands += after
    in_specs += [ANYWHERE] * len(after)
    return pl.pallas_call(
        functools.partial(leave_kernel, n),
        grid=(steps,),
        in_specs=in_specs,
        out_specs=by_rows,
        out_shape=shape_of(tokens.shape),
        scratch_shapes=[pltpu.VMEM((chans // LANES, width * spaced(rows), LANES), F32)],
        input_output_aliases=aliases,
        compiler_params=params(),
        cost_estimate=cost(2 * rows * width * width * chans, 8 * rows * width * chans),
        name="leave_rows",
    )(*operands)


def columns_kernel(count, outs, back, flags, table_f, table_b, kernel, *rest):
    spectrum, rest = (rest[0], rest[1:]) if back else (None, rest)
    received, (*outgoing, held) = rest[:count], rest[-outs - 1 :]
    step, last = pl.program_id(0), pl.num_programs(0) - 1
    per, _, height, chans = kernel.shape

    def load(j):
        return jnp.concatenate([ref[:, :, j].reshape(-1, chans) for ref in received], axis=0)

    def store(j, values):
        values = values.astype(BF16)
        size = values.shape[0] // len(outgoing)
        for i, ref in enumerate(outgoing):
            n, _, _, rows, _ = ref.shape
            ref[:, :, j] = values[i * size : (i + 1) * size].reshape(n, 2, rows, chans)

    def filtered(slot, found):
        found = found.astype(BF16)
        real, imag = found[:height].astype(F32), found[height:].astype(F32)
        k_real, k_imag = kernel[slot, 0].astype(F32), kernel[slot, 1].astype(F32)
        if back:
            s_real, s_imag = spectrum[slot, 0].astype(F32), spectrum[slot, 1].astype(F32)
            held[slot, 0] = (real * s_real + imag * s_imag).astype(BF16)
            held[slot, 1] = (imag * s_real - real * s_imag).astype(BF16)
            k_imag = -k_imag
        else:
            held[slot, 0] = found[:height]
            held[slot, 1] = found[height:]
        upper = (k_real * real - k_imag * imag).astype(BF16)
        lower = (k_real * imag + k_imag * real).astype(BF16)
        return jnp.concatenate([upper, lower], axis=0)

    @pl.when(step < last)
    def _():
        at = [1 + step * per + i for i in range(per)]
        found = dot(table_f[2], jnp.concatenate([load(j) for j in at], axis=1))
        weighted = [filtered(i, found[:, i * chans : (i + 1) * chans]) for i in range(per)]
        result = dot(table_b[2], jnp.concatenate(weighted, axis=1))
        for i, j in enumerate(at):
            store(j, result[:, i * chans : (i + 1) * chans])

    @pl.when(step == last)
    def _():
        values = load(0)
        kind = 2 - flags[1]
        zero = filtered(0, dot(table_f[kind], values))
        middle = filtered(1, dot(table_f[0], values))
        store(0, dot(table_b[kind], zero) + dot(table_b[0], middle))
        for i in range(2, per):
            held[i] = jnp.zeros_like(held[i])


def columns(flags, tables, kernel, received, outs, spectrum=None, after=()):
    count = len(received)
    n, _, half, rows, chans = received[0].shape
    sent = (n, 2, half, count * rows // outs, chans)
    slots, _, height, _ = kernel.shape
    per = columns_per_step(half)
    held = pl.BlockSpec((per, 2, height, chans), lambda t, flags: (t, 0, 0, 0))
    table = resident((3, 2 * height, 2 * height))
    back = spectrum is not None
    outputs = pl.pallas_call(
        functools.partial(columns_kernel, count, outs, back),
        grid_spec=pltpu.PrefetchScalarGridSpec(
            num_scalar_prefetch=1,
            grid=(slots // per,),
            in_specs=[table, table, held]
            + [held] * back
            + [resident(r.shape) for r in received]
            + [ANYWHERE] * len(after),
            out_specs=[resident(sent)] * outs + [held],
        ),
        out_shape=[shape_of(sent)] * outs + [shape_of(kernel.shape)],
        compiler_params=params(),
        cost_estimate=cost(16 * height * height * chans * slots, 20 * height * chans * slots),
        name="filter_columns",
    )(flags, *tables, kernel, *([spectrum] if back else []), *received, *after)
    return outputs[:outs], outputs[outs]


def columns_per_step(half):
    return 3 if (half - 1) % 3 == 0 else 2 if (half - 1) % 2 == 0 else 1


def slot_count(half):
    per = max(2, columns_per_step(half))
    return half - 1 + per


def filter_part_kernel(copies, flags, mirror, own, *rest):
    mains, extras = rest[:copies], rest[copies : 2 * copies]
    kernel, scr_own, scr_main, scr_extra = rest[-4:]
    part = pl.program_id(0)
    upper, first, me = flags[0], flags[1], flags[2]
    _, height, wide, _ = own.shape
    half = wide // 2
    share = height // copies
    pitch_own, pitch = spaced(wide), spaced(half)

    def spread_own(m, carry):
        scr_own[pl.ds(pl.multiple_of(m * pitch_own, 8), wide), :] = own[0, m].astype(F32)
        return carry

    lax.fori_loop(0, height, spread_own, 0, unroll=8)
    for i in range(copies):
        owner = jnp.bitwise_xor(me, i)

        def spread_main(m, carry):
            at = pl.multiple_of((owner * share + m) * pitch, 8)
            scr_main[pl.ds(at, half), :] = mains[i][0, m].astype(F32)
            return carry

        lax.fori_loop(0, share, spread_main, 0, unroll=8)
        at = pl.multiple_of(owner * share, share)
        scr_extra[pl.ds(at, share), :] = extras[i][0].astype(F32)
    sign = jnp.where(part == 0, 0.5, -0.5)
    extra = scr_extra[...]
    middle = 0.5 * extra + sign * dot(mirror[...], extra.astype(BF16))
    kernel[half, 0] = jnp.where(first == 1, middle, 0.0).astype(BF16)
    for i in range(half + 1, kernel.shape[0]):
        kernel[i, 0] = jnp.zeros((height, LANES), BF16)
    for j in range(half):
        mine = scr_own[pl.ds(j + upper, height, stride=pitch_own), :]
        if j == 0:
            other = scr_main[pl.ds(half - 1, height, stride=pitch), :]
            lower = jnp.where(first == 1, mine, extra)
            other = jnp.where(upper == 1, other, lower)
        else:
            other = scr_main[pl.ds(half - j - upper, height, stride=pitch), :]
        turned = dot(mirror[...], other.astype(BF16))
        kernel[(j - 1) % half, 0] = (0.5 * mine + sign * turned).astype(BF16)


def filter_part(flags, mirror, own, mains, extras, after):
    _, height, wide, chans = own.shape
    copies = len(mains)
    half, share = wide // 2, height // copies
    slots = slot_count(half)
    return pl.pallas_call(
        functools.partial(filter_part_kernel, copies),
        grid_spec=pltpu.PrefetchScalarGridSpec(
            num_scalar_prefetch=1,
            grid=(2, chans // LANES),
            in_specs=[
                pl.BlockSpec((height, height), lambda p, c, flags: (0, 0)),
                pl.BlockSpec((1, height, wide, LANES), lambda p, c, flags: (p, 0, 0, c)),
            ]
            + [pl.BlockSpec((1, share, half, LANES), lambda p, c, flags: (p, 0, 0, c))] * copies
            + [pl.BlockSpec((1, share, LANES), lambda p, c, flags: (p, 0, c))] * copies
            + [ANYWHERE] * len(after),
            out_specs=pl.BlockSpec((slots, 1, height, LANES), lambda p, c, flags: (0, p, 0, c)),
            scratch_shapes=[
                pltpu.VMEM((height * spaced(wide), LANES), F32),
                pltpu.VMEM((height * spaced(half), LANES), F32),
                pltpu.VMEM((height, LANES), F32),
            ],
        ),
        out_shape=shape_of((slots, 2, height, chans)),
        compiler_params=params(),
        cost_estimate=cost(4 * height * height * chans * half, 16 * height * half * chans),
        name="filter_part",
    )(flags, mirror, own, *mains, *extras, *after)


def filter_gradient_kernel(copies, flags, mirror, *rest):
    mine, theirs = rest[:copies], rest[copies : 2 * copies]
    out, gathered, turned = rest[-3:]
    part = pl.program_id(0)
    upper, me = flags[0], flags[2]
    _, height, wide, _ = out.shape
    half = wide // 2
    share = height // copies
    pitch = spaced(height)
    for i in range(copies):
        at = pl.multiple_of(jnp.bitwise_xor(me, i) * share, share)
        gathered[0:half, pl.ds(at, share), :] = mine[i][:, 0]
        gathered[half:, pl.ds(at, share), :] = theirs[i][:, 0]
    sign = jnp.where(part == 0, 1.0, -1.0)
    for k in range(wide):
        if k == 0:
            index = jnp.where(upper == 1, 2 * half, half - 1)
        elif k < half:
            index = k - 1 - upper
            index = jnp.where(index < 0, half - 1, index)
        elif k == half:
            index = jnp.where(upper == 1, half - 2, 2 * half - 2)
        else:
            index = wide - 2 - k + upper
            index = half + jnp.where(index < 0, half - 1, index)
        value = gathered[index]
        if 0 < k < half:
            value = value.astype(F32)
        else:
            other = sign * dot(mirror[...], value)
            if k == 0:
                other = jnp.where(upper == 1, other, value.astype(F32))
            elif k == half:
                other = jnp.where(upper == 1, value.astype(F32), other)
            value = other
        turned[pl.ds(k * pitch, height), :] = value

    def step(m, carry):
        out[0, m] = turned[pl.ds(m, wide, stride=pitch), :]
        return carry

    lax.fori_loop(0, height, step, 0, unroll=8)


def filter_gradient(flags, mirror, mine, theirs, height, wide, after):
    _, _, share, chans = mine[0].shape
    copies, half = len(mine), wide // 2
    block = lambda slots: pl.BlockSpec(
        (slots, 1, share, LANES), lambda p, c, flags: (0, p, 0, c)
    )
    return pl.pallas_call(
        functools.partial(filter_gradient_kernel, copies),
        grid_spec=pltpu.PrefetchScalarGridSpec(
            num_scalar_prefetch=1,
            grid=(2, chans // LANES),
            in_specs=[pl.BlockSpec((height, height), lambda p, c, flags: (0, 0))]
            + [block(half)] * copies
            + [block(half + 1)] * copies
            + [ANYWHERE] * len(after),
            out_specs=pl.BlockSpec((1, height, wide, LANES), lambda p, c, flags: (p, 0, 0, c)),
            scratch_shapes=[
                pltpu.VMEM((wide + 1, height, LANES), BF16),
                pltpu.VMEM((wide * spaced(height), LANES), F32),
            ],
        ),
        out_shape=shape_of((2, height, wide, chans), F32),
        compiler_params=params(),
        cost_estimate=cost(2 * height * height * chans * wide, 12 * height * wide * chans),
        name="filter_gradient",
    )(flags, mirror, *mine, *theirs, *after)


def swap(value, axis, size, partner):
    return lax.ppermute(value, axis, [(i, partner(i)) for i in range(size)])


def swap_bits(value, axis, size, bits):
    return swap(value, axis, size, lambda i: i ^ bits)


def exchange(value):
    return lax.all_to_all(value, "space", split_axis=0, concat_axis=0, tiled=True)


def gather_copies(value, copies):
    parts = {0: value}
    bit = copies // 2
    while bit:
        for key in list(parts):
            parts[key ^ bit] = swap_bits(parts[key], "copy", copies, bit)
        bit //= 2
    return [parts[i] for i in range(copies)]


def reduce_shares(value, axes, extra=None):
    places, place = [], 0
    for name in axes:
        digits = lax.axis_size(name).bit_length() - 1
        places += [(name, bit, place + digits - 1 - bit) for bit in range(digits)]
        place += digits
    for name, bit, place in places:
        size, own = lax.axis_size(name), (lax.axis_index(name) >> bit) & 1
        kept = lax.dynamic_index_in_dim(value, own, place, keepdims=True)
        sent = lax.dynamic_index_in_dim(value, 1 - own, place, keepdims=True)
        other = swap_bits(sent, name, size, 1 << bit)
        value = (kept.astype(F32) + other.astype(F32)).astype(value.dtype)
        if extra is not None:
            extra = extra + swap_bits(extra, name, size, 1 << bit)
    return value, extra


def body(noisy_tokens, grad_out, filter_weight, weight_in, weight_out, gain_one, gain_two):
    _, rows_dev, width, chans = noisy_tokens.shape
    height, wide = filter_weight.shape[1:3]
    digits = (2,) * (lax.axis_size("copy").bit_length() - 1)
    hidden = weight_in.shape[1]
    half = wide // 2
    n, copies = lax.axis_size("space"), lax.axis_size("copy")
    chunks = 2
    rows = rows_dev // chunks
    tokens, upstream = noisy_tokens[0], grad_out[0]
    me, copy = lax.axis_index("space"), lax.axis_index("copy")

    share = height // copies
    at = copy * share
    opposite = lambda d: n - 1 - d
    main = lax.dynamic_slice(filter_weight, (0, at, half, 0), (2, share, half, chans))
    main = swap(main, "space", n, opposite)
    to_lower = [(n // 2, 0)] + [(e, n - e) for e in range(n // 2 + 1, n)]
    single = lax.dynamic_slice(filter_weight, (0, at, 0, 0), (2, share, 1, chans))
    single = lax.ppermute(single.reshape(2, share, chans), "space", to_lower)

    forward, weighted = row_tables(width, n)
    table_in = jnp.asarray(forward.reshape(width, width))
    table_out = jnp.asarray(np.ascontiguousarray(weighted.reshape(width, width).T))
    whole, cut = (
        column_tables(height, n, c).reshape(3, 2 * height, 2 * height) for c in (1, chunks)
    )
    forward_in, backward_in = (
        jnp.asarray(np.ascontiguousarray(t.transpose(0, 2, 1))) for t in (whole, cut)
    )
    out_tabs = jnp.asarray(cut)
    mirror = jnp.asarray(mirror_table(height))
    gain_a, gain_b = gain_one.reshape(1, chans), gain_two.reshape(1, chans)
    upper = (me >= n // 2).astype(jnp.int32)
    first = (me == 0).astype(jnp.int32)

    def flags(index):
        return jnp.stack([upper, first, index.astype(jnp.int32)])

    def split(value):
        return value.reshape(n, 2, half, -1, chans)

    def join(value):
        return value.reshape(width, -1, chans)

    entered = hold(enter(tokens, gain_a, table_in, 2), (main, single))
    arrived = [split(exchange(entered))]
    mains, singles = gather_copies(main, copies), gather_copies(single, copies)
    weights = (weight_in, weight_out, weight_in.T, weight_out.T)
    kernel = filter_part(flags(copy), mirror, filter_weight, mains, singles, weights[2:])
    returned, spectrum = columns(flags(copy), (forward_in, out_tabs), kernel, arrived, chunks)

    tables = (table_out, table_in)
    arrived = []
    previous = None
    for c in range(chunks):
        received = exchange(join(returned[c]))
        block_out, sent, sums = mlp(
            [received], tokens, upstream, gain_b, tables, weights, previous, c, 4
        )
        arrived.append(split(exchange(sent[0])))
        previous = [block_out, *sums]

    axes = ("copy", "space")
    sum_in, sum_out, sum_gain = sums
    both = jnp.concatenate([sum_in, sum_out], axis=0).astype(BF16)
    both = both.reshape((2,) * ((copies * n).bit_length() - 1) + (-1, hidden))
    gains = jnp.stack([jnp.sum(sum_gain[8:], axis=0) / gain_one, jnp.sum(sum_gain[:8], axis=0)])
    part, gains = reduce_shares(both, axes, gains)
    factor = 1.0 / math.sqrt(copies * rows_dev * n * width)
    part = (part.reshape(-1, hidden).astype(F32) * factor).astype(BF16)
    gains = gains * factor

    returned, terms = columns(
        flags(copy), (backward_in, out_tabs), kernel, arrived, chunks, spectrum, (part, gains)
    )
    grads = lax.all_gather(part, axes, tiled=True)
    received = exchange(join(returned[0]))
    grad_tokens = leave([received], tokens, upstream, gain_a, table_out, None, 0, 2, ())

    terms = terms.reshape(terms.shape[:2] + digits + (share, chans))
    terms = jnp.moveaxis(terms, range(2, 2 + len(digits)), range(len(digits)))
    reduced, _ = reduce_shares(terms, ("copy",))
    reduced = reduced.reshape(-1, 2, share, chans)
    mirrored = swap(reduced[:half], "space", n, opposite)
    to_upper = [(0, n // 2)] + [(d, n - d) for d in range(1, n // 2)]
    single = lax.ppermute(
        jnp.where(me == 0, reduced[half], reduced[half - 1]), "space", to_upper
    )
    mine = gather_copies(reduced[:half], copies)
    received = exchange(hold(join(returned[1]), (mirrored, single, *mine, grad_tokens)))
    theirs = gather_copies(jnp.concatenate([mirrored, single[None]], axis=0), copies)
    grad_filter = filter_gradient(
        flags(copy), mirror, mine, theirs, height, wide, ()
    )
    grad_tokens = leave(
        [received], tokens, upstream, gain_a, table_out, grad_tokens, 1, 2, (grad_filter,)
    )
    return (
        block_out[None],
        grad_tokens[None],
        grad_filter,
        grads[:chans],
        grads[chans:].T,
        gains[0],
        gains[1],
    )


def dft_parts(length):
    index = jnp.arange(length, dtype=jnp.int32)
    phase = index[:, None] * index[None, :] % length
    angle = phase.astype(jnp.float32) * (2.0 * math.pi / length)
    factor = 1.0 / math.sqrt(length)
    return (
        (jnp.cos(angle) * factor).astype(jnp.bfloat16),
        (jnp.sin(angle) * factor).astype(jnp.bfloat16),
    )


def row_table(length):
    cosine, sine = dft_parts(length)
    return jnp.stack([cosine, -sine])


def column_table(length, direction):
    cosine, sine = dft_parts(length)
    upper = jnp.stack([cosine, direction * sine], axis=1)
    lower = jnp.stack([-direction * sine, cosine], axis=1)
    return jnp.stack([upper, lower])


def plain_layer_norm(values):
    centre = jnp.mean(values, axis=-1, keepdims=True)
    centred = values - centre
    variance = jnp.mean(centred * centred, axis=-1, keepdims=True)
    rstd_value = lax.rsqrt(variance + EPS)
    return (centred * rstd_value, rstd_value)


def plain_norm_backward(upstream, normed, rstd_value, gain):
    scaled = upstream * gain
    result = (
        scaled
        - jnp.mean(scaled, axis=-1, keepdims=True)
        - normed * jnp.mean(scaled * normed, axis=-1, keepdims=True)
    ) * rstd_value
    lead = tuple(range(upstream.ndim - 1))
    return (result, jnp.sum(upstream * normed, axis=lead))


def apply_filter(spectrum, filter_weight, direction):
    real_part = spectrum[0].astype(jnp.float32)
    imag_part = spectrum[1].astype(jnp.float32)
    kernel_real = filter_weight[0].astype(jnp.float32)
    kernel_imag = direction * filter_weight[1].astype(jnp.float32)
    return jnp.stack(
        [
            kernel_real * real_part - kernel_imag * imag_part,
            kernel_real * imag_part + kernel_imag * real_part,
        ]
    )


def exact_gelu(values):
    return jax.nn.gelu(values, approximate=False)


def spectral(values, filter_weight, direction):
    width = values.shape[2]
    rows_tab = row_table(width)
    rows = jnp.einsum(
        "pkw,bhwc->pbhkc", rows_tab, values, preferred_element_type=jnp.float32
    ).astype(jnp.bfloat16)
    columns = lax.all_to_all(rows, "space", split_axis=3, concat_axis=2, tiled=True)
    height = columns.shape[2]
    spectrum = jnp.einsum(
        "qmph,pbhkc->qbmkc", column_table(height, 1), columns, preferred_element_type=jnp.float32
    ).astype(jnp.bfloat16)
    weighted = apply_filter(spectrum, filter_weight[:, None], direction).astype(jnp.bfloat16)
    returned = jnp.einsum(
        "qmph,pbhkc->qbmkc", column_table(height, -1), weighted, preferred_element_type=jnp.float32
    ).astype(jnp.bfloat16)
    back_rows = lax.all_to_all(returned, "space", split_axis=2, concat_axis=3, tiled=True)
    output = jnp.einsum("pkw,pbhkc->bhwc", rows_tab, back_rows, preferred_element_type=jnp.float32)
    return (output, spectrum)


def plain_body(noisy_tokens, grad_out, filter_weight, weight_in, weight_out, gain_one, gain_two):
    batch, rows_dev, width, chans = noisy_tokens.shape
    inputs = noisy_tokens.astype(jnp.float32)
    normed_one, rstd_one = plain_layer_norm(inputs)
    mixed_in = (normed_one * gain_one).astype(jnp.bfloat16)
    spatial, spectrum = spectral(mixed_in, filter_weight, 1)
    normed_two, rstd_two = plain_layer_norm(spatial)
    mlp_in = (normed_two * gain_two).astype(jnp.bfloat16).reshape(-1, chans)
    preact = jnp.dot(mlp_in, weight_in, preferred_element_type=jnp.float32)
    activated = exact_gelu(preact).astype(jnp.bfloat16)
    mlp_out = jnp.dot(activated, weight_out, preferred_element_type=jnp.float32)
    block_out = (inputs + mlp_out.reshape(inputs.shape)).astype(jnp.bfloat16)
    upstream = grad_out.reshape(-1, chans)
    grad_act = jnp.dot(upstream, weight_out.T, preferred_element_type=jnp.float32)
    grad_pre = jax.vjp(exact_gelu, preact)[1](grad_act)[0].astype(jnp.bfloat16)
    sum_out = jnp.dot(activated.T, upstream, preferred_element_type=jnp.float32)
    sum_in = jnp.dot(mlp_in.T, grad_pre, preferred_element_type=jnp.float32)
    grad_mlp = jnp.dot(grad_pre, weight_in.T, preferred_element_type=jnp.float32).reshape(
        inputs.shape
    )
    grad_spatial, sum_gain_two = plain_norm_backward(grad_mlp, normed_two, rstd_two, gain_two)
    back_spatial, adjoint = spectral(grad_spatial.astype(jnp.bfloat16), filter_weight, -1)
    spec_f = spectrum.astype(jnp.float32)
    adj_f = adjoint.astype(jnp.float32)
    filter_terms = jnp.stack(
        [
            jnp.sum(adj_f[0] * spec_f[0] + adj_f[1] * spec_f[1], axis=0),
            jnp.sum(adj_f[1] * spec_f[0] - adj_f[0] * spec_f[1], axis=0),
        ]
    )
    grad_filter = lax.psum(filter_terms.astype(jnp.bfloat16), "copy").astype(jnp.float32)
    grad_normed, sum_gain_one = plain_norm_backward(back_spatial, normed_one, rstd_one, gain_one)
    grad_tokens = (grad_out.astype(jnp.float32) + grad_normed).astype(jnp.bfloat16)
    local_sums = (sum_in, sum_out, sum_gain_one, sum_gain_two)
    summed = lax.psum(
        (local_sums[0], local_sums[1], local_sums[2], local_sums[3]), ("copy", "space")
    )
    total_tokens = batch * lax.axis_size("copy") * rows_dev * lax.axis_size("space") * width
    factor = 1.0 / math.sqrt(total_tokens)
    return (
        block_out,
        grad_tokens,
        grad_filter,
        (summed[0] * factor).astype(jnp.bfloat16),
        (summed[1] * factor).astype(jnp.bfloat16),
        summed[2] * factor,
        summed[3] * factor,
    )


def solution(mesh):
    def program(*arrays):
        rows_dev, wide = arrays[0].shape[1], arrays[2].shape[2]
        n = lax.axis_size("space")
        tiled = rows_dev % 32 == 0 and wide % 32 == 0 and n & (n - 1) == 0
        return (body if tiled else plain_body)(*arrays)

    return jax.shard_map(
        program,
        mesh=mesh,
        in_specs=(
            P("copy", "space", None, None),
            P("copy", "space", None, None),
            P(None, None, "space", None),
            P(),
            P(),
            P(),
            P(),
        ),
        out_specs=(
            P("copy", "space", None, None),
            P("copy", "space", None, None),
            P(None, None, "space", None),
            P(),
            P(),
            P(),
            P(),
        ),
        check_vma=False,
    )
```

```python
import functools
import math

import jax
import jax.numpy as jnp
import ml_dtypes
import numpy as np
from jax import lax
from jax.experimental import pallas as pl
from jax.experimental.pallas import tpu as pltpu
from jax.sharding import PartitionSpec as P

EPS = 1e-06
LANES = 128
VMEM_LIMIT = 60 * 1024 * 1024
BF16 = jnp.bfloat16
F32 = jnp.float32


def dft_pair(length):
    index = np.arange(length, dtype=np.int64)
    angle = (index[:, None] * index[None, :] % length) * (2.0 * math.pi / length)
    factor = 1.0 / math.sqrt(length)
    rounded = lambda a: a.astype(np.float32).astype(ml_dtypes.bfloat16).astype(np.float32)
    return rounded(np.cos(angle) * factor), rounded(np.sin(angle) * factor)


def row_tables(width, n):
    cosine, sine = dft_pair(width)
    own = width // n
    half = own // 2
    forward = np.zeros((n, 2, half, width), np.float32)
    weight = np.full((n, 2, half, 1), 2.0, np.float32)
    for d in range(n):
        first = own * d + (1 if d >= n // 2 else 0)
        forward[d, 0] = cosine[first : first + half]
        forward[d, 1] = -sine[first : first + half]
    forward[0, 1, 0] = cosine[width // 2]
    weight[0, :, 0] = 1.0
    shape = (n, 2 * half, width)
    return (
        forward.reshape(shape).astype(ml_dtypes.bfloat16),
        (forward * weight).reshape(shape).astype(ml_dtypes.bfloat16),
    )


def column_tables(height, n, chunks):
    cosine, sine = dft_pair(height)
    zero = np.zeros_like(cosine)
    rows = height // n // chunks

    def arrange(blocks):
        full = np.stack([np.stack(line, axis=1) for line in blocks])
        full = full.reshape(2 * height, 2, n, chunks, rows)
        return full.transpose(0, 3, 2, 1, 4).reshape(2 * height, 2 * height)

    middle = arrange([[zero, cosine], [zero, -sine]])
    first = arrange([[cosine, zero], [-sine, zero]])
    other = arrange([[cosine, sine], [-sine, cosine]])
    backward = np.stack([middle, first, other]).transpose(0, 2, 1)
    backward = backward.reshape(3, chunks, n, 2 * rows, 2 * height)
    return backward.astype(ml_dtypes.bfloat16)


def mirror_table(height):
    table = np.zeros((height, height), np.float32)
    table[np.arange(height), (-np.arange(height)) % height] = 1.0
    return table.astype(ml_dtypes.bfloat16)


def dot(a, b):
    return jnp.dot(a, b, preferred_element_type=F32)


def dot_tn(a, b):
    return lax.dot_general(a, b, (((0,), (0,)), ((), ())), preferred_element_type=F32)


def normalize(values):
    centred = values - jnp.mean(values, axis=-1, keepdims=True)
    variance = jnp.mean(centred * centred, axis=-1, keepdims=True)
    rstd = lax.rsqrt(variance + EPS)
    return centred * rstd, rstd


def norm_backward(upstream, normed, rstd, gain):
    scaled = upstream * gain
    return (
        scaled
        - jnp.mean(scaled, axis=-1, keepdims=True)
        - normed * jnp.mean(scaled * normed, axis=-1, keepdims=True)
    ) * rstd


def gelu_and_slope(v):
    e = jnp.exp(v * v * -0.5)
    d = 1.0 + (0.3275911 / math.sqrt(2.0)) * jnp.abs(v)
    t = pl.reciprocal(d, approx=True)
    t = t * (2.0 - d * t)
    poly = 0.5 * 1.061405429
    for coefficient in (-1.453152027, 1.421413741, -0.284496736, 0.254829592):
        poly = poly * t + 0.5 * coefficient
    tail = poly * t * e
    phi = jnp.where(v < 0.0, tail, 1.0 - tail)
    return v * phi, phi + v * e * (1.0 / math.sqrt(2.0 * math.pi))


def spaced(count):
    groups = -(-count // 8)
    return 8 * (groups + 1 - groups % 2)


def lanes(c):
    return slice(c * LANES, (c + 1) * LANES)


def unpack(received, scratch):
    count, rows, chans = received[0].shape
    pitch = spaced(rows)

    def step(k, carry):
        for s, ref in enumerate(received):
            start = pl.multiple_of((s * count + k) * pitch, 8)
            for c in range(chans // LANES):
                scratch[c, pl.ds(start, rows), :] = ref[k, :, lanes(c)].astype(F32)
        return carry

    lax.fori_loop(0, count, step, 0, unroll=2)


def read_row(scratch, row, columns, rows):
    parts = [
        scratch[c, pl.ds(row, columns, stride=spaced(rows)), :].astype(BF16)
        for c in range(scratch.shape[0])
    ]
    return jnp.concatenate(parts, axis=1)


def write_row(scratch, row, columns, values):
    start = pl.multiple_of(row * spaced(columns), 8)
    for c in range(scratch.shape[0]):
        scratch[c, pl.ds(start, columns), :] = values[:, lanes(c)]


def pack(scratch, columns, outgoing):
    count, rows, _ = outgoing[0].shape

    def step(k, carry):
        for s, ref in enumerate(outgoing):
            for c in range(scratch.shape[0]):
                part = scratch[c, pl.ds(s * count + k, rows, stride=spaced(columns)), :]
                ref[k, :, lanes(c)] = part.astype(BF16)
        return carry

    lax.fori_loop(0, count, step, 0, unroll=2)


def params():
    return pltpu.CompilerParams(vmem_limit_bytes=VMEM_LIMIT)


def resident(shape):
    return pl.BlockSpec(shape, lambda *_: (0,) * len(shape), pipeline_mode=pl.Buffered(1))


ANYWHERE = pl.BlockSpec(memory_space=pl.ANY)


def cost(flops, size):
    return pl.CostEstimate(flops=int(flops), bytes_accessed=int(size), transcendentals=0)


def shape_of(shape, dtype=BF16):
    return jax.ShapeDtypeStruct(tuple(shape), dtype)


def hold(value, after):
    return pl.pallas_call(
        lambda *refs: None,
        in_specs=[ANYWHERE] * (1 + len(after)),
        out_specs=ANYWHERE,
        out_shape=shape_of(value.shape, value.dtype),
        input_output_aliases={0: 0},
        compiler_params=params(),
        cost_estimate=cost(0, 0),
        name="hold",
    )(value, *after)


def enter_kernel(tokens, gain, table, *rest):
    outgoing, scratch = rest[-2:-1], rest[-1]
    step = pl.program_id(0)
    block, width, _ = tokens.shape
    for r in range(block):
        normed, _ = normalize(tokens[r].astype(F32))
        mixed = (normed * gain[...]).astype(BF16)
        write_row(scratch, step * block + r, width, dot(table[...], mixed))

    @pl.when(step == pl.num_programs(0) - 1)
    def _():
        pack(scratch, width, outgoing)


def enter(tokens, gain, table, block):
    rows, width, chans = tokens.shape
    steps = rows // block
    out = (width, rows, chans)
    return pl.pallas_call(
        enter_kernel,
        grid=(steps,),
        in_specs=[
            pl.BlockSpec((block, width, chans), lambda i: (i, 0, 0)),
            resident((1, chans)),
            resident((width, width)),
        ],
        out_specs=resident(out),
        out_shape=shape_of(out),
        scratch_shapes=[pltpu.VMEM((chans // LANES, rows * spaced(width), LANES), F32)],
        compiler_params=params(),
        cost_estimate=cost(2 * rows * width * width * chans, 4 * rows * width * chans),
        name="enter_rows",
    )(tokens, gain, table)


def mlp_kernel(
    n, later, tokens, upstream, gain, table_out, table_in, w_in, w_out, w_in_t, w_out_t, *rest
):
    received, rest = rest[:n], rest[n:]
    if later:
        (_, *before), rest = rest[:4], rest[4:]
    block_out, outgoing, rest = rest[0], rest[1 : n + 1], rest[n + 1 :]
    sum_in, sum_out, sum_gain, unpacked, packed = rest
    step = pl.program_id(0)
    block, width, chans = tokens.shape
    rows = received[0].shape[1]
    hidden = w_in.shape[1]
    part = min(512, hidden)

    @pl.when(step == 0)
    def _():
        unpack(received, unpacked)
        for i, ref in enumerate((sum_in, sum_out, sum_gain)):
            ref[...] = before[i][...] if later else jnp.zeros_like(ref)

    spatial = jnp.concatenate(
        [
            dot(table_out[...], read_row(unpacked, step * block + r, width, rows))
            for r in range(block)
        ],
        axis=0,
    )
    normed, rstd = normalize(spatial)
    mlp_in = (normed * gain[...]).astype(BF16)
    grad = upstream[...].reshape(block * width, chans)
    out = tokens[...].reshape(block * width, chans).astype(F32)
    grad_mlp = jnp.zeros_like(spatial)

    def first(cols):
        return dot(mlp_in, w_in[:, cols]), dot(grad, w_out_t[:, cols])

    parts = [slice(f, f + part) for f in range(0, hidden, part)]
    ahead = first(parts[0])
    for f, cols in enumerate(parts):
        preact, grad_act = ahead
        if f + 1 < len(parts):
            ahead = first(parts[f + 1])
        value, slope = gelu_and_slope(preact)
        activated = value.astype(BF16)
        grad_pre = (grad_act * slope).astype(BF16)
        out = out + dot(activated, w_out[cols, :])
        grad_mlp = grad_mlp + dot(grad_pre, w_in_t[cols, :])
        sum_out[:, cols] += dot_tn(grad, activated)
        sum_in[:, cols] += dot_tn(mlp_in, grad_pre)
    block_out[...] = out.astype(BF16).reshape(block, width, chans)
    grad_spatial = norm_backward(grad_mlp, normed, rstd, gain[...])
    sum_gain[0:8] += jnp.sum((grad_mlp * normed).reshape(-1, 8, chans), axis=0)
    sum_gain[8:16] += jnp.sum((grad_spatial * spatial).reshape(-1, 8, chans), axis=0)
    sent = grad_spatial.astype(BF16)
    for r in range(block):
        values = dot(table_in[...], sent[r * width : (r + 1) * width])
        write_row(packed, step * block + r, width, values)

    @pl.when(step == pl.num_programs(0) - 1)
    def _():
        pack(packed, width, outgoing)


def mlp(received, tokens, upstream, gain, tables, weights, previous, chunk, block):
    n = len(received)
    count, rows, chans = received[0].shape
    width = tokens.shape[1]
    hidden = weights[0].shape[1]
    steps = rows // block
    by_rows = pl.BlockSpec((block, width, chans), lambda i: (i + chunk * steps, 0, 0))
    operands = [tokens, upstream, gain, *tables, *weights, *received]
    in_specs = [
        by_rows,
        by_rows,
        resident((1, chans)),
        resident((width, width)),
        resident((width, width)),
        resident((chans, hidden)),
        resident((hidden, chans)),
        resident((hidden, chans)),
        resident((chans, hidden)),
    ] + [resident((count, rows, chans))] * n
    aliases = {}
    if previous is not None:
        aliases = {len(operands): 0}
        operands += previous
        in_specs += [ANYWHERE] + [resident(p.shape) for p in previous[1:]]
    flops = 2 * rows * width * chans * (6 * hidden + 2 * width)
    outputs = pl.pallas_call(
        functools.partial(mlp_kernel, n, previous is not None),
        grid=(steps,),
        in_specs=in_specs,
        out_specs=[by_rows]
        + [resident((count, rows, chans))] * n
        + [resident((chans, hidden)), resident((chans, hidden)), resident((16, chans))],
        out_shape=[shape_of(tokens.shape)]
        + [shape_of((count, rows, chans))] * n
        + [shape_of((chans, hidden), F32)] * 2
        + [shape_of((16, chans), F32)],
        scratch_shapes=[
            pltpu.VMEM((chans // LANES, width * spaced(rows), LANES), F32),
            pltpu.VMEM((chans // LANES, rows * spaced(width), LANES), F32),
        ],
        input_output_aliases=aliases,
        compiler_params=params(),
        cost_estimate=cost(flops, 10 * rows * width * chans),
        name="mlp_rows",
    )(*operands)
    return outputs[0], outputs[1 : n + 1], outputs[n + 1 :]


def leave_kernel(n, tokens, upstream, gain, table_out, *rest):
    received, (grad_tokens, unpacked) = rest[:n], rest[-2:]
    step = pl.program_id(0)
    block, width, _ = tokens.shape
    rows = received[0].shape[1]

    @pl.when(step == 0)
    def _():
        unpack(received, unpacked)

    for r in range(block):
        back = dot(table_out[...], read_row(unpacked, step * block + r, width, rows))
        normed, rstd = normalize(tokens[r].astype(F32))
        grad = norm_backward(back, normed, rstd, gain[...])
        grad_tokens[r] = (upstream[r].astype(F32) + grad).astype(BF16)


def leave(received, tokens, upstream, gain, table_out, previous, chunk, block, after):
    n = len(received)
    count, rows, chans = received[0].shape
    width = tokens.shape[1]
    steps = rows // block
    by_rows = pl.BlockSpec((block, width, chans), lambda i: (i + chunk * steps, 0, 0))
    operands = [tokens, upstream, gain, table_out, *received]
    in_specs = [by_rows, by_rows, resident((1, chans)), resident((width, width))]
    in_specs += [resident((count, rows, chans))] * n
    aliases = {}
    if previous is not None:
        aliases = {len(operands): 0}
        operands.append(previous)
        in_specs.append(ANYWHERE)
    operands += after
    in_specs += [ANYWHERE] * len(after)
    return pl.pallas_call(
        functools.partial(leave_kernel, n),
        grid=(steps,),
        in_specs=in_specs,
        out_specs=by_rows,
        out_shape=shape_of(tokens.shape),
        scratch_shapes=[pltpu.VMEM((chans // LANES, width * spaced(rows), LANES), F32)],
        input_output_aliases=aliases,
        compiler_params=params(),
        cost_estimate=cost(2 * rows * width * width * chans, 8 * rows * width * chans),
        name="leave_rows",
    )(*operands)


def columns_kernel(count, outs, back, flags, table_f, table_b, kernel, *rest):
    spectrum, rest = (rest[0], rest[1:]) if back else (None, rest)
    received, (*outgoing, held) = rest[:count], rest[-outs - 1 :]
    step, last = pl.program_id(0), pl.num_programs(0) - 1
    per, _, height, chans = kernel.shape

    def load(j):
        return jnp.concatenate([ref[:, :, j].reshape(-1, chans) for ref in received], axis=0)

    def store(j, values):
        values = values.astype(BF16)
        size = values.shape[0] // len(outgoing)
        for i, ref in enumerate(outgoing):
            n, _, _, rows, _ = ref.shape
            ref[:, :, j] = values[i * size : (i + 1) * size].reshape(n, 2, rows, chans)

    def filtered(slot, found):
        found = found.astype(BF16)
        real, imag = found[:height].astype(F32), found[height:].astype(F32)
        k_real, k_imag = kernel[slot, 0].astype(F32), kernel[slot, 1].astype(F32)
        if back:
            s_real, s_imag = spectrum[slot, 0].astype(F32), spectrum[slot, 1].astype(F32)
            held[slot, 0] = (real * s_real + imag * s_imag).astype(BF16)
            held[slot, 1] = (imag * s_real - real * s_imag).astype(BF16)
            k_imag = -k_imag
        else:
            held[slot, 0] = found[:height]
            held[slot, 1] = found[height:]
        upper = (k_real * real - k_imag * imag).astype(BF16)
        lower = (k_real * imag + k_imag * real).astype(BF16)
        return jnp.concatenate([upper, lower], axis=0)

    @pl.when(step < last)
    def _():
        at = [1 + step * per + i for i in range(per)]
        found = dot(table_f[2], jnp.concatenate([load(j) for j in at], axis=1))
        weighted = [filtered(i, found[:, i * chans : (i + 1) * chans]) for i in range(per)]
        result = dot(table_b[2], jnp.concatenate(weighted, axis=1))
        for i, j in enumerate(at):
            store(j, result[:, i * chans : (i + 1) * chans])

    @pl.when(step == last)
    def _():
        values = load(0)
        kind = 2 - flags[1]
        zero = filtered(0, dot(table_f[kind], values))
        middle = filtered(1, dot(table_f[0], values))
        store(0, dot(table_b[kind], zero) + dot(table_b[0], middle))
        for i in range(2, per):
            held[i] = jnp.zeros_like(held[i])


def columns(flags, tables, kernel, received, outs, spectrum=None, after=()):
    count = len(received)
    n, _, half, rows, chans = received[0].shape
    sent = (n, 2, half, count * rows // outs, chans)
    slots, _, height, _ = kernel.shape
    per = columns_per_step(half)
    held = pl.BlockSpec((per, 2, height, chans), lambda t, flags: (t, 0, 0, 0))
    table = resident((3, 2 * height, 2 * height))
    back = spectrum is not None
    outputs = pl.pallas_call(
        functools.partial(columns_kernel, count, outs, back),
        grid_spec=pltpu.PrefetchScalarGridSpec(
            num_scalar_prefetch=1,
            grid=(slots // per,),
            in_specs=[table, table, held]
            + [held] * back
            + [resident(r.shape) for r in received]
            + [ANYWHERE] * len(after),
            out_specs=[resident(sent)] * outs + [held],
        ),
        out_shape=[shape_of(sent)] * outs + [shape_of(kernel.shape)],
        compiler_params=params(),
        cost_estimate=cost(16 * height * height * chans * slots, 20 * height * chans * slots),
        name="filter_columns",
    )(flags, *tables, kernel, *([spectrum] if back else []), *received, *after)
    return outputs[:outs], outputs[outs]


def columns_per_step(half):
    return 3 if (half - 1) % 3 == 0 else 2 if (half - 1) % 2 == 0 else 1


def slot_count(half):
    per = max(2, columns_per_step(half))
    return half - 1 + per


def filter_part_kernel(copies, flags, mirror, own, *rest):
    mains, extras = rest[:copies], rest[copies : 2 * copies]
    kernel, scr_own, scr_main, scr_extra = rest[-4:]
    part = pl.program_id(0)
    upper, first, me = flags[0], flags[1], flags[2]
    _, height, wide, _ = own.shape
    half = wide // 2
    share = height // copies
    pitch_own, pitch = spaced(wide), spaced(half)

    def spread_own(m, carry):
        scr_own[pl.ds(pl.multiple_of(m * pitch_own, 8), wide), :] = own[0, m].astype(F32)
        return carry

    lax.fori_loop(0, height, spread_own, 0, unroll=8)
    for i in range(copies):
        owner = jnp.bitwise_xor(me, i)

        def spread_main(m, carry):
            at = pl.multiple_of((owner * share + m) * pitch, 8)
            scr_main[pl.ds(at, half), :] = mains[i][0, m].astype(F32)
            return carry

        lax.fori_loop(0, share, spread_main, 0, unroll=8)
        at = pl.multiple_of(owner * share, share)
        scr_extra[pl.ds(at, share), :] = extras[i][0].astype(F32)
    sign = jnp.where(part == 0, 0.5, -0.5)
    extra = scr_extra[...]
    middle = 0.5 * extra + sign * dot(mirror[...], extra.astype(BF16))
    kernel[half, 0] = jnp.where(first == 1, middle, 0.0).astype(BF16)
    for i in range(half + 1, kernel.shape[0]):
        kernel[i, 0] = jnp.zeros((height, LANES), BF16)
    for j in range(half):
        mine = scr_own[pl.ds(j + upper, height, stride=pitch_own), :]
        if j == 0:
            other = scr_main[pl.ds(half - 1, height, stride=pitch), :]
            lower = jnp.where(first == 1, mine, extra)
            other = jnp.where(upper == 1, other, lower)
        else:
            other = scr_main[pl.ds(half - j - upper, height, stride=pitch), :]
        turned = dot(mirror[...], other.astype(BF16))
        kernel[(j - 1) % half, 0] = (0.5 * mine + sign * turned).astype(BF16)


def filter_part(flags, mirror, own, mains, extras, after):
    _, height, wide, chans = own.shape
    copies = len(mains)
    half, share = wide // 2, height // copies
    slots = slot_count(half)
    return pl.pallas_call(
        functools.partial(filter_part_kernel, copies),
        grid_spec=pltpu.PrefetchScalarGridSpec(
            num_scalar_prefetch=1,
            grid=(2, chans // LANES),
            in_specs=[
                pl.BlockSpec((height, height), lambda p, c, flags: (0, 0)),
                pl.BlockSpec((1, height, wide, LANES), lambda p, c, flags: (p, 0, 0, c)),
            ]
            + [pl.BlockSpec((1, share, half, LANES), lambda p, c, flags: (p, 0, 0, c))] * copies
            + [pl.BlockSpec((1, share, LANES), lambda p, c, flags: (p, 0, c))] * copies
            + [ANYWHERE] * len(after),
            out_specs=pl.BlockSpec((slots, 1, height, LANES), lambda p, c, flags: (0, p, 0, c)),
            scratch_shapes=[
                pltpu.VMEM((height * spaced(wide), LANES), F32),
                pltpu.VMEM((height * spaced(half), LANES), F32),
                pltpu.VMEM((height, LANES), F32),
            ],
        ),
        out_shape=shape_of((slots, 2, height, chans)),
        compiler_params=params(),
        cost_estimate=cost(4 * height * height * chans * half, 16 * height * half * chans),
        name="filter_part",
    )(flags, mirror, own, *mains, *extras, *after)


def filter_gradient_kernel(copies, flags, mirror, *rest):
    mine, theirs = rest[:copies], rest[copies : 2 * copies]
    out, gathered, turned = rest[-3:]
    part = pl.program_id(0)
    upper, me = flags[0], flags[2]
    _, height, wide, _ = out.shape
    half = wide // 2
    share = height // copies
    pitch = spaced(height)
    for i in range(copies):
        at = pl.multiple_of(jnp.bitwise_xor(me, i) * share, share)
        gathered[0:half, pl.ds(at, share), :] = mine[i][:, 0]
        gathered[half:, pl.ds(at, share), :] = theirs[i][:, 0]
    sign = jnp.where(part == 0, 1.0, -1.0)
    for k in range(wide):
        if k == 0:
            index = jnp.where(upper == 1, 2 * half, half - 1)
        elif k < half:
            index = k - 1 - upper
            index = jnp.where(index < 0, half - 1, index)
        elif k == half:
            index = jnp.where(upper == 1, half - 2, 2 * half - 2)
        else:
            index = wide - 2 - k + upper
            index = half + jnp.where(index < 0, half - 1, index)
        value = gathered[index]
        if 0 < k < half:
            value = value.astype(F32)
        else:
            other = sign * dot(mirror[...], value)
            if k == 0:
                other = jnp.where(upper == 1, other, value.astype(F32))
            elif k == half:
                other = jnp.where(upper == 1, value.astype(F32), other)
            value = other
        turned[pl.ds(k * pitch, height), :] = value

    def step(m, carry):
        out[0, m] = turned[pl.ds(m, wide, stride=pitch), :]
        return carry

    lax.fori_loop(0, height, step, 0, unroll=8)


def filter_gradient(flags, mirror, mine, theirs, height, wide, after):
    _, _, share, chans = mine[0].shape
    copies, half = len(mine), wide // 2
    block = lambda slots: pl.BlockSpec(
        (slots, 1, share, LANES), lambda p, c, flags: (0, p, 0, c)
    )
    return pl.pallas_call(
        functools.partial(filter_gradient_kernel, copies),
        grid_spec=pltpu.PrefetchScalarGridSpec(
            num_scalar_prefetch=1,
            grid=(2, chans // LANES),
            in_specs=[pl.BlockSpec((height, height), lambda p, c, flags: (0, 0))]
            + [block(half)] * copies
            + [block(half + 1)] * copies
            + [ANYWHERE] * len(after),
            out_specs=pl.BlockSpec((1, height, wide, LANES), lambda p, c, flags: (p, 0, 0, c)),
            scratch_shapes=[
                pltpu.VMEM((wide + 1, height, LANES), BF16),
                pltpu.VMEM((wide * spaced(height), LANES), F32),
            ],
        ),
        out_shape=shape_of((2, height, wide, chans), F32),
        compiler_params=params(),
        cost_estimate=cost(2 * height * height * chans * wide, 12 * height * wide * chans),
        name="filter_gradient",
    )(flags, mirror, *mine, *theirs, *after)


def swap(value, axis, size, partner):
    return lax.ppermute(value, axis, [(i, partner(i)) for i in range(size)])


def swap_bits(value, axis, size, bits):
    return swap(value, axis, size, lambda i: i ^ bits)


def exchange(value):
    return lax.all_to_all(value, "space", split_axis=0, concat_axis=0, tiled=True)


def exchange_after(value, after):
    return exchange(hold(value, tuple(after)) if after else value)


def gather_copies(value, copies):
    parts = {0: value}
    bit = copies // 2
    while bit:
        for key in list(parts):
            parts[key ^ bit] = swap_bits(parts[key], "copy", copies, bit)
        bit //= 2
    return [parts[i] for i in range(copies)]


def reduce_shares(value, axes, extra=None):
    places, place = [], 0
    for name in axes:
        digits = lax.axis_size(name).bit_length() - 1
        places += [(name, bit, place + digits - 1 - bit) for bit in range(digits)]
        place += digits
    for name, bit, place in places:
        size, own = lax.axis_size(name), (lax.axis_index(name) >> bit) & 1
        kept = lax.dynamic_index_in_dim(value, own, place, keepdims=True)
        sent = lax.dynamic_index_in_dim(value, 1 - own, place, keepdims=True)
        other = swap_bits(sent, name, size, 1 << bit)
        value = (kept.astype(F32) + other.astype(F32)).astype(value.dtype)
        if extra is not None:
            extra = extra + swap_bits(extra, name, size, 1 << bit)
    return value, extra


def body(noisy_tokens, grad_out, filter_weight, weight_in, weight_out, gain_one, gain_two):
    _, rows_dev, width, chans = noisy_tokens.shape
    height, wide = filter_weight.shape[1:3]
    digits = (2,) * (lax.axis_size("copy").bit_length() - 1)
    hidden = weight_in.shape[1]
    half = wide // 2
    n, copies = lax.axis_size("space"), lax.axis_size("copy")
    chunks = 2
    rows = rows_dev // chunks
    tokens, upstream = noisy_tokens[0], grad_out[0]
    me, copy = lax.axis_index("space"), lax.axis_index("copy")

    share = height // copies
    at = copy * share
    opposite = lambda d: n - 1 - d
    main = lax.dynamic_slice(filter_weight, (0, at, half, 0), (2, share, half, chans))
    main = swap(main, "space", n, opposite)
    to_lower = [(n // 2, 0)] + [(e, n - e) for e in range(n // 2 + 1, n)]
    single = lax.dynamic_slice(filter_weight, (0, at, 0, 0), (2, share, 1, chans))
    single = lax.ppermute(single.reshape(2, share, chans), "space", to_lower)

    forward, weighted = row_tables(width, n)
    table_in = jnp.asarray(forward.reshape(width, width))
    table_out = jnp.asarray(np.ascontiguousarray(weighted.reshape(width, width).T))
    whole, cut = (
        column_tables(height, n, c).reshape(3, 2 * height, 2 * height) for c in (1, chunks)
    )
    forward_in, backward_in = (
        jnp.asarray(np.ascontiguousarray(t.transpose(0, 2, 1))) for t in (whole, cut)
    )
    out_tabs = jnp.asarray(cut)
    mirror = jnp.asarray(mirror_table(height))
    gain_a, gain_b = gain_one.reshape(1, chans), gain_two.reshape(1, chans)
    upper = (me >= n // 2).astype(jnp.int32)
    first = (me == 0).astype(jnp.int32)

    def flags(index):
        return jnp.stack([upper, first, index.astype(jnp.int32)])

    def split(value):
        return value.reshape(n, 2, half, -1, chans)

    def join(value):
        return value.reshape(width, -1, chans)

    entered = hold(enter(tokens, gain_a, table_in, 2), (main, single))
    arrived = [split(exchange(entered))]
    mains, singles = gather_copies(main, copies), gather_copies(single, copies)
    weights = (weight_in, weight_out, weight_in.T, weight_out.T)
    kernel = filter_part(flags(copy), mirror, filter_weight, mains, singles, weights[2:])
    returned, spectrum = columns(flags(copy), (forward_in, out_tabs), kernel, arrived, chunks)

    tables = (table_out, table_in)
    received, arrived = [], []
    for r in returned:
        received.append(exchange_after(join(r), received))
    previous = None
    for c in range(chunks):
        block_out, sent, sums = mlp(
            [received[c]], tokens, upstream, gain_b, tables, weights, previous, c, 4
        )
        arrived.append(exchange_after(sent[0], arrived))
        previous = [block_out, *sums]

    axes = ("copy", "space")
    sum_in, sum_out, sum_gain = sums
    both = jnp.concatenate([sum_in, sum_out], axis=0).astype(BF16)
    both = both.reshape((2,) * ((copies * n).bit_length() - 1) + (-1, hidden))
    gains = jnp.stack([jnp.sum(sum_gain[8:], axis=0) / gain_one, jnp.sum(sum_gain[:8], axis=0)])
    part, gains = reduce_shares(both, axes, gains)
    factor = 1.0 / math.sqrt(copies * rows_dev * n * width)
    part = (part.reshape(-1, hidden).astype(F32) * factor).astype(BF16)
    gains = gains * factor

    returned, terms = columns(
        flags(copy), (backward_in, out_tabs), kernel, [split(a) for a in arrived], chunks, spectrum, (part, gains)
    )
    grads = lax.all_gather(part, axes, tiled=True)
    received = exchange(join(returned[0]))
    grad_tokens = leave(
        [received], tokens, upstream, gain_a, table_out, None, 0, 2, (grads,)
    )

    terms = terms.reshape(terms.shape[:2] + digits + (share, chans))
    terms = jnp.moveaxis(terms, range(2, 2 + len(digits)), range(len(digits)))
    reduced, _ = reduce_shares(terms, ("copy",))
    reduced = reduced.reshape(-1, 2, share, chans)
    mirrored = swap(reduced[:half], "space", n, opposite)
    to_upper = [(0, n // 2)] + [(d, n - d) for d in range(1, n // 2)]
    single = lax.ppermute(
        jnp.where(me == 0, reduced[half], reduced[half - 1]), "space", to_upper
    )
    mine = gather_copies(reduced[:half], copies)
    received = exchange(hold(join(returned[1]), (mirrored, single, *mine, grad_tokens)))
    theirs = gather_copies(jnp.concatenate([mirrored, single[None]], axis=0), copies)
    grad_filter = filter_gradient(
        flags(copy), mirror, mine, theirs, height, wide, ()
    )
    grad_tokens = leave(
        [received], tokens, upstream, gain_a, table_out, grad_tokens, 1, 2, (grad_filter,)
    )
    return (
        block_out[None],
        grad_tokens[None],
        grad_filter,
        grads[:chans],
        grads[chans:].T,
        gains[0],
        gains[1],
    )


def dft_parts(length):
    index = jnp.arange(length, dtype=jnp.int32)
    phase = index[:, None] * index[None, :] % length
    angle = phase.astype(jnp.float32) * (2.0 * math.pi / length)
    factor = 1.0 / math.sqrt(length)
    return (
        (jnp.cos(angle) * factor).astype(jnp.bfloat16),
        (jnp.sin(angle) * factor).astype(jnp.bfloat16),
    )


def row_table(length):
    cosine, sine = dft_parts(length)
    return jnp.stack([cosine, -sine])


def column_table(length, direction):
    cosine, sine = dft_parts(length)
    upper = jnp.stack([cosine, direction * sine], axis=1)
    lower = jnp.stack([-direction * sine, cosine], axis=1)
    return jnp.stack([upper, lower])


def plain_layer_norm(values):
    centre = jnp.mean(values, axis=-1, keepdims=True)
    centred = values - centre
    variance = jnp.mean(centred * centred, axis=-1, keepdims=True)
    rstd_value = lax.rsqrt(variance + EPS)
    return (centred * rstd_value, rstd_value)


def plain_norm_backward(upstream, normed, rstd_value, gain):
    scaled = upstream * gain
    result = (
        scaled
        - jnp.mean(scaled, axis=-1, keepdims=True)
        - normed * jnp.mean(scaled * normed, axis=-1, keepdims=True)
    ) * rstd_value
    lead = tuple(range(upstream.ndim - 1))
    return (result, jnp.sum(upstream * normed, axis=lead))


def apply_filter(spectrum, filter_weight, direction):
    real_part = spectrum[0].astype(jnp.float32)
    imag_part = spectrum[1].astype(jnp.float32)
    kernel_real = filter_weight[0].astype(jnp.float32)
    kernel_imag = direction * filter_weight[1].astype(jnp.float32)
    return jnp.stack(
        [
            kernel_real * real_part - kernel_imag * imag_part,
            kernel_real * imag_part + kernel_imag * real_part,
        ]
    )


def exact_gelu(values):
    return jax.nn.gelu(values, approximate=False)


def spectral(values, filter_weight, direction):
    width = values.shape[2]
    rows_tab = row_table(width)
    rows = jnp.einsum(
        "pkw,bhwc->pbhkc", rows_tab, values, preferred_element_type=jnp.float32
    ).astype(jnp.bfloat16)
    columns = lax.all_to_all(rows, "space", split_axis=3, concat_axis=2, tiled=True)
    height = columns.shape[2]
    spectrum = jnp.einsum(
        "qmph,pbhkc->qbmkc", column_table(height, 1), columns, preferred_element_type=jnp.float32
    ).astype(jnp.bfloat16)
    weighted = apply_filter(spectrum, filter_weight[:, None], direction).astype(jnp.bfloat16)
    returned = jnp.einsum(
        "qmph,pbhkc->qbmkc", column_table(height, -1), weighted, preferred_element_type=jnp.float32
    ).astype(jnp.bfloat16)
    back_rows = lax.all_to_all(returned, "space", split_axis=2, concat_axis=3, tiled=True)
    output = jnp.einsum("pkw,pbhkc->bhwc", rows_tab, back_rows, preferred_element_type=jnp.float32)
    return (output, spectrum)


def plain_body(noisy_tokens, grad_out, filter_weight, weight_in, weight_out, gain_one, gain_two):
    batch, rows_dev, width, chans = noisy_tokens.shape
    inputs = noisy_tokens.astype(jnp.float32)
    normed_one, rstd_one = plain_layer_norm(inputs)
    mixed_in = (normed_one * gain_one).astype(jnp.bfloat16)
    spatial, spectrum = spectral(mixed_in, filter_weight, 1)
    normed_two, rstd_two = plain_layer_norm(spatial)
    mlp_in = (normed_two * gain_two).astype(jnp.bfloat16).reshape(-1, chans)
    preact = jnp.dot(mlp_in, weight_in, preferred_element_type=jnp.float32)
    activated = exact_gelu(preact).astype(jnp.bfloat16)
    mlp_out = jnp.dot(activated, weight_out, preferred_element_type=jnp.float32)
    block_out = (inputs + mlp_out.reshape(inputs.shape)).astype(jnp.bfloat16)
    upstream = grad_out.reshape(-1, chans)
    grad_act = jnp.dot(upstream, weight_out.T, preferred_element_type=jnp.float32)
    grad_pre = jax.vjp(exact_gelu, preact)[1](grad_act)[0].astype(jnp.bfloat16)
    sum_out = jnp.dot(activated.T, upstream, preferred_element_type=jnp.float32)
    sum_in = jnp.dot(mlp_in.T, grad_pre, preferred_element_type=jnp.float32)
    grad_mlp = jnp.dot(grad_pre, weight_in.T, preferred_element_type=jnp.float32).reshape(
        inputs.shape
    )
    grad_spatial, sum_gain_two = plain_norm_backward(grad_mlp, normed_two, rstd_two, gain_two)
    back_spatial, adjoint = spectral(grad_spatial.astype(jnp.bfloat16), filter_weight, -1)
    spec_f = spectrum.astype(jnp.float32)
    adj_f = adjoint.astype(jnp.float32)
    filter_terms = jnp.stack(
        [
            jnp.sum(adj_f[0] * spec_f[0] + adj_f[1] * spec_f[1], axis=0),
            jnp.sum(adj_f[1] * spec_f[0] - adj_f[0] * spec_f[1], axis=0),
        ]
    )
    grad_filter = lax.psum(filter_terms.astype(jnp.bfloat16), "copy").astype(jnp.float32)
    grad_normed, sum_gain_one = plain_norm_backward(back_spatial, normed_one, rstd_one, gain_one)
    grad_tokens = (grad_out.astype(jnp.float32) + grad_normed).astype(jnp.bfloat16)
    local_sums = (sum_in, sum_out, sum_gain_one, sum_gain_two)
    summed = lax.psum(
        (local_sums[0], local_sums[1], local_sums[2], local_sums[3]), ("copy", "space")
    )
    total_tokens = batch * lax.axis_size("copy") * rows_dev * lax.axis_size("space") * width
    factor = 1.0 / math.sqrt(total_tokens)
    return (
        block_out,
        grad_tokens,
        grad_filter,
        (summed[0] * factor).astype(jnp.bfloat16),
        (summed[1] * factor).astype(jnp.bfloat16),
        summed[2] * factor,
        summed[3] * factor,
    )


def solution(mesh):
    def program(*arrays):
        rows_dev, wide = arrays[0].shape[1], arrays[2].shape[2]
        n = lax.axis_size("space")
        tiled = rows_dev % 32 == 0 and wide % 32 == 0 and n & (n - 1) == 0
        return (body if tiled else plain_body)(*arrays)

    return jax.shard_map(
        program,
        mesh=mesh,
        in_specs=(
            P("copy", "space", None, None),
            P("copy", "space", None, None),
            P(None, None, "space", None),
            P(),
            P(),
            P(),
            P(),
        ),
        out_specs=(
            P("copy", "space", None, None),
            P("copy", "space", None, None),
            P(None, None, "space", None),
            P(),
            P(),
            P(),
            P(),
        ),
        check_vma=False,
    )
```

```python
import functools
import math

import jax
import jax.numpy as jnp
import ml_dtypes
import numpy as np
from jax import lax
from jax.experimental import pallas as pl
from jax.experimental.pallas import tpu as pltpu
from jax.sharding import PartitionSpec as P

EPS = 1e-06
LANES = 128
VMEM_LIMIT = 60 * 1024 * 1024
BF16 = jnp.bfloat16
F32 = jnp.float32


def dft_pair(length):
    index = np.arange(length, dtype=np.int64)
    angle = (index[:, None] * index[None, :] % length) * (2.0 * math.pi / length)
    factor = 1.0 / math.sqrt(length)
    rounded = lambda a: a.astype(np.float32).astype(ml_dtypes.bfloat16).astype(np.float32)
    return rounded(np.cos(angle) * factor), rounded(np.sin(angle) * factor)


def row_tables(width, n):
    cosine, sine = dft_pair(width)
    own = width // n
    half = own // 2
    forward = np.zeros((n, 2, half, width), np.float32)
    weight = np.full((n, 2, half, 1), 2.0, np.float32)
    for d in range(n):
        first = own * d + (1 if d >= n // 2 else 0)
        forward[d, 0] = cosine[first : first + half]
        forward[d, 1] = -sine[first : first + half]
    forward[0, 1, 0] = cosine[width // 2]
    weight[0, :, 0] = 1.0
    shape = (n, 2 * half, width)
    return (
        forward.reshape(shape).astype(ml_dtypes.bfloat16),
        (forward * weight).reshape(shape).astype(ml_dtypes.bfloat16),
    )


def column_tables(height, n, chunks):
    cosine, sine = dft_pair(height)
    zero = np.zeros_like(cosine)
    rows = height // n // chunks

    def arrange(blocks):
        full = np.stack([np.stack(line, axis=1) for line in blocks])
        full = full.reshape(2 * height, 2, n, chunks, rows)
        return full.transpose(0, 3, 2, 1, 4).reshape(2 * height, 2 * height)

    middle = arrange([[zero, cosine], [zero, -sine]])
    first = arrange([[cosine, zero], [-sine, zero]])
    other = arrange([[cosine, sine], [-sine, cosine]])
    backward = np.stack([middle, first, other]).transpose(0, 2, 1)
    backward = backward.reshape(3, chunks, n, 2 * rows, 2 * height)
    return backward.astype(ml_dtypes.bfloat16)


def mirror_table(height):
    table = np.zeros((height, height), np.float32)
    table[np.arange(height), (-np.arange(height)) % height] = 1.0
    return table.astype(ml_dtypes.bfloat16)


def dot(a, b):
    return jnp.dot(a, b, preferred_element_type=F32)


def dot_tn(a, b):
    return lax.dot_general(a, b, (((0,), (0,)), ((), ())), preferred_element_type=F32)


def normalize(values):
    centred = values - jnp.mean(values, axis=-1, keepdims=True)
    variance = jnp.mean(centred * centred, axis=-1, keepdims=True)
    rstd = lax.rsqrt(variance + EPS)
    return centred * rstd, rstd


def norm_backward(upstream, normed, rstd, gain):
    scaled = upstream * gain
    return (
        scaled
        - jnp.mean(scaled, axis=-1, keepdims=True)
        - normed * jnp.mean(scaled * normed, axis=-1, keepdims=True)
    ) * rstd


def gelu_and_slope(v):
    e = jnp.exp(v * v * -0.5)
    d = 1.0 + (0.3275911 / math.sqrt(2.0)) * jnp.abs(v)
    t = pl.reciprocal(d, approx=True)
    t = t * (2.0 - d * t)
    poly = 0.5 * 1.061405429
    for coefficient in (-1.453152027, 1.421413741, -0.284496736, 0.254829592):
        poly = poly * t + 0.5 * coefficient
    tail = poly * t * e
    phi = jnp.where(v < 0.0, tail, 1.0 - tail)
    return v * phi, phi + v * e * (1.0 / math.sqrt(2.0 * math.pi))


def spaced(count):
    groups = -(-count // 8)
    return 8 * (groups + 1 - groups % 2)


def lanes(c):
    return slice(c * LANES, (c + 1) * LANES)


def unpack(received, scratch):
    count, rows, chans = received[0].shape
    pitch = spaced(rows)

    def step(k, carry):
        for s, ref in enumerate(received):
            start = pl.multiple_of((s * count + k) * pitch, 8)
            for c in range(chans // LANES):
                scratch[c, pl.ds(start, rows), :] = ref[k, :, lanes(c)].astype(F32)
        return carry

    lax.fori_loop(0, count, step, 0, unroll=2)


def read_row(scratch, row, columns, rows):
    parts = [
        scratch[c, pl.ds(row, columns, stride=spaced(rows)), :].astype(BF16)
        for c in range(scratch.shape[0])
    ]
    return jnp.concatenate(parts, axis=1)


def write_row(scratch, row, columns, values):
    start = pl.multiple_of(row * spaced(columns), 8)
    for c in range(scratch.shape[0]):
        scratch[c, pl.ds(start, columns), :] = values[:, lanes(c)]


def pack(scratch, columns, outgoing):
    count, rows, _ = outgoing[0].shape

    def step(k, carry):
        for s, ref in enumerate(outgoing):
            for c in range(scratch.shape[0]):
                part = scratch[c, pl.ds(s * count + k, rows, stride=spaced(columns)), :]
                ref[k, :, lanes(c)] = part.astype(BF16)
        return carry

    lax.fori_loop(0, count, step, 0, unroll=2)


def params():
    return pltpu.CompilerParams(vmem_limit_bytes=VMEM_LIMIT)


def resident(shape):
    return pl.BlockSpec(shape, lambda *_: (0,) * len(shape), pipeline_mode=pl.Buffered(1))


ANYWHERE = pl.BlockSpec(memory_space=pl.ANY)


def cost(flops, size):
    return pl.CostEstimate(flops=int(flops), bytes_accessed=int(size), transcendentals=0)


def shape_of(shape, dtype=BF16):
    return jax.ShapeDtypeStruct(tuple(shape), dtype)


def hold(value, after):
    return pl.pallas_call(
        lambda *refs: None,
        in_specs=[ANYWHERE] * (1 + len(after)),
        out_specs=ANYWHERE,
        out_shape=shape_of(value.shape, value.dtype),
        input_output_aliases={0: 0},
        compiler_params=params(),
        cost_estimate=cost(0, 0),
        name="hold",
    )(value, *after)


def enter_kernel(tokens, gain, table, *rest):
    outgoing, scratch = rest[-2:-1], rest[-1]
    step = pl.program_id(0)
    block, width, _ = tokens.shape
    for r in range(block):
        normed, _ = normalize(tokens[r].astype(F32))
        mixed = (normed * gain[...]).astype(BF16)
        write_row(scratch, step * block + r, width, dot(table[...], mixed))

    @pl.when(step == pl.num_programs(0) - 1)
    def _():
        pack(scratch, width, outgoing)


def enter(tokens, gain, table, block):
    rows, width, chans = tokens.shape
    steps = rows // block
    out = (width, rows, chans)
    return pl.pallas_call(
        enter_kernel,
        grid=(steps,),
        in_specs=[
            pl.BlockSpec((block, width, chans), lambda i: (i, 0, 0)),
            resident((1, chans)),
            resident((width, width)),
        ],
        out_specs=resident(out),
        out_shape=shape_of(out),
        scratch_shapes=[pltpu.VMEM((chans // LANES, rows * spaced(width), LANES), F32)],
        compiler_params=params(),
        cost_estimate=cost(2 * rows * width * width * chans, 4 * rows * width * chans),
        name="enter_rows",
    )(tokens, gain, table)


def mlp_kernel(
    n, later, tokens, upstream, gain, table_out, table_in, w_in, w_out, w_in_t, w_out_t, *rest
):
    received, rest = rest[:n], rest[n:]
    if later:
        (_, *before), rest = rest[:4], rest[4:]
    block_out, outgoing, rest = rest[0], rest[1 : n + 1], rest[n + 1 :]
    sum_in, sum_out, sum_gain, unpacked, packed = rest
    step = pl.program_id(0)
    block, width, chans = tokens.shape
    rows = received[0].shape[1]
    hidden = w_in.shape[1]
    part = min(512, hidden)

    @pl.when(step == 0)
    def _():
        unpack(received, unpacked)
        for i, ref in enumerate((sum_in, sum_out, sum_gain)):
            ref[...] = before[i][...] if later else jnp.zeros_like(ref)

    spatial = jnp.concatenate(
        [
            dot(table_out[...], read_row(unpacked, step * block + r, width, rows))
            for r in range(block)
        ],
        axis=0,
    )
    normed, rstd = normalize(spatial)
    mlp_in = (normed * gain[...]).astype(BF16)
    grad = upstream[...].reshape(block * width, chans)
    out = tokens[...].reshape(block * width, chans).astype(F32)
    grad_mlp = jnp.zeros_like(spatial)

    def first(cols):
        return dot(mlp_in, w_in[:, cols]), dot(grad, w_out_t[:, cols])

    parts = [slice(f, f + part) for f in range(0, hidden, part)]
    ahead = first(parts[0])
    for f, cols in enumerate(parts):
        preact, grad_act = ahead
        if f + 1 < len(parts):
            ahead = first(parts[f + 1])
        value, slope = gelu_and_slope(preact)
        activated = value.astype(BF16)
        grad_pre = (grad_act * slope).astype(BF16)
        out = out + dot(activated, w_out[cols, :])
        grad_mlp = grad_mlp + dot(grad_pre, w_in_t[cols, :])
        sum_out[:, cols] += dot_tn(grad, activated)
        sum_in[:, cols] += dot_tn(mlp_in, grad_pre)
    block_out[...] = out.astype(BF16).reshape(block, width, chans)
    grad_spatial = norm_backward(grad_mlp, normed, rstd, gain[...])
    sum_gain[0:8] += jnp.sum((grad_mlp * normed).reshape(-1, 8, chans), axis=0)
    sum_gain[8:16] += jnp.sum((grad_spatial * spatial).reshape(-1, 8, chans), axis=0)
    sent = grad_spatial.astype(BF16)
    for r in range(block):
        values = dot(table_in[...], sent[r * width : (r + 1) * width])
        write_row(packed, step * block + r, width, values)

    @pl.when(step == pl.num_programs(0) - 1)
    def _():
        pack(packed, width, outgoing)


def mlp(received, tokens, upstream, gain, tables, weights, previous, chunk, block):
    n = len(received)
    count, rows, chans = received[0].shape
    width = tokens.shape[1]
    hidden = weights[0].shape[1]
    steps = rows // block
    by_rows = pl.BlockSpec((block, width, chans), lambda i: (i + chunk * steps, 0, 0))
    operands = [tokens, upstream, gain, *tables, *weights, *received]
    in_specs = [
        by_rows,
        by_rows,
        resident((1, chans)),
        resident((width, width)),
        resident((width, width)),
        resident((chans, hidden)),
        resident((hidden, chans)),
        resident((hidden, chans)),
        resident((chans, hidden)),
    ] + [resident((count, rows, chans))] * n
    aliases = {}
    if previous is not None:
        aliases = {len(operands): 0}
        operands += previous
        in_specs += [ANYWHERE] + [resident(p.shape) for p in previous[1:]]
    flops = 2 * rows * width * chans * (6 * hidden + 2 * width)
    outputs = pl.pallas_call(
        functools.partial(mlp_kernel, n, previous is not None),
        grid=(steps,),
        in_specs=in_specs,
        out_specs=[by_rows]
        + [resident((count, rows, chans))] * n
        + [resident((chans, hidden)), resident((chans, hidden)), resident((16, chans))],
        out_shape=[shape_of(tokens.shape)]
        + [shape_of((count, rows, chans))] * n
        + [shape_of((chans, hidden), F32)] * 2
        + [shape_of((16, chans), F32)],
        scratch_shapes=[
            pltpu.VMEM((chans // LANES, width * spaced(rows), LANES), F32),
            pltpu.VMEM((chans // LANES, rows * spaced(width), LANES), F32),
        ],
        input_output_aliases=aliases,
        compiler_params=params(),
        cost_estimate=cost(flops, 10 * rows * width * chans),
        name="mlp_rows",
    )(*operands)
    return outputs[0], outputs[1 : n + 1], outputs[n + 1 :]


def leave_kernel(n, tokens, upstream, gain, table_out, *rest):
    received, (grad_tokens, unpacked) = rest[:n], rest[-2:]
    step = pl.program_id(0)
    block, width, _ = tokens.shape
    rows = received[0].shape[1]

    @pl.when(step == 0)
    def _():
        unpack(received, unpacked)

    for r in range(block):
        back = dot(table_out[...], read_row(unpacked, step * block + r, width, rows))
        normed, rstd = normalize(tokens[r].astype(F32))
        grad = norm_backward(back, normed, rstd, gain[...])
        grad_tokens[r] = (upstream[r].astype(F32) + grad).astype(BF16)


def leave(received, tokens, upstream, gain, table_out, previous, chunk, block, after):
    n = len(received)
    count, rows, chans = received[0].shape
    width = tokens.shape[1]
    steps = rows // block
    by_rows = pl.BlockSpec((block, width, chans), lambda i: (i + chunk * steps, 0, 0))
    operands = [tokens, upstream, gain, table_out, *received]
    in_specs = [by_rows, by_rows, resident((1, chans)), resident((width, width))]
    in_specs += [resident((count, rows, chans))] * n
    aliases = {}
    if previous is not None:
        aliases = {len(operands): 0}
        operands.append(previous)
        in_specs.append(ANYWHERE)
    operands += after
    in_specs += [ANYWHERE] * len(after)
    return pl.pallas_call(
        functools.partial(leave_kernel, n),
        grid=(steps,),
        in_specs=in_specs,
        out_specs=by_rows,
        out_shape=shape_of(tokens.shape),
        scratch_shapes=[pltpu.VMEM((chans // LANES, width * spaced(rows), LANES), F32)],
        input_output_aliases=aliases,
        compiler_params=params(),
        cost_estimate=cost(2 * rows * width * width * chans, 8 * rows * width * chans),
        name="leave_rows",
    )(*operands)


def columns_kernel(count, outs, back, flags, table_f, table_b, kernel, *rest):
    spectrum, rest = (rest[0], rest[1:]) if back else (None, rest)
    received, (*outgoing, held) = rest[:count], rest[-outs - 1 :]
    step, last = pl.program_id(0), pl.num_programs(0) - 1
    per, _, height, chans = kernel.shape

    def load(j):
        return jnp.concatenate([ref[:, :, j].reshape(-1, chans) for ref in received], axis=0)

    def store(j, values):
        values = values.astype(BF16)
        size = values.shape[0] // len(outgoing)
        for i, ref in enumerate(outgoing):
            n, _, _, rows, _ = ref.shape
            ref[:, :, j] = values[i * size : (i + 1) * size].reshape(n, 2, rows, chans)

    def filtered(slot, found):
        found = found.astype(BF16)
        real, imag = found[:height].astype(F32), found[height:].astype(F32)
        k_real, k_imag = kernel[slot, 0].astype(F32), kernel[slot, 1].astype(F32)
        if back:
            s_real, s_imag = spectrum[slot, 0].astype(F32), spectrum[slot, 1].astype(F32)
            held[slot, 0] = (real * s_real + imag * s_imag).astype(BF16)
            held[slot, 1] = (imag * s_real - real * s_imag).astype(BF16)
            k_imag = -k_imag
        else:
            held[slot, 0] = found[:height]
            held[slot, 1] = found[height:]
        upper = (k_real * real - k_imag * imag).astype(BF16)
        lower = (k_real * imag + k_imag * real).astype(BF16)
        return jnp.concatenate([upper, lower], axis=0)

    @pl.when(step < last)
    def _():
        at = [1 + step * per + i for i in range(per)]
        found = dot(table_f[2], jnp.concatenate([load(j) for j in at], axis=1))
        weighted = [filtered(i, found[:, i * chans : (i + 1) * chans]) for i in range(per)]
        result = dot(table_b[2], jnp.concatenate(weighted, axis=1))
        for i, j in enumerate(at):
            store(j, result[:, i * chans : (i + 1) * chans])

    @pl.when(step == last)
    def _():
        values = load(0)
        kind = 2 - flags[1]
        zero = filtered(0, dot(table_f[kind], values))
        middle = filtered(1, dot(table_f[0], values))
        store(0, dot(table_b[kind], zero) + dot(table_b[0], middle))
        for i in range(2, per):
            held[i] = jnp.zeros_like(held[i])


def columns(flags, tables, kernel, received, outs, spectrum=None, after=()):
    count = len(received)
    n, _, half, rows, chans = received[0].shape
    sent = (n, 2, half, count * rows // outs, chans)
    slots, _, height, _ = kernel.shape
    per = columns_per_step(half)
    held = pl.BlockSpec((per, 2, height, chans), lambda t, flags: (t, 0, 0, 0))
    table = resident((3, 2 * height, 2 * height))
    back = spectrum is not None
    outputs = pl.pallas_call(
        functools.partial(columns_kernel, count, outs, back),
        grid_spec=pltpu.PrefetchScalarGridSpec(
            num_scalar_prefetch=1,
            grid=(slots // per,),
            in_specs=[table, table, held]
            + [held] * back
            + [resident(r.shape) for r in received]
            + [ANYWHERE] * len(after),
            out_specs=[resident(sent)] * outs + [held],
        ),
        out_shape=[shape_of(sent)] * outs + [shape_of(kernel.shape)],
        compiler_params=params(),
        cost_estimate=cost(16 * height * height * chans * slots, 20 * height * chans * slots),
        name="filter_columns",
    )(flags, *tables, kernel, *([spectrum] if back else []), *received, *after)
    return outputs[:outs], outputs[outs]


def columns_per_step(half):
    return 3 if (half - 1) % 3 == 0 else 2 if (half - 1) % 2 == 0 else 1


def slot_count(half):
    per = max(2, columns_per_step(half))
    return half - 1 + per


def filter_part_kernel(copies, flags, mirror, own, *rest):
    mains, extras = rest[:copies], rest[copies : 2 * copies]
    kernel, scr_own, scr_main, scr_extra = rest[-4:]
    part = pl.program_id(0)
    upper, first, me = flags[0], flags[1], flags[2]
    _, height, wide, _ = own.shape
    half = wide // 2
    share = height // copies
    pitch_own, pitch = spaced(wide), spaced(half)

    def spread_own(m, carry):
        scr_own[pl.ds(pl.multiple_of(m * pitch_own, 8), wide), :] = own[0, m].astype(F32)
        return carry

    lax.fori_loop(0, height, spread_own, 0, unroll=8)
    for i in range(copies):
        owner = jnp.bitwise_xor(me, i)

        def spread_main(m, carry):
            at = pl.multiple_of((owner * share + m) * pitch, 8)
            scr_main[pl.ds(at, half), :] = mains[i][0, m].astype(F32)
            return carry

        lax.fori_loop(0, share, spread_main, 0, unroll=8)
        at = pl.multiple_of(owner * share, share)
        scr_extra[pl.ds(at, share), :] = extras[i][0].astype(F32)
    sign = jnp.where(part == 0, 0.5, -0.5)
    extra = scr_extra[...]
    middle = 0.5 * extra + sign * dot(mirror[...], extra.astype(BF16))
    kernel[half, 0] = jnp.where(first == 1, middle, 0.0).astype(BF16)
    for i in range(half + 1, kernel.shape[0]):
        kernel[i, 0] = jnp.zeros((height, LANES), BF16)
    for j in range(half):
        mine = scr_own[pl.ds(j + upper, height, stride=pitch_own), :]
        if j == 0:
            other = scr_main[pl.ds(half - 1, height, stride=pitch), :]
            lower = jnp.where(first == 1, mine, extra)
            other = jnp.where(upper == 1, other, lower)
        else:
            other = scr_main[pl.ds(half - j - upper, height, stride=pitch), :]
        turned = dot(mirror[...], other.astype(BF16))
        kernel[(j - 1) % half, 0] = (0.5 * mine + sign * turned).astype(BF16)


def filter_part(flags, mirror, own, mains, extras, after):
    _, height, wide, chans = own.shape
    copies = len(mains)
    half, share = wide // 2, height // copies
    slots = slot_count(half)
    return pl.pallas_call(
        functools.partial(filter_part_kernel, copies),
        grid_spec=pltpu.PrefetchScalarGridSpec(
            num_scalar_prefetch=1,
            grid=(2, chans // LANES),
            in_specs=[
                pl.BlockSpec((height, height), lambda p, c, flags: (0, 0)),
                pl.BlockSpec((1, height, wide, LANES), lambda p, c, flags: (p, 0, 0, c)),
            ]
            + [pl.BlockSpec((1, share, half, LANES), lambda p, c, flags: (p, 0, 0, c))] * copies
            + [pl.BlockSpec((1, share, LANES), lambda p, c, flags: (p, 0, c))] * copies
            + [ANYWHERE] * len(after),
            out_specs=pl.BlockSpec((slots, 1, height, LANES), lambda p, c, flags: (0, p, 0, c)),
            scratch_shapes=[
                pltpu.VMEM((height * spaced(wide), LANES), F32),
                pltpu.VMEM((height * spaced(half), LANES), F32),
                pltpu.VMEM((height, LANES), F32),
            ],
        ),
        out_shape=shape_of((slots, 2, height, chans)),
        compiler_params=params(),
        cost_estimate=cost(4 * height * height * chans * half, 16 * height * half * chans),
        name="filter_part",
    )(flags, mirror, own, *mains, *extras, *after)


def filter_gradient_kernel(copies, flags, mirror, *rest):
    mine, theirs = rest[:copies], rest[copies : 2 * copies]
    out, gathered, turned = rest[-3:]
    part = pl.program_id(0)
    upper, me = flags[0], flags[2]
    _, height, wide, _ = out.shape
    half = wide // 2
    share = height // copies
    pitch = spaced(height)
    for i in range(copies):
        at = pl.multiple_of(jnp.bitwise_xor(me, i) * share, share)
        gathered[0:half, pl.ds(at, share), :] = mine[i][:, 0]
        gathered[half:, pl.ds(at, share), :] = theirs[i][:, 0]
    sign = jnp.where(part == 0, 1.0, -1.0)
    for k in range(wide):
        if k == 0:
            index = jnp.where(upper == 1, 2 * half, half - 1)
        elif k < half:
            index = k - 1 - upper
            index = jnp.where(index < 0, half - 1, index)
        elif k == half:
            index = jnp.where(upper == 1, half - 2, 2 * half - 2)
        else:
            index = wide - 2 - k + upper
            index = half + jnp.where(index < 0, half - 1, index)
        value = gathered[index]
        if 0 < k < half:
            value = value.astype(F32)
        else:
            other = sign * dot(mirror[...], value)
            if k == 0:
                other = jnp.where(upper == 1, other, value.astype(F32))
            elif k == half:
                other = jnp.where(upper == 1, value.astype(F32), other)
            value = other
        turned[pl.ds(k * pitch, height), :] = value

    def step(m, carry):
        out[0, m] = turned[pl.ds(m, wide, stride=pitch), :]
        return carry

    lax.fori_loop(0, height, step, 0, unroll=8)


def filter_gradient(flags, mirror, mine, theirs, height, wide, after):
    _, _, share, chans = mine[0].shape
    copies, half = len(mine), wide // 2
    block = lambda slots: pl.BlockSpec(
        (slots, 1, share, LANES), lambda p, c, flags: (0, p, 0, c)
    )
    return pl.pallas_call(
        functools.partial(filter_gradient_kernel, copies),
        grid_spec=pltpu.PrefetchScalarGridSpec(
            num_scalar_prefetch=1,
            grid=(2, chans // LANES),
            in_specs=[pl.BlockSpec((height, height), lambda p, c, flags: (0, 0))]
            + [block(half)] * copies
            + [block(half + 1)] * copies
            + [ANYWHERE] * len(after),
            out_specs=pl.BlockSpec((1, height, wide, LANES), lambda p, c, flags: (p, 0, 0, c)),
            scratch_shapes=[
                pltpu.VMEM((wide + 1, height, LANES), BF16),
                pltpu.VMEM((wide * spaced(height), LANES), F32),
            ],
        ),
        out_shape=shape_of((2, height, wide, chans), F32),
        compiler_params=params(),
        cost_estimate=cost(2 * height * height * chans * wide, 12 * height * wide * chans),
        name="filter_gradient",
    )(flags, mirror, *mine, *theirs, *after)


def swap(value, axis, size, partner):
    return lax.ppermute(value, axis, [(i, partner(i)) for i in range(size)])


def swap_bits(value, axis, size, bits):
    return swap(value, axis, size, lambda i: i ^ bits)


def exchange(value):
    return lax.all_to_all(value, "space", split_axis=0, concat_axis=0, tiled=True)


def exchange_after(value, after):
    return exchange(hold(value, tuple(after)) if after else value)


def gather_copies(value, copies):
    parts = {0: value}
    bit = copies // 2
    while bit:
        for key in list(parts):
            parts[key ^ bit] = swap_bits(parts[key], "copy", copies, bit)
        bit //= 2
    return [parts[i] for i in range(copies)]


def reduce_shares(value, axes, extra=None):
    places, place = [], 0
    for name in axes:
        digits = lax.axis_size(name).bit_length() - 1
        places += [(name, bit, place + digits - 1 - bit) for bit in range(digits)]
        place += digits
    for name, bit, place in places:
        size, own = lax.axis_size(name), (lax.axis_index(name) >> bit) & 1
        kept = lax.dynamic_index_in_dim(value, own, place, keepdims=True)
        sent = lax.dynamic_index_in_dim(value, 1 - own, place, keepdims=True)
        other = swap_bits(sent, name, size, 1 << bit)
        value = (kept.astype(F32) + other.astype(F32)).astype(value.dtype)
        if extra is not None:
            extra = extra + swap_bits(extra, name, size, 1 << bit)
    return value, extra


def body(noisy_tokens, grad_out, filter_weight, weight_in, weight_out, gain_one, gain_two):
    _, rows_dev, width, chans = noisy_tokens.shape
    height, wide = filter_weight.shape[1:3]
    digits = (2,) * (lax.axis_size("copy").bit_length() - 1)
    hidden = weight_in.shape[1]
    half = wide // 2
    n, copies = lax.axis_size("space"), lax.axis_size("copy")
    chunks = 2
    rows = rows_dev // chunks
    tokens, upstream = noisy_tokens[0], grad_out[0]
    me, copy = lax.axis_index("space"), lax.axis_index("copy")

    share = height // copies
    at = copy * share
    opposite = lambda d: n - 1 - d
    main = lax.dynamic_slice(filter_weight, (0, at, half, 0), (2, share, half, chans))
    main = swap(main, "space", n, opposite)
    to_lower = [(n // 2, 0)] + [(e, n - e) for e in range(n // 2 + 1, n)]
    single = lax.dynamic_slice(filter_weight, (0, at, 0, 0), (2, share, 1, chans))
    single = lax.ppermute(single.reshape(2, share, chans), "space", to_lower)

    forward, weighted = row_tables(width, n)
    table_in = jnp.asarray(forward.reshape(width, width))
    table_out = jnp.asarray(np.ascontiguousarray(weighted.reshape(width, width).T))
    whole, cut = (
        column_tables(height, n, c).reshape(3, 2 * height, 2 * height) for c in (1, chunks)
    )
    forward_in, backward_in = (
        jnp.asarray(np.ascontiguousarray(t.transpose(0, 2, 1))) for t in (whole, cut)
    )
    out_tabs = jnp.asarray(cut)
    mirror = jnp.asarray(mirror_table(height))
    gain_a, gain_b = gain_one.reshape(1, chans), gain_two.reshape(1, chans)
    upper = (me >= n // 2).astype(jnp.int32)
    first = (me == 0).astype(jnp.int32)

    def flags(index):
        return jnp.stack([upper, first, index.astype(jnp.int32)])

    def split(value):
        return value.reshape(n, 2, half, -1, chans)

    def join(value):
        return value.reshape(width, -1, chans)

    entered = hold(enter(tokens, gain_a, table_in, 2), (main, single))
    arrived = [split(exchange(entered))]
    mains, singles = gather_copies(main, copies), gather_copies(single, copies)
    weights = (weight_in, weight_out, weight_in.T, weight_out.T)
    kernel = filter_part(flags(copy), mirror, filter_weight, mains, singles, weights[2:])
    returned, spectrum = columns(flags(copy), (forward_in, out_tabs), kernel, arrived, chunks)

    tables = (table_out, table_in)
    received, arrived = [], []
    for r in returned:
        received.append(exchange_after(join(r), received))
    previous = None
    for c in range(chunks):
        block_out, sent, sums = mlp(
            [received[c]], tokens, upstream, gain_b, tables, weights, previous, c, 4
        )
        arrived.append(exchange_after(sent[0], arrived))
        previous = [block_out, *sums]

    sum_in, sum_out, sum_gain = sums
    both = jnp.concatenate([sum_in, sum_out], axis=0).astype(BF16)
    both = both.reshape((2,) * ((copies * n).bit_length() - 1) + (-1, hidden))
    gains = jnp.stack([jnp.sum(sum_gain[8:], axis=0) / gain_one, jnp.sum(sum_gain[:8], axis=0)])
    by_copy, gains = reduce_shares(both, ("copy",), gains)
    part, gains = reduce_shares(by_copy[(0,) * len(digits)], ("space",), gains)
    factor = 1.0 / math.sqrt(copies * rows_dev * n * width)
    part = (part.reshape(-1, hidden).astype(F32) * factor).astype(BF16)
    gains = gains * factor

    returned, terms = columns(
        flags(copy), (backward_in, out_tabs), kernel, [split(a) for a in arrived], chunks, spectrum, (by_copy,)
    )
    grads = lax.all_gather(lax.all_gather(part, "space", tiled=True), "copy", tiled=True)
    received = exchange(join(returned[0]))
    grad_tokens = leave(
        [received], tokens, upstream, gain_a, table_out, None, 0, 2, (grads, gains)
    )

    terms = terms.reshape(terms.shape[:2] + digits + (share, chans))
    terms = jnp.moveaxis(terms, range(2, 2 + len(digits)), range(len(digits)))
    reduced, _ = reduce_shares(terms, ("copy",))
    reduced = reduced.reshape(-1, 2, share, chans)
    mirrored = swap(reduced[:half], "space", n, opposite)
    to_upper = [(0, n // 2)] + [(d, n - d) for d in range(1, n // 2)]
    single = lax.ppermute(
        jnp.where(me == 0, reduced[half], reduced[half - 1]), "space", to_upper
    )
    mine = gather_copies(reduced[:half], copies)
    received = exchange(hold(join(returned[1]), (mirrored, single, *mine, grad_tokens)))
    theirs = gather_copies(jnp.concatenate([mirrored, single[None]], axis=0), copies)
    grad_filter = filter_gradient(
        flags(copy), mirror, mine, theirs, height, wide, ()
    )
    grad_tokens = leave(
        [received], tokens, upstream, gain_a, table_out, grad_tokens, 1, 2, (grad_filter,)
    )
    return (
        block_out[None],
        grad_tokens[None],
        grad_filter,
        grads[:chans],
        grads[chans:].T,
        gains[0],
        gains[1],
    )


def dft_parts(length):
    index = jnp.arange(length, dtype=jnp.int32)
    phase = index[:, None] * index[None, :] % length
    angle = phase.astype(jnp.float32) * (2.0 * math.pi / length)
    factor = 1.0 / math.sqrt(length)
    return (
        (jnp.cos(angle) * factor).astype(jnp.bfloat16),
        (jnp.sin(angle) * factor).astype(jnp.bfloat16),
    )


def row_table(length):
    cosine, sine = dft_parts(length)
    return jnp.stack([cosine, -sine])


def column_table(length, direction):
    cosine, sine = dft_parts(length)
    upper = jnp.stack([cosine, direction * sine], axis=1)
    lower = jnp.stack([-direction * sine, cosine], axis=1)
    return jnp.stack([upper, lower])


def plain_layer_norm(values):
    centre = jnp.mean(values, axis=-1, keepdims=True)
    centred = values - centre
    variance = jnp.mean(centred * centred, axis=-1, keepdims=True)
    rstd_value = lax.rsqrt(variance + EPS)
    return (centred * rstd_value, rstd_value)


def plain_norm_backward(upstream, normed, rstd_value, gain):
    scaled = upstream * gain
    result = (
        scaled
        - jnp.mean(scaled, axis=-1, keepdims=True)
        - normed * jnp.mean(scaled * normed, axis=-1, keepdims=True)
    ) * rstd_value
    lead = tuple(range(upstream.ndim - 1))
    return (result, jnp.sum(upstream * normed, axis=lead))


def apply_filter(spectrum, filter_weight, direction):
    real_part = spectrum[0].astype(jnp.float32)
    imag_part = spectrum[1].astype(jnp.float32)
    kernel_real = filter_weight[0].astype(jnp.float32)
    kernel_imag = direction * filter_weight[1].astype(jnp.float32)
    return jnp.stack(
        [
            kernel_real * real_part - kernel_imag * imag_part,
            kernel_real * imag_part + kernel_imag * real_part,
        ]
    )


def exact_gelu(values):
    return jax.nn.gelu(values, approximate=False)


def spectral(values, filter_weight, direction):
    width = values.shape[2]
    rows_tab = row_table(width)
    rows = jnp.einsum(
        "pkw,bhwc->pbhkc", rows_tab, values, preferred_element_type=jnp.float32
    ).astype(jnp.bfloat16)
    columns = lax.all_to_all(rows, "space", split_axis=3, concat_axis=2, tiled=True)
    height = columns.shape[2]
    spectrum = jnp.einsum(
        "qmph,pbhkc->qbmkc", column_table(height, 1), columns, preferred_element_type=jnp.float32
    ).astype(jnp.bfloat16)
    weighted = apply_filter(spectrum, filter_weight[:, None], direction).astype(jnp.bfloat16)
    returned = jnp.einsum(
        "qmph,pbhkc->qbmkc", column_table(height, -1), weighted, preferred_element_type=jnp.float32
    ).astype(jnp.bfloat16)
    back_rows = lax.all_to_all(returned, "space", split_axis=2, concat_axis=3, tiled=True)
    output = jnp.einsum("pkw,pbhkc->bhwc", rows_tab, back_rows, preferred_element_type=jnp.float32)
    return (output, spectrum)


def plain_body(noisy_tokens, grad_out, filter_weight, weight_in, weight_out, gain_one, gain_two):
    batch, rows_dev, width, chans = noisy_tokens.shape
    inputs = noisy_tokens.astype(jnp.float32)
    normed_one, rstd_one = plain_layer_norm(inputs)
    mixed_in = (normed_one * gain_one).astype(jnp.bfloat16)
    spatial, spectrum = spectral(mixed_in, filter_weight, 1)
    normed_two, rstd_two = plain_layer_norm(spatial)
    mlp_in = (normed_two * gain_two).astype(jnp.bfloat16).reshape(-1, chans)
    preact = jnp.dot(mlp_in, weight_in, preferred_element_type=jnp.float32)
    activated = exact_gelu(preact).astype(jnp.bfloat16)
    mlp_out = jnp.dot(activated, weight_out, preferred_element_type=jnp.float32)
    block_out = (inputs + mlp_out.reshape(inputs.shape)).astype(jnp.bfloat16)
    upstream = grad_out.reshape(-1, chans)
    grad_act = jnp.dot(upstream, weight_out.T, preferred_element_type=jnp.float32)
    grad_pre = jax.vjp(exact_gelu, preact)[1](grad_act)[0].astype(jnp.bfloat16)
    sum_out = jnp.dot(activated.T, upstream, preferred_element_type=jnp.float32)
    sum_in = jnp.dot(mlp_in.T, grad_pre, preferred_element_type=jnp.float32)
    grad_mlp = jnp.dot(grad_pre, weight_in.T, preferred_element_type=jnp.float32).reshape(
        inputs.shape
    )
    grad_spatial, sum_gain_two = plain_norm_backward(grad_mlp, normed_two, rstd_two, gain_two)
    back_spatial, adjoint = spectral(grad_spatial.astype(jnp.bfloat16), filter_weight, -1)
    spec_f = spectrum.astype(jnp.float32)
    adj_f = adjoint.astype(jnp.float32)
    filter_terms = jnp.stack(
        [
            jnp.sum(adj_f[0] * spec_f[0] + adj_f[1] * spec_f[1], axis=0),
            jnp.sum(adj_f[1] * spec_f[0] - adj_f[0] * spec_f[1], axis=0),
        ]
    )
    grad_filter = lax.psum(filter_terms.astype(jnp.bfloat16), "copy").astype(jnp.float32)
    grad_normed, sum_gain_one = plain_norm_backward(back_spatial, normed_one, rstd_one, gain_one)
    grad_tokens = (grad_out.astype(jnp.float32) + grad_normed).astype(jnp.bfloat16)
    local_sums = (sum_in, sum_out, sum_gain_one, sum_gain_two)
    summed = lax.psum(
        (local_sums[0], local_sums[1], local_sums[2], local_sums[3]), ("copy", "space")
    )
    total_tokens = batch * lax.axis_size("copy") * rows_dev * lax.axis_size("space") * width
    factor = 1.0 / math.sqrt(total_tokens)
    return (
        block_out,
        grad_tokens,
        grad_filter,
        (summed[0] * factor).astype(jnp.bfloat16),
        (summed[1] * factor).astype(jnp.bfloat16),
        summed[2] * factor,
        summed[3] * factor,
    )


def solution(mesh):
    def program(*arrays):
        rows_dev, wide = arrays[0].shape[1], arrays[2].shape[2]
        n = lax.axis_size("space")
        tiled = rows_dev % 32 == 0 and wide % 32 == 0 and n & (n - 1) == 0
        return (body if tiled else plain_body)(*arrays)

    return jax.shard_map(
        program,
        mesh=mesh,
        in_specs=(
            P("copy", "space", None, None),
            P("copy", "space", None, None),
            P(None, None, "space", None),
            P(),
            P(),
            P(),
            P(),
        ),
        out_specs=(
            P("copy", "space", None, None),
            P("copy", "space", None, None),
            P(None, None, "space", None),
            P(),
            P(),
            P(),
            P(),
        ),
        check_vma=False,
    )
```
